32 devices in a mesh: fsdp: 8 (over y, x, core), rep: 4 (over z).
Axes of the slice: x: 2, y: 2, z: 4, core: 2. Of those that a mesh axis runs over, the one named last changes fastest.
Arguments:
- tokens: bfloat16 [32768, 768], P(('fsdp', 'rep')), may hold values from -6 to 6
- segment_ids: int32 [32768], P(('fsdp', 'rep')), may hold values from 0 to 127, never falling along the last dimension, each value on 1 to 1024 neighbouring positions
- w_in: bfloat16 [768, 3376], P(('fsdp', 'rep')), may hold values from -0.21875 to 0.21875
- w_out: bfloat16 [1536, 768], P(None, ('fsdp', 'rep')), may hold values from -0.15625 to 0.15625
- norm_gain: bfloat16 [768], P(('fsdp', 'rep')), may hold values from 0.25 to 1.75
- conv_w: float32 [4, 1792], replicated, may hold values from -3 to 3
- conv_b: float32 [1792], replicated, may hold values from -1.5 to 1.5
- dt_bias: float32 [48], replicated, may hold values from -7.5 to -2
- a_log: float32 [48], replicated, may hold values from -1.5 to 0
- d_skip: float32 [24], replicated, may hold values from 0.5 to 1.5
- out_gain: float32 [1536], replicated, may hold values from 0.25 to 1.75
- cotangent: bfloat16 [32768, 768], P(('fsdp', 'rep')), may hold values from -6 to 6
Outputs:
- output: bfloat16 [32768, 768], P(('fsdp', 'rep'))
- d_tokens: float32 [32768, 768], P(('fsdp', 'rep'))
- d_w_in: float32 [768, 3376], P(('fsdp', 'rep'))
- d_w_out: float32 [1536, 768], P(None, ('fsdp', 'rep'))
- d_norm_gain: float32 [768], P(('fsdp', 'rep'))
- d_conv_w: float32 [4, 1792], replicated
- d_conv_b: float32 [1792], replicated
- d_dt_bias: float32 [48], replicated
- d_a_log: float32 [48], replicated
- d_d_skip: float32 [24], replicated
- d_out_gain: float32 [1536], replicated
The draws below stay inside these ranges and needn't reach their ends.
Inputs may be any that keep to these rules, and one draw needn't show every extreme that they name: `segment_ids`: segment ids never fall along the tokens; each segment has 1 to 1024 tokens and one has exactly 1024.
All inputs are finite; a program needn't handle non-finite values.
Results may differ from the reference program's by a relative error of at most 0.0083.
Values may be sent and summed in bfloat16 or wider, within the bound.
A program may use at most 256 MiB of HBM per device.

```python
import math
import jax
import jax.numpy as jnp
import numpy as np
from jax import lax

D = 768
HEADS = 24
HEAD_DIM = 64
STATE = 64
CONV = 4
TOK_DEV = 1024
INNER = 1536
CHANNELS = 1792
PROJ = 3376
TOKENS = 32768
N_FSDP = 8
N_REP = 4


def head_kinds(key):
    shuffled = jax.random.permutation(jax.random.fold_in(key, 101), 2 * HEADS)
    quick_count = HEADS
    return shuffled < quick_count


def draw_dt_bias(key, part):
    quick_heads = head_kinds(key)
    spread = jax.random.uniform(jax.random.fold_in(key, 202), (2 * HEADS,), jnp.float32)
    return jnp.where(quick_heads, -3.0 + spread, -7.5 + spread).astype(jnp.float32)


def draw_a_log(key, part):
    quick_heads = head_kinds(key)
    spread = jax.random.uniform(jax.random.fold_in(key, 303), (2 * HEADS,), jnp.float32)
    return jnp.where(quick_heads, -1.0 + spread, -1.5 + 1.5 * spread).astype(jnp.float32)


def spiked(array, own_key, source, target, shards_of, factor):
    def block_of(position):
        return (jnp.arange(array.shape[position]) // (array.shape[position] // shards_of)).reshape((-1,) + (1,) * (array.ndim - 1 - position))

    one_side = jax.random.permutation(own_key, shards_of)[block_of(target)]
    second = (block_of(target) + shards_of // 2) % shards_of
    return jnp.where((block_of(source) == one_side) | (block_of(source) == second), factor * array, array)


def block_levels(key, shape, cuts, low, largest):
    factor_of, own = 1.0, jax.random.fold_in(key, 6)
    for axis_at, parts in cuts:
        steps = jnp.exp(jax.random.uniform(jax.random.fold_in(own, axis_at), (parts,), jnp.float32, low / len(cuts), largest / len(cuts)))
        factor_of = factor_of * jnp.repeat(steps, shape[axis_at] // parts).reshape([-1 if axis == axis_at else 1 for axis in range(len(shape))])
    return factor_of


def profile(number_of, total, bound, slope):
    loads = [(1 << 20) // math.isqrt(grade ** slope) + 1 for grade in range(2, number_of + 1)]
    spare, counts = total - bound - (number_of - 1), [1] * (number_of - 1)
    while spare > 0:
        candidates = [i for i in range(number_of - 1) if counts[i] < bound]
        mass, remaining = sum([loads[i] for i in candidates]), spare
        for i in candidates:
            more = min(bound - counts[i], max(1, remaining * loads[i] // mass), spare)
            counts[i] = counts[i] + more
            spare = spare - more
    return np.array([bound] + counts)


def uneven(key, amount, total, bound, skew):
    if amount == 2:
        one = jax.random.randint(key, (), max(1, total - bound), min(bound, total - 1) + 1)
        return jnp.stack([one, total - one])
    tallies = jnp.asarray(profile(amount, total, bound, skew), jnp.int32)
    pairs = (amount - 1) // 2
    giver, sink = tallies[1:1 + 2 * pairs:2], tallies[2:2 + 2 * pairs:2]
    slack = jnp.minimum(giver - 1, bound - sink)
    moved = jax.random.randint(jax.random.fold_in(key, 1), (pairs,), 0, 1 << 20) % (slack + 1)
    tallies = tallies.at[1:1 + 2 * pairs:2].set(giver - moved).at[2:2 + 2 * pairs:2].set(sink + moved)
    return tallies[jax.random.permutation(jax.random.fold_in(key, 2), amount)]


def bell_draw(rng, shape, deviation, most, shards=(), kind=jnp.bfloat16):
    factor_of = block_levels(rng, shape, shards, -0.22, 0.18) if shards else 1.0
    entries = jax.random.normal(rng, shape, jnp.float32) * deviation * factor_of
    return jnp.minimum(jnp.maximum(entries, -most), most).astype(kind)


def bell_draw_with(rng, extent, scale, most, cuts, heavy, held_as=jnp.bfloat16):
    values = scale * jax.random.normal(rng, extent, jnp.float32)
    if cuts:
        values = values * block_levels(rng, extent, cuts, -0.22, 0.18)
    return jnp.clip(spiked(values, jax.random.fold_in(rng, 3), *heavy), -most, most).astype(held_as)


def setup_inputs(seed: int = 0) -> dict:
    arg_keys = jax.random.split(jax.random.key(seed), 13)
    tokens = bell_draw_with(arg_keys[0], (TOKENS, D), 1.0, 6.0, ((0, 32),), (0, 1, 32, 2.75))
    segment_ids = jnp.searchsorted(jnp.cumsum(uneven(arg_keys[1], TOKENS * 4 // TOK_DEV, TOKENS, TOK_DEV, 2)), jnp.arange(TOKENS), side="right").astype(jnp.int32)
    w_in = bell_draw(arg_keys[2], (D, PROJ), D ** -0.5, 0.21875, ((0, 32),))
    w_out = bell_draw(arg_keys[3], (INNER, D), INNER ** -0.5, 0.15625, ((1, 32),))
    norm_gain = jnp.clip(1.0 + 0.15 * jax.random.normal(arg_keys[4], (D,), jnp.float32), 0.25, 1.75).astype(jnp.bfloat16)
    conv_w = bell_draw(arg_keys[5], (CONV, CHANNELS), CONV ** -0.5, 3.0, (), jnp.float32)
    conv_b = bell_draw(arg_keys[6], (CHANNELS,), 0.3, 1.5, (), jnp.float32)
    dt_bias = draw_dt_bias(jax.random.fold_in(arg_keys[12], 71), 0)
    a_log = draw_a_log(jax.random.fold_in(arg_keys[12], 71), 0)
    d_skip = jnp.clip(jax.random.uniform(arg_keys[9], (HEADS,), jnp.float32, 0.5, 1.5), 0.5, 1.5)
    out_gain = jnp.clip(1.0 + 0.15 * jax.random.normal(arg_keys[10], (INNER,), jnp.float32), 0.25, 1.75)
    cotangent = bell_draw_with(arg_keys[11], (TOKENS, D), 1.0, 6.0, ((0, 32),), (0, 1, 32, 2.75))
    return dict(tokens=tokens, segment_ids=segment_ids, w_in=w_in, w_out=w_out, norm_gain=norm_gain, conv_w=conv_w, conv_b=conv_b, dt_bias=dt_bias, a_log=a_log, d_skip=d_skip, out_gain=out_gain, cotangent=cotangent)


@jax.custom_vjp
def low(v):
    return lax.optimization_barrier(v.astype(jnp.bfloat16)).astype(jnp.float32)

@jax.custom_vjp
def low_back(v):
    return v

def low_keep(v):
    return (low(v), None)

def low_pass(kept, grad):
    return (grad,)

def back_keep(v):
    return (v, None)

def back_low(kept, grad):
    return (low(grad),)
low.defvjp(low_keep, low_pass)
low_back.defvjp(back_keep, back_low)
eps = 1e-05
highest = lax.Precision.HIGHEST

def matmul(left, right):
    return jnp.dot(left, right, precision=highest)

def conv_silu(conv_in, conv_w, conv_b, segment_ids):
    length = conv_in.shape[0]
    summed = conv_b[None, :] + conv_w[0][None, :] * conv_in
    for offset in range(1, conv_w.shape[0]):
        earlier = jnp.concatenate([jnp.zeros((offset, conv_in.shape[1]), conv_in.dtype), conv_in[:length - offset]], axis=0)
        before = jnp.concatenate([jnp.full((offset,), -1, jnp.int32), segment_ids[:length - offset].astype(jnp.int32)], axis=0)
        same_doc = (before == segment_ids.astype(jnp.int32)).astype(conv_in.dtype)
        summed = summed + conv_w[offset][None, :] * earlier * same_doc[:, None]
    return jax.nn.silu(summed)

def decays(dt_raw, dt_bias, a_log):
    head_count = dt_bias.shape[0] // 2
    step_sizes = jax.nn.softplus(dt_raw + dt_bias[None, :])
    log_rates = -step_sizes * jnp.exp(a_log)[None, :]
    cum_fwd = jnp.cumsum(log_rates[:, :head_count], axis=0)
    cum_bwd = jnp.cumsum(log_rates[:, head_count:], axis=0) - log_rates[:, head_count:]
    return (step_sizes[:, :head_count], step_sizes[:, head_count:], cum_fwd, cum_bwd)

def head_decays(lower_mask, upper_mask, cum_fwd_h, cum_bwd_h):
    fwd_gap = jnp.where(lower_mask, cum_fwd_h[:, None] - cum_fwd_h[None, :], 0.0)
    bwd_gap = jnp.where(upper_mask, cum_bwd_h[None, :] - cum_bwd_h[:, None], 0.0)
    return (jnp.where(lower_mask, jnp.exp(fwd_gap), 0.0), jnp.where(upper_mask, jnp.exp(bwd_gap), 0.0))

def mixer_layer(residual, w_in, w_out, norm_gain, conv_w, conv_b, dt_bias, a_log, d_skip, out_gain, segment_ids):
    length = residual.shape[0]
    inv_rms = lax.rsqrt(lax.optimization_barrier(jnp.mean(residual * residual, axis=1, keepdims=True)) + eps)
    normed = low(residual * inv_rms * norm_gain[None, :])
    projected = low_back(matmul(normed, w_in))
    gate_in = projected[:, :INNER]
    conv_in = projected[:, INNER:INNER + CHANNELS]
    dt_raw = projected[:, INNER + CHANNELS:]
    act = conv_silu(conv_in, conv_w, conv_b, segment_ids)
    values = act[:, :INNER]
    b_fwd = low(act[:, INNER:INNER + STATE])
    c_fwd = low(act[:, INNER + STATE:INNER + 2 * STATE])
    b_bwd = low(act[:, INNER + 2 * STATE:INNER + 3 * STATE])
    c_bwd = low(act[:, INNER + 3 * STATE:])
    dt_fwd, dt_bwd, cum_fwd, cum_bwd = decays(dt_raw, dt_bias, a_log)
    g_fwd = low_back(matmul(c_fwd, b_fwd.T))
    g_bwd = low_back(matmul(c_bwd, b_bwd.T))
    positions = jnp.arange(length, dtype=jnp.int32)
    same_seg = segment_ids[:, None] == segment_ids[None, :]
    lower_mask = same_seg & (positions[None, :] < positions[:, None])
    upper_mask = same_seg & (positions[None, :] > positions[:, None])
    values_low = low(values)
    per_head = values_low.reshape(length, HEADS, HEAD_DIM).transpose(1, 0, 2)

    def one_head(pieces):
        dt_fwd_h, dt_bwd_h, cum_fwd_h, cum_bwd_h, head_vals = pieces
        decay_fwd, decay_bwd = head_decays(lower_mask, upper_mask, cum_fwd_h, cum_bwd_h)
        mixer_head = low(g_fwd * decay_fwd * dt_fwd_h[None, :] + g_bwd * decay_bwd * dt_bwd_h[None, :])
        return matmul(mixer_head, head_vals)
    mixed_out = lax.map(jax.checkpoint(one_head), (dt_fwd.T, dt_bwd.T, cum_fwd.T, cum_bwd.T, per_head))
    mixed_out = low_back(mixed_out).transpose(1, 0, 2).reshape(length, INNER)
    ssm_out = mixed_out + values * jnp.repeat(d_skip, HEAD_DIM)[None, :]
    gated_out = ssm_out * jax.nn.silu(gate_in)
    inv_out = lax.rsqrt(lax.optimization_barrier(jnp.mean(gated_out * gated_out, axis=1, keepdims=True)) + eps)
    normed_out = low(gated_out * inv_out * out_gain[None, :])
    return residual + matmul(normed_out, w_out)

def reference(tokens, segment_ids, w_in, w_out, norm_gain, conv_w, conv_b, dt_bias, a_log, d_skip, out_gain, cotangent):
    params = (w_in.astype(jnp.float32), w_out.astype(jnp.float32), norm_gain.astype(jnp.float32), conv_w.astype(jnp.float32), conv_b.astype(jnp.float32), dt_bias.astype(jnp.float32), a_log.astype(jnp.float32), d_skip.astype(jnp.float32), out_gain.astype(jnp.float32))
    seq_count = N_FSDP * N_REP
    token_rows = tokens.reshape(seq_count, TOK_DEV, D)
    seg_rows = segment_ids.astype(jnp.int32).reshape(seq_count, TOK_DEV)
    cot_rows = cotangent.reshape(seq_count, TOK_DEV, D)

    def per_seq(totals, pieces):
        rows_in, seg_row, cot_row = pieces

        def local_layer(residual, *weights):
            return mixer_layer(residual, *weights, seg_row)
        result, pullback = jax.vjp(local_layer, rows_in.astype(jnp.float32), *params)
        gradients = pullback(cot_row.astype(jnp.float32))
        new_totals = tuple((total + grad for total, grad in zip(totals, gradients[1:])))
        return (new_totals, (result.astype(jnp.bfloat16), gradients[0]))
    zero_sums = tuple((jnp.zeros(param.shape, jnp.float32) for param in params))
    totals, (outputs, d_rows) = lax.scan(per_seq, zero_sums, (token_rows, seg_rows, cot_rows))
    return (outputs.reshape(TOKENS, D), d_rows.reshape(TOKENS, D), totals[0], totals[1], totals[2], totals[3], totals[4], totals[5], totals[6], totals[7], totals[8])
```

```python
import functools

import jax
import jax.numpy as jnp
import numpy as np
from jax import lax
from jax.experimental import pallas as pl
from jax.experimental.pallas import tpu as pltpu
from jax.sharding import PartitionSpec as P

eps = 1e-05
Q = 128
HALO = 16
f32 = jnp.float32
bf16 = jnp.bfloat16
AXES = ("fsdp", "rep")


def nn(a, b):
    return lax.dot_general(a, b, (((1,), (0,)), ((), ())), preferred_element_type=f32)


def nt(a, b):
    return lax.dot_general(a, b, (((1,), (1,)), ((), ())), preferred_element_type=f32)


def tn(a, b):
    return lax.dot_general(a, b, (((0,), (0,)), ((), ())), preferred_element_type=f32)


def split2(x):
    hi = x.astype(bf16)
    lo = (x - hi.astype(f32)).astype(bf16)
    return jnp.concatenate([hi, lo], axis=1)


def split_rows(x):
    hi = x.astype(bf16)
    return jnp.concatenate([hi, (x - hi.astype(f32)).astype(bf16)], axis=0)


def nn_exact(ones_mask, x):
    hi = x.astype(bf16)
    r = x - hi.astype(f32)
    mid = r.astype(bf16)
    lo = (r - mid.astype(f32)).astype(bf16)
    return nn(ones_mask, hi) + (nn(ones_mask, mid) + nn(ones_mask, lo))


def iotas(shape):
    return (
        lax.broadcasted_iota(jnp.int32, shape, 0),
        lax.broadcasted_iota(jnp.int32, shape, 1),
    )


def front_kernel(
    sizes,
    tok_ref, halo_ref, gain_ref, w_ref, cw_ref, cb_ref, dtb_ref, rate_ref, aux_ref, x2_ref,
    normed_ref, gate_ref, conv_ref, act_ref, low_ref, dsil_ref, dt_ref, cum_ref, dtraw_ref, sb_ref,
    ext_ref, state_ref,
):
    inner, channels, heads, state = sizes
    step = pl.program_id(0)

    @pl.when(step == 0)
    def _():
        state_ref[...] = jnp.zeros_like(state_ref)

    gain = gain_ref[...]

    def norm(x):
        x = x.astype(f32)
        inv = lax.rsqrt(jnp.mean(x * x, axis=1, keepdims=True) + eps)
        return (x * inv * gain).astype(bf16)

    normed = norm(tok_ref[...])
    normed_ref[...] = normed
    both = jnp.concatenate([norm(halo_ref[...]), normed], axis=0)
    gate_ref[...] = nn(normed, w_ref[:, :inner])
    dt_raw = nn(normed, w_ref[:, inner + channels :])
    dtraw_ref[...] = dt_raw
    aux = aux_ref[...]
    m1, m2, m3 = aux[:, 0:1], aux[:, 1:2], aux[:, 2:3]
    block = 256
    for at in range(0, channels, block):
        sl = slice(at, at + block)
        ext_ref[:, sl] = nn(both, w_ref[:, inner + at : inner + at + block])
        x0 = ext_ref[HALO : HALO + Q, sl]
        conv_ref[:, sl] = x0
        pre = cb_ref[:, sl] + cw_ref[0:1, sl] * x0
        pre += cw_ref[1:2, sl] * (ext_ref[HALO - 1 : HALO - 1 + Q, sl] * m1)
        pre += cw_ref[2:3, sl] * (ext_ref[HALO - 2 : HALO - 2 + Q, sl] * m2)
        pre += cw_ref[3:4, sl] * (ext_ref[HALO - 3 : HALO - 3 + Q, sl] * m3)
        sig = 1.0 / (1.0 + jnp.exp(-pre))
        act = pre * sig
        act_ref[:, sl] = act
        low_ref[:, sl] = act.astype(bf16)
        dsil_ref[:, sl] = sig * (1.0 + pre * (1.0 - sig))
    v = dt_raw + dtb_ref[...]
    dt = jnp.maximum(v, 0.0) + jnp.log1p(jnp.exp(-jnp.abs(v)))
    dt_ref[...] = dt
    rate = -dt * rate_ref[...]
    row, col = iotas((Q, Q))
    cum = nn_exact((col <= row).astype(bf16), rate)
    cum_ref[...] = cum
    sb_ref[0] = state_ref[...].astype(bf16)
    weight = dt[:, heads:] * jnp.exp(cum[:, heads:] - rate[:, heads:]) * aux[:, 5:6]
    whole = jnp.exp(cum[Q - 1 :, heads:]) * aux[0:1, 7:8]
    scales = split2(jnp.concatenate([weight, jnp.broadcast_to(whole, (8, heads))], axis=0))
    b_bwd = low_ref[:, inner + 2 * state : inner + 3 * state]
    for at in range(0, inner, block):
        sl = slice(at, at + block)
        wide = nn(scales, x2_ref[:, sl])
        vs = (low_ref[:, sl].astype(f32) * wide[:Q]).astype(bf16)
        state_ref[:, sl] = state_ref[:, sl] * wide[Q : Q + 1] + tn(b_bwd, vs)


def front(tokens, gain_row, w_in, conv_w, conv_b, dt_bias, rate_row, aux, x2, sizes):
    inner, channels, heads, state = sizes
    t, d = tokens.shape
    n = t // Q
    proj = w_in.shape[1]
    rev = lambda i: (n - 1 - i, 0)
    fixed = lambda i: (0, 0)
    blk = lambda width: pl.BlockSpec((Q, width), rev)
    whole = lambda a: pl.BlockSpec(a.shape, fixed)
    per = Q // HALO
    out = lambda width, dtype: jax.ShapeDtypeStruct((t, width), dtype)
    return pl.pallas_call(
        functools.partial(front_kernel, sizes),
        grid=(n,),
        in_specs=[
            blk(d),
            pl.BlockSpec((HALO, d), lambda i: (jnp.maximum((n - 1 - i) * per - 1, 0), 0)),
            whole(gain_row), whole(w_in), whole(conv_w), whole(conv_b), whole(dt_bias), whole(rate_row),
            blk(aux.shape[1]), whole(x2),
        ],
        out_specs=[
            blk(d), blk(inner), blk(channels), blk(channels), blk(channels), blk(channels),
            blk(2 * heads), blk(2 * heads), blk(2 * heads),
            pl.BlockSpec((1, state, inner), lambda i: (n - 1 - i, 0, 0)),
        ],
        out_shape=[
            out(d, bf16), out(inner, f32), out(channels, f32), out(channels, f32), out(channels, bf16), out(channels, f32),
            out(2 * heads, f32), out(2 * heads, f32), out(2 * heads, f32),
            jax.ShapeDtypeStruct((n, state, inner), bf16),
        ],
        scratch_shapes=[pltpu.VMEM((HALO + Q, channels), f32), pltpu.VMEM((state, inner), f32)],
        compiler_params=pltpu.CompilerParams(
            dimension_semantics=("arbitrary",), vmem_limit_bytes=60 * 1024 * 1024
        ),
        cost_estimate=pl.CostEstimate(flops=2 * t * d * proj, bytes_accessed=50_000_000, transcendentals=0),
    )(tokens, tokens, gain_row, w_in, conv_w, conv_b, dt_bias, rate_row, aux, x2)


def middle_kernel(
    sizes,
    tok_ref, act_ref, gate_ref, dt_ref, cum_ref, aux_ref, segrow_ref, cot_ref, sb_ref, w_ref,
    rate_ref, skip_ref, og_ref, x2_ref, r_ref,
    out_ref, nout_ref, dgate_ref, dy_ref, dv_ref, dbc_ref, drate_ref, dq_ref, sf_ref, dog_ref, dsk_ref,
    decay_ref, mix_ref, state_ref, adj_ref, ssm_ref, gated_ref, dno_ref, yf_ref, yb_ref, wide_ref,
    p_ref, q_ref, scal_ref,
):
    inner, channels, heads, state = sizes
    quad = 256
    step = pl.program_id(0)

    @pl.when(step == 0)
    def _():
        state_ref[...] = jnp.zeros_like(state_ref)
        adj_ref[...] = jnp.zeros_like(adj_ref)
        dog_ref[...] = jnp.zeros_like(dog_ref)
        dsk_ref[...] = jnp.zeros_like(dsk_ref)
        q_ref[...] = jnp.zeros_like(q_ref)

    sf_ref[0] = state_ref[...].astype(bf16)
    aux = aux_ref[...]
    row, col = iotas((Q, Q))
    lower = col < row
    same = aux[:, 3:4] == segrow_ref[0]
    b_f = act_ref[:, inner : inner + state].astype(bf16)
    c_f = act_ref[:, inner + state : inner + 2 * state].astype(bf16)
    b_b = act_ref[:, inner + 2 * state : inner + 3 * state].astype(bf16)
    c_b = act_ref[:, inner + 3 * state :].astype(bf16)
    g = jnp.where(same & (col != row), jnp.where(lower, nt(c_f, b_f), nt(c_b, b_b)), 0.0)
    dt = dt_ref[...]
    cum = cum_ref[...]
    rate = -dt * rate_ref[...]
    cf, cb = cum[:, :heads], cum[:, heads:] - rate[:, heads:]
    dtf, dtb = dt[:, :heads], dt[:, heads:]
    total_f, total_b = cum[Q - 1 :, :heads], cum[Q - 1 :, heads:]
    ldt = jnp.log(jnp.maximum(dt, 1e-37))
    rows = jnp.transpose(
        jnp.concatenate(
            [cf - ldt[:, :heads], cb + ldt[:, heads:], jnp.zeros((Q, Q - 2 * heads), f32)], axis=1
        )
    )
    scales = split2(
        jnp.concatenate(
            [
                jnp.exp(cf) * aux[:, 6:7],
                jnp.exp(total_b - cb) * aux[:, 7:8],
                dtf * jnp.exp(total_f - cf) * aux[:, 4:5],
                dtb * jnp.exp(cb) * aux[:, 5:6],
                jnp.broadcast_to(jnp.exp(total_f) * aux[Q - 1 :, 6:7], (8, heads)),
                jnp.broadcast_to(jnp.exp(total_b) * aux[0:1, 7:8], (8, heads)),
            ],
            axis=0,
        )
    )
    lane = lax.broadcasted_iota(jnp.int32, (1, Q), 1)
    first = (lane < Q // 2).astype(bf16)
    second = (lane >= Q // 2).astype(bf16)

    def apart(x):
        return jnp.concatenate([x * first, x * second], axis=0)

    squares = jnp.zeros((Q, quad), f32)
    dots = jnp.zeros((Q, quad), f32)
    cot = cot_ref[...]
    for at in range(0, inner, quad):
        sl = slice(at, at + quad)
        wide_ref[:, sl] = nn(scales, x2_ref[:, sl])
        v = act_ref[:, sl]
        low = v.astype(bf16)
        yf = nn(c_f, state_ref[:, sl].astype(bf16)) * wide_ref[:Q, sl]
        yb = nn(c_b, sb_ref[0, :, sl]) * wide_ref[Q : 2 * Q, sl]
        yf_ref[:, sl] = yf
        yb_ref[:, sl] = yb
        parts = []
        for half in range(2):
            mixes = []
            for h in (at // 64 + 2 * half, at // 64 + 2 * half + 1):
                gap = jnp.where(
                    lower,
                    cf[:, h : h + 1] - rows[h : h + 1, :],
                    rows[heads + h : heads + h + 1, :] - cb[:, h : h + 1],
                )
                decay = jnp.exp(gap)
                decay_ref[h] = decay
                mix = (g * decay).astype(bf16)
                mix_ref[h * Q : (h + 1) * Q, :] = mix
                mixes.append(mix)
            parts.append(
                nn(jnp.concatenate(mixes, axis=1), apart(low[:, half * Q : (half + 1) * Q]))
            )
        ssm = jnp.concatenate(parts, axis=1) + yf + yb + skip_ref[:, sl] * v
        ssm_ref[:, sl] = ssm
        gate = gate_ref[:, sl]
        gated = ssm * (gate / (1.0 + jnp.exp(-gate)))
        gated_ref[:, sl] = gated
        dno = nn(cot, w_ref[:, sl])
        dno_ref[:, sl] = dno
        squares += gated * gated
        dots += dno * og_ref[:, sl] * gated

    inv = lax.rsqrt(jnp.sum(squares, axis=1, keepdims=True) / inner + eps)
    drag = inv * (inv * jnp.sum(dots, axis=1, keepdims=True) / inner)
    dg = jnp.zeros((Q, Q), f32)
    d_cf = jnp.zeros((Q, state), f32)
    d_cb = jnp.zeros((Q, state), f32)
    d_bb = jnp.zeros((Q, state), f32)
    heads_of = jnp.zeros((3 * Q, Q), f32)
    for at in range(0, inner, quad):
        sl = slice(at, at + quad)
        v = act_ref[:, sl]
        low = v.astype(bf16)
        low_f = low.astype(f32)
        ssm, gate, gated, dno = ssm_ref[:, sl], gate_ref[:, sl], gated_ref[:, sl], dno_ref[:, sl]
        og = og_ref[:, sl]
        unit = gated * inv
        nout_ref[:, sl] = (unit * og).astype(bf16)
        dog_ref[:, sl] += jnp.sum(dno * unit, axis=0, keepdims=True)
        d_gated = inv * (dno * og) - gated * (inv * drag)
        sig = 1.0 / (1.0 + jnp.exp(-gate))
        d_ssm = d_gated * (gate * sig)
        dgate_ref[:, sl] = (d_gated * ssm * (sig * (1.0 + gate * (1.0 - sig)))).astype(bf16)
        dsk_ref[:, sl] += jnp.sum(d_ssm * v, axis=0, keepdims=True)
        dy = d_ssm.astype(bf16)
        dy_ref[:, sl] = dy
        dy_f = dy.astype(f32)
        parts = []
        for half in range(2):
            h0 = at // 64 + 2 * half
            cut = slice(half * Q, (half + 1) * Q)
            d_mix = nt(dy[:, cut], apart(low[:, cut]))
            for i in range(2):
                h = h0 + i
                x = d_mix[:, i * Q : (i + 1) * Q] * decay_ref[h]
                dg += x
                full = x * g
                under = jnp.where(lower, full, 0.0)
                over = full - under
                q_ref[h : h + 1, :] = jnp.sum(under, axis=0, keepdims=True)
                q_ref[heads + h : heads + h + 1, :] = jnp.sum(over, axis=0, keepdims=True)
                p_ref[:, h : h + 1] = jnp.sum(under, axis=1, keepdims=True)
                p_ref[:, heads + h : heads + h + 1] = jnp.sum(over, axis=1, keepdims=True)
            parts.append(tn(mix_ref[h0 * Q : (h0 + 2) * Q, :], apart(dy[:, cut])))
        adj = adj_ref[:, sl]
        adj_low = adj.astype(bf16)
        sf_low = state_ref[:, sl].astype(bf16)
        sb_low = sb_ref[0, :, sl]
        wide_wb = wide_ref[3 * Q : 4 * Q, sl]
        dvb = wide_wb * nn(b_b, adj_low)
        dv_ref[:, sl] = d_ssm * skip_ref[:, sl] + jnp.concatenate(parts, axis=1) + dvb
        prods = jnp.concatenate(
            [
                (dy_f * yf_ref[:, sl]).astype(bf16),
                (dy_f * yb_ref[:, sl]).astype(bf16),
                (low_f * dvb).astype(bf16),
            ],
            axis=0,
        )
        heads_of += nn(prods, r_ref[sl, :])
        dye_f = (dy_f * wide_ref[:Q, sl]).astype(bf16)
        dye_b = (dy_f * wide_ref[Q : 2 * Q, sl]).astype(bf16)
        vs_f = (low_f * wide_ref[2 * Q : 3 * Q, sl]).astype(bf16)
        vs_b = (low_f * wide_wb).astype(bf16)
        d_cf += nt(dye_f, sf_low)
        d_cb += nt(dye_b, sb_low)
        d_bb += nt(vs_b, adj_low)
        across_b = wide_ref[4 * Q + 8 : 4 * Q + 9, sl]
        scal_ref[:, sl] = jnp.sum(adj * sb_low.astype(f32), axis=0, keepdims=True) * across_b
        adj_ref[:, sl] = adj * across_b + tn(c_b, dye_b)
        state_ref[:, sl] = state_ref[:, sl] * wide_ref[4 * Q : 4 * Q + 1, sl] + tn(b_f, vs_f)

    out_ref[...] = (tok_ref[...].astype(f32) + nt(nout_ref[...], w_ref[...])).astype(bf16)
    dg = jnp.where(same & (col != row), dg, 0.0)
    dg_f = jnp.where(lower, dg, 0.0)
    dg_b = (dg - dg_f).astype(bf16)
    dg_f = dg_f.astype(bf16)
    dbc_ref[...] = jnp.concatenate(
        [tn(dg_f, c_f), d_cf + nn(dg_f, b_f), d_bb + tn(dg_b, c_b), d_cb + nn(dg_b, b_b)], axis=1
    )
    q_cols = jnp.transpose(q_ref[...])[:, : 2 * heads]
    dots_f, dots_b, dots_v = heads_of[:Q, :heads], heads_of[Q : 2 * Q, :heads], heads_of[2 * Q :, :heads]
    through = nn(split_rows(jnp.broadcast_to(scal_ref[...], (8, inner))), r_ref[...])
    through = (through[0:1] + through[8:9])[:, :heads]
    diff = p_ref[:, : 2 * heads] - q_cols
    d_rate_f = nn_exact((col >= row).astype(bf16), diff[:, :heads] + dots_f)
    d_rate_b = (
        nn_exact((col <= row).astype(bf16), diff[:, heads:] + dots_b)
        + nn_exact((col > row).astype(bf16), dots_v)
        + through
    )
    drate_ref[...] = jnp.concatenate([d_rate_f, d_rate_b], axis=1)
    dq_ref[...] = jnp.concatenate([q_cols[:, :heads], q_cols[:, heads:] + dots_v], axis=1)


def middle(tokens, act, gate, dt, cum, aux, segrow, cot, sb, w_out_t, rate_row, skip_row, og_row, x2, r, sizes):
    inner, channels, heads, state = sizes
    t, d = tokens.shape
    n = t // Q
    fwd = lambda i: (i, 0)
    fixed = lambda i: (0, 0)
    cube = lambda i: (i, 0, 0)
    blk = lambda width: pl.BlockSpec((Q, width), fwd)
    whole = lambda a: pl.BlockSpec(a.shape, fixed)
    out = lambda width, dtype: jax.ShapeDtypeStruct((t, width), dtype)
    line = jax.ShapeDtypeStruct((1, inner), f32)
    return pl.pallas_call(
        functools.partial(middle_kernel, sizes),
        grid=(n,),
        in_specs=[
            blk(d), blk(channels), blk(inner), blk(2 * heads), blk(2 * heads), blk(aux.shape[1]),
            pl.BlockSpec((1, 1, Q), cube), blk(d), pl.BlockSpec((1, state, inner), cube),
            whole(w_out_t), whole(rate_row), whole(skip_row), whole(og_row), whole(x2), whole(r),
        ],
        out_specs=[
            blk(d), blk(inner), blk(inner), blk(inner), blk(inner), blk(4 * state),
            blk(2 * heads), blk(2 * heads), pl.BlockSpec((1, state, inner), cube),
            pl.BlockSpec((1, inner), fixed), pl.BlockSpec((1, inner), fixed),
        ],
        out_shape=[
            out(d, bf16), out(inner, bf16), out(inner, bf16), out(inner, bf16), out(inner, f32),
            out(4 * state, f32), out(2 * heads, f32), out(2 * heads, f32),
            jax.ShapeDtypeStruct((n, state, inner), bf16), line, line,
        ],
        scratch_shapes=[
            pltpu.VMEM((heads, Q, Q), f32),
            pltpu.VMEM((heads * Q, Q), bf16),
            pltpu.VMEM((state, inner), f32),
            pltpu.VMEM((state, inner), f32),
            pltpu.VMEM((Q, inner), f32),
            pltpu.VMEM((Q, inner), f32),
            pltpu.VMEM((Q, inner), f32),
            pltpu.VMEM((Q, inner), f32),
            pltpu.VMEM((Q, inner), f32),
            pltpu.VMEM((4 * Q + 16, inner), f32),
            pltpu.VMEM((Q, Q), f32),
            pltpu.VMEM((Q, Q), f32),
            pltpu.VMEM((1, inner), f32),
        ],
        compiler_params=pltpu.CompilerParams(
            dimension_semantics=("arbitrary",), vmem_limit_bytes=60 * 1024 * 1024
        ),
        cost_estimate=pl.CostEstimate(flops=30_000_000_000, bytes_accessed=60_000_000, transcendentals=0),
    )(tokens, act, gate, dt, cum, aux, segrow, cot, sb, w_out_t, rate_row, skip_row, og_row, x2, r)


def back_kernel(
    sizes,
    tok_ref, cot_ref, gain_ref, w_ref, cw_ref, dtb_ref, rate_ref, aux_ref, x2_ref, r_ref,
    low_ref, dsil_ref, conv_ref, dt_ref, cum_ref, dtraw_ref,
    dgate_ref, dy_ref, dv_ref, dbc_ref, drate_ref, dq_ref, sf_ref,
    dproj_ref, dtok_ref, dgain_ref, dcw_ref, dcb_ref, ddtb_ref, dalog_ref,
    adj_ref, dpre_ref, scal_ref,
):
    inner, channels, heads, state = sizes
    quad = 256
    step = pl.program_id(0)

    @pl.when(step == 0)
    def _():
        adj_ref[...] = jnp.zeros_like(adj_ref)
        dpre_ref[...] = jnp.zeros_like(dpre_ref)
        dgain_ref[...] = jnp.zeros_like(dgain_ref)
        dcw_ref[...] = jnp.zeros_like(dcw_ref)
        dcb_ref[...] = jnp.zeros_like(dcb_ref)
        ddtb_ref[...] = jnp.zeros_like(ddtb_ref)
        dalog_ref[...] = jnp.zeros_like(dalog_ref)

    dpre_ref[Q:, :] = dpre_ref[0:8, :]
    aux = aux_ref[...]
    dt = dt_ref[...]
    cum = cum_ref[...]
    cf, dtf = cum[:, :heads], dt[:, :heads]
    total_f = cf[Q - 1 :, :]
    scales = split2(
        jnp.concatenate(
            [
                jnp.exp(cf) * aux[:, 6:7],
                dtf * jnp.exp(total_f - cf) * aux[:, 4:5],
                jnp.broadcast_to(jnp.exp(total_f) * aux[Q - 1 :, 6:7], (8, heads)),
            ],
            axis=0,
        )
    )
    b_f = low_ref[:, inner : inner + state]
    c_f = low_ref[:, inner + state : inner + 2 * state]
    dots = jnp.zeros((Q, Q), f32)
    d_bf = jnp.zeros((Q, state), f32)
    for at in range(0, inner, quad):
        sl = slice(at, at + quad)
        wide = nn(scales, x2_ref[:, sl])
        low_f = low_ref[:, sl].astype(f32)
        adj = adj_ref[:, sl]
        adj_low = adj.astype(bf16)
        wide_wf = wide[Q : 2 * Q]
        dvf = wide_wf * nn(b_f, adj_low)
        dots += nn((low_f * dvf).astype(bf16), r_ref[sl, :])
        d_bf += nt((low_f * wide_wf).astype(bf16), adj_low)
        across = wide[2 * Q : 2 * Q + 1]
        scal_ref[:, sl] = jnp.sum(adj * sf_ref[0, :, sl].astype(f32), axis=0, keepdims=True) * across
        dye = (dy_ref[:, sl].astype(f32) * wide[:Q]).astype(bf16)
        adj_ref[:, sl] = adj * across + tn(c_f, dye)
        dpre_ref[:Q, sl] = (dv_ref[:, sl] + dvf) * dsil_ref[:, sl]
    d_bc = dbc_ref[...] + jnp.concatenate([d_bf, jnp.zeros((Q, 3 * state), f32)], axis=1)
    dpre_ref[:Q, inner:] = d_bc * dsil_ref[:, inner:]

    n1, n2, n3 = aux[:, 8:9], aux[:, 9:10], aux[:, 10:11]
    for at in range(0, channels, quad):
        sl = slice(at, at + quad)
        conv = conv_ref[:, sl]
        z = dpre_ref[:Q, sl]
        dcb_ref[:, sl] += jnp.sum(z, axis=0, keepdims=True)
        dcw_ref[0:1, sl] += jnp.sum(z * conv, axis=0, keepdims=True)
        total = cw_ref[0:1, sl] * z
        for k, mask in ((1, n1), (2, n2), (3, n3)):
            z = dpre_ref[k : Q + k, sl] * mask
            dcw_ref[k : k + 1, sl] += jnp.sum(z * conv, axis=0, keepdims=True)
            total += cw_ref[k : k + 1, sl] * z
        dproj_ref[:, inner + at : inner + at + quad] = total.astype(bf16)
    dproj_ref[:, :inner] = dgate_ref[...]

    row, col = iotas((Q, Q))
    through = nn(split_rows(jnp.broadcast_to(scal_ref[...], (8, inner))), r_ref[...])
    through = (through[0:1] + through[8:9])[:, :heads]
    dots = dots[:, :heads]
    extra = nn_exact((col < row).astype(bf16), dots) + through
    none = jnp.zeros((Q, heads), f32)
    d_rate = drate_ref[...] + jnp.concatenate([extra, none], axis=1)
    d_dt = dq_ref[...] + jnp.concatenate([dots, none], axis=1)
    d_dt = jnp.where(dt > 0.0, d_dt / jnp.maximum(dt, 1e-37), 0.0)
    a = rate_ref[...]
    v = dtraw_ref[...] + dtb_ref[...]
    d_v = (d_dt - d_rate * a) / (1.0 + jnp.exp(-v))
    ddtb_ref[...] += jnp.sum(d_v, axis=0, keepdims=True)
    dalog_ref[...] += jnp.sum(d_rate * (-dt * a), axis=0, keepdims=True)
    dproj_ref[:, inner + channels :] = d_v.astype(bf16)

    d_normed = (
        nt(dproj_ref[:, :inner], w_ref[:, :inner])
        + nt(dproj_ref[:, inner : inner + channels], w_ref[:, inner : inner + channels])
        + nt(dproj_ref[:, inner + channels :], w_ref[:, inner + channels :])
    )
    x = tok_ref[...].astype(f32)
    inv = lax.rsqrt(jnp.mean(x * x, axis=1, keepdims=True) + eps)
    unit = x * inv
    dgain_ref[...] += jnp.sum(d_normed * unit, axis=0, keepdims=True)
    a = d_normed * gain_ref[...]
    dtok_ref[...] = cot_ref[...].astype(f32) + inv * (a - unit * jnp.mean(a * unit, axis=1, keepdims=True))


def back(
    tokens, cot, gain_row, w_in, conv_w, dt_bias, rate_row, aux, x2, r, low, dsil, conv, dt, cum, dtraw,
    dgate, dy, dv, dbc, drate, dq, sf, sizes,
):
    inner, channels, heads, state = sizes
    t, d = tokens.shape
    n = t // Q
    proj = w_in.shape[1]
    rev = lambda i: (n - 1 - i, 0)
    fixed = lambda i: (0, 0)
    blk = lambda a: pl.BlockSpec((Q, a.shape[1]), rev)
    whole = lambda a: pl.BlockSpec(a.shape, fixed)
    lines = [(1, d), (conv_w.shape[0], channels), (1, channels), (1, 2 * heads), (1, 2 * heads)]
    return pl.pallas_call(
        functools.partial(back_kernel, sizes),
        grid=(n,),
        in_specs=[
            blk(tokens), blk(cot), whole(gain_row), whole(w_in), whole(conv_w), whole(dt_bias), whole(rate_row),
            blk(aux), whole(x2), whole(r), blk(low), blk(dsil), blk(conv), blk(dt), blk(cum), blk(dtraw),
            blk(dgate), blk(dy), blk(dv), blk(dbc), blk(drate), blk(dq),
            pl.BlockSpec((1, state, inner), lambda i: (n - 1 - i, 0, 0)),
        ],
        out_specs=[pl.BlockSpec((Q, proj), rev), pl.BlockSpec((Q, d), rev)]
        + [pl.BlockSpec(s, fixed) for s in lines],
        out_shape=[jax.ShapeDtypeStruct((t, proj), bf16), jax.ShapeDtypeStruct((t, d), f32)]
        + [jax.ShapeDtypeStruct(s, f32) for s in lines],
        scratch_shapes=[
            pltpu.VMEM((state, inner), f32),
            pltpu.VMEM((Q + 8, channels), f32),
            pltpu.VMEM((1, inner), f32),
        ],
        compiler_params=pltpu.CompilerParams(
            dimension_semantics=("arbitrary",), vmem_limit_bytes=60 * 1024 * 1024
        ),
        cost_estimate=pl.CostEstimate(flops=20_000_000_000, bytes_accessed=60_000_000, transcendentals=0),
    )(
        tokens, cot, gain_row, w_in, conv_w, dt_bias, rate_row, aux, x2, r, low, dsil, conv, dt, cum, dtraw,
        dgate, dy, dv, dbc, drate, dq, sf,
    )


def features(segment_ids):
    t = segment_ids.shape[0]
    n = t // Q
    seg = segment_ids.astype(f32)
    earlier = [jnp.concatenate([jnp.full((k,), -1.0, f32), seg[: t - k]]) == seg for k in (1, 2, 3)]
    later = [jnp.concatenate([seg[k:], jnp.full((k,), -1.0, f32)]) == seg for k in (1, 2, 3)]
    chunks = seg.reshape(n, Q)
    ends, starts = chunks[:, -1:], chunks[:, :1]
    none = jnp.full((1, 1), -1.0, f32)
    like = lambda edge: (chunks == edge).reshape(t)
    columns = earlier + [
        seg,
        like(ends),
        like(starts),
        like(jnp.concatenate([none, ends[:-1]])),
        like(jnp.concatenate([starts[1:], none])),
    ] + later
    aux = jnp.stack([c.astype(f32) for c in columns], axis=1)
    return aux, chunks.reshape(n, 1, Q)


def local(tokens, segment_ids, w_in, w_out_t, gain, conv_w, conv_b, dt_bias, a_log, d_skip, out_gain, cotangent):
    heads = d_skip.shape[0]
    inner = out_gain.shape[0]
    channels = conv_w.shape[1]
    state = (channels - inner) // 4
    width = inner // heads
    sizes = (inner, channels, heads, state)
    aux, segrow = features(segment_ids)
    spread = np.arange(inner)[None, :] // width == np.arange(heads)[:, None]
    x2 = jnp.asarray(np.concatenate([spread, spread], axis=0), bf16)
    r = jnp.asarray(np.pad(spread.T, ((0, 0), (0, Q - heads))), bf16)
    gain_row = gain.astype(f32)[None, :]
    rate_row = jnp.exp(a_log)[None, :]
    dtb_row = dt_bias[None, :]
    skip_row = jnp.repeat(d_skip, width)[None, :]
    normed, gate, conv, act, low, dsil, dt, cum, dtraw, sb = front(
        tokens, gain_row, w_in, conv_w, conv_b[None, :], dtb_row, rate_row, aux, x2, sizes
    )
    output, nout, dgate, dy, dv, dbc, drate, dq, sf, d_og, d_sk = middle(
        tokens, act, gate, dt, cum, aux, segrow, cotangent, sb, w_out_t, rate_row, skip_row,
        out_gain[None, :], x2, r, sizes,
    )
    d_w_out_t = tn(cotangent, nout)
    dproj, d_tokens, d_gain, d_cw, d_cb, d_dtb, d_alog = back(
        tokens, cotangent, gain_row, w_in, conv_w, dtb_row, rate_row, aux, x2, r, low, dsil, conv, dt, cum, dtraw,
        dgate, dy, dv, dbc, drate, dq, sf, sizes,
    )
    d_w_in = tn(normed, dproj)
    d_sk = jnp.sum(d_sk.reshape(heads, width), axis=1)
    return output, d_tokens, d_w_in, d_w_out_t, d_gain[0], (d_cw, d_cb[0], d_dtb[0], d_alog[0], d_sk, d_og[0])


def body(tokens, segment_ids, w_in, w_out, norm_gain, conv_w, conv_b, dt_bias, a_log, d_skip, out_gain, cotangent):
    full_in = lax.all_gather(w_in, AXES, axis=0, tiled=True)
    full_out_t = lax.all_gather(w_out.T, AXES, axis=0, tiled=True)
    full_gain = lax.all_gather(norm_gain, AXES, axis=0, tiled=True)
    output, d_tokens, g_in, g_out_t, g_gain, small = local(
        tokens, segment_ids, full_in, full_out_t, full_gain, conv_w, conv_b, dt_bias, a_log, d_skip, out_gain,
        cotangent,
    )
    d_w_in = lax.psum_scatter(g_in, AXES, scatter_dimension=0, tiled=True)
    d_w_out = lax.psum_scatter(g_out_t, AXES, scatter_dimension=0, tiled=True).T
    d_gain = lax.psum_scatter(g_gain, AXES, scatter_dimension=0, tiled=True)
    small = lax.psum(small, AXES)
    return (output, d_tokens, d_w_in, d_w_out, d_gain) + tuple(small)


def solution(mesh):
    rows, cols, line, none = P(AXES, None), P(None, AXES), P(AXES), P()
    return jax.shard_map(
        body,
        mesh=mesh,
        in_specs=(rows, line, rows, cols, line, none, none, none, none, none, none, rows),
        out_specs=(rows, rows, rows, cols, line, none, none, none, none, none, none),
        check_vma=False,
    )
```

```python
import functools

import jax
import jax.numpy as jnp
import numpy as np
from jax import lax
from jax.experimental import pallas as pl
from jax.experimental.pallas import tpu as pltpu
from jax.sharding import PartitionSpec as P

eps = 1e-05
Q = 128
HALO = 16
f32 = jnp.float32
bf16 = jnp.bfloat16
AXES = ("fsdp", "rep")
BIAS_AT, LOG_AT, SKIP_AT = 768, 896, 1024


def nn(a, b):
    return lax.dot_general(a, b, (((1,), (0,)), ((), ())), preferred_element_type=f32)


def nt(a, b):
    return lax.dot_general(a, b, (((1,), (1,)), ((), ())), preferred_element_type=f32)


def tn(a, b):
    return lax.dot_general(a, b, (((0,), (0,)), ((), ())), preferred_element_type=f32)


def split2(x):
    hi = x.astype(bf16)
    lo = (x - hi.astype(f32)).astype(bf16)
    return jnp.concatenate([hi, lo], axis=1)


def split_rows(x):
    hi = x.astype(bf16)
    return jnp.concatenate([hi, (x - hi.astype(f32)).astype(bf16)], axis=0)


def nn_exact(ones_mask, x):
    hi = x.astype(bf16)
    r = x - hi.astype(f32)
    mid = r.astype(bf16)
    lo = (r - mid.astype(f32)).astype(bf16)
    return nn(ones_mask, hi) + (nn(ones_mask, mid) + nn(ones_mask, lo))


def iotas(shape):
    return (
        lax.broadcasted_iota(jnp.int32, shape, 0),
        lax.broadcasted_iota(jnp.int32, shape, 1),
    )


def front_kernel(
    sizes,
    tok_ref, halo_ref, gain_ref, w_ref, cw_ref, cb_ref, dtb_ref, rate_ref, aux_ref, x2_ref,
    normed_ref, gate_ref, conv_ref, act_ref, low_ref, dsil_ref, dt_ref, cum_ref, dtraw_ref, sb_ref,
    ext_ref, state_ref,
):
    inner, channels, heads, state = sizes
    step = pl.program_id(0)

    @pl.when(step == 0)
    def _():
        state_ref[...] = jnp.zeros_like(state_ref)

    gain = gain_ref[...]

    def norm(x):
        x = x.astype(f32)
        inv = lax.rsqrt(jnp.mean(x * x, axis=1, keepdims=True) + eps)
        return (x * inv * gain).astype(bf16)

    normed = norm(tok_ref[...])
    normed_ref[...] = normed
    both = jnp.concatenate([norm(halo_ref[...]), normed], axis=0)
    gate_ref[...] = nn(normed, w_ref[:, :inner])
    dt_raw = nn(normed, w_ref[:, inner + channels : inner + channels + 2 * heads])
    dtraw_ref[...] = dt_raw
    aux = aux_ref[...]
    m1, m2, m3 = aux[:, 0:1], aux[:, 1:2], aux[:, 2:3]
    block = 256
    for at in range(0, channels, block):
        sl = slice(at, at + block)
        ext_ref[:, sl] = nn(both, w_ref[:, inner + at : inner + at + block])
        x0 = ext_ref[HALO : HALO + Q, sl]
        conv_ref[:, sl] = x0
        pre = cb_ref[:, sl] + cw_ref[0:1, sl] * x0
        pre += cw_ref[1:2, sl] * (ext_ref[HALO - 1 : HALO - 1 + Q, sl] * m1)
        pre += cw_ref[2:3, sl] * (ext_ref[HALO - 2 : HALO - 2 + Q, sl] * m2)
        pre += cw_ref[3:4, sl] * (ext_ref[HALO - 3 : HALO - 3 + Q, sl] * m3)
        sig = 1.0 / (1.0 + jnp.exp(-pre))
        act = pre * sig
        act_ref[:, sl] = act
        low_ref[:, sl] = act.astype(bf16)
        dsil_ref[:, sl] = sig * (1.0 + pre * (1.0 - sig))
    v = dt_raw + dtb_ref[...]
    dt = jnp.maximum(v, 0.0) + jnp.log1p(jnp.exp(-jnp.abs(v)))
    dt_ref[...] = dt
    rate = -dt * rate_ref[...]
    row, col = iotas((Q, Q))
    cum = nn_exact((col <= row).astype(bf16), rate)
    cum_ref[...] = cum
    sb_ref[0] = state_ref[...].astype(bf16)
    weight = dt[:, heads:] * jnp.exp(cum[:, heads:] - rate[:, heads:]) * aux[:, 5:6]
    whole = jnp.exp(cum[Q - 1 :, heads:]) * aux[0:1, 7:8]
    scales = split2(jnp.concatenate([weight, jnp.broadcast_to(whole, (8, heads))], axis=0))
    b_bwd = low_ref[:, inner + 2 * state : inner + 3 * state]
    for at in range(0, inner, block):
        sl = slice(at, at + block)
        wide = nn(scales, x2_ref[:, sl])
        vs = (low_ref[:, sl].astype(f32) * wide[:Q]).astype(bf16)
        state_ref[:, sl] = state_ref[:, sl] * wide[Q : Q + 1] + tn(b_bwd, vs)


def front(tokens, gain_row, w_in, conv_w, conv_b, dt_bias, rate_row, aux, x2, sizes):
    inner, channels, heads, state = sizes
    t, d = tokens.shape
    n = t // Q
    proj = w_in.shape[1]
    rev = lambda i: (n - 1 - i, 0)
    fixed = lambda i: (0, 0)
    blk = lambda width: pl.BlockSpec((Q, width), rev)
    whole = lambda a: pl.BlockSpec(a.shape, fixed)
    per = Q // HALO
    out = lambda width, dtype: jax.ShapeDtypeStruct((t, width), dtype)
    return pl.pallas_call(
        functools.partial(front_kernel, sizes),
        grid=(n,),
        in_specs=[
            blk(d),
            pl.BlockSpec((HALO, d), lambda i: (jnp.maximum((n - 1 - i) * per - 1, 0), 0)),
            whole(gain_row), whole(w_in), whole(conv_w), whole(conv_b), whole(dt_bias), whole(rate_row),
            blk(aux.shape[1]), whole(x2),
        ],
        out_specs=[
            blk(d), blk(inner), blk(channels), blk(channels), blk(channels), blk(channels),
            blk(2 * heads), blk(2 * heads), blk(2 * heads),
            pl.BlockSpec((1, state, inner), lambda i: (n - 1 - i, 0, 0)),
        ],
        out_shape=[
            out(d, bf16), out(inner, f32), out(channels, f32), out(channels, f32), out(channels, bf16), out(channels, f32),
            out(2 * heads, f32), out(2 * heads, f32), out(2 * heads, f32),
            jax.ShapeDtypeStruct((n, state, inner), bf16),
        ],
        scratch_shapes=[pltpu.VMEM((HALO + Q, channels), f32), pltpu.VMEM((state, inner), f32)],
        compiler_params=pltpu.CompilerParams(
            dimension_semantics=("arbitrary",), vmem_limit_bytes=60 * 1024 * 1024
        ),
        cost_estimate=pl.CostEstimate(flops=2 * t * d * proj, bytes_accessed=50_000_000, transcendentals=0),
    )(tokens, tokens, gain_row, w_in, conv_w, conv_b, dt_bias, rate_row, aux, x2)


def middle_kernel(
    sizes,
    tok_ref, act_ref, gate_ref, dt_ref, cum_ref, aux_ref, segrow_ref, cot_ref, sb_ref, w_ref,
    rate_ref, skip_ref, og_ref, x2_ref, r_ref,
    out_ref, nout_ref, dgate_ref, dy_ref, dv_ref, dbc_ref, drate_ref, dq_ref, sf_ref, dog_ref, dsk_ref,
    decay_ref, mix_ref, state_ref, adj_ref, ssm_ref, gated_ref, dno_ref, yf_ref, yb_ref, wide_ref,
    p_ref, q_ref, scal_ref,
):
    inner, channels, heads, state = sizes
    quad = 256
    step = pl.program_id(0)

    @pl.when(step == 0)
    def _():
        state_ref[...] = jnp.zeros_like(state_ref)
        adj_ref[...] = jnp.zeros_like(adj_ref)
        dog_ref[...] = jnp.zeros_like(dog_ref)
        dsk_ref[...] = jnp.zeros_like(dsk_ref)
        q_ref[...] = jnp.zeros_like(q_ref)

    sf_ref[0] = state_ref[...].astype(bf16)
    aux = aux_ref[...]
    row, col = iotas((Q, Q))
    lower = col < row
    same = aux[:, 3:4] == segrow_ref[0]
    b_f = act_ref[:, inner : inner + state].astype(bf16)
    c_f = act_ref[:, inner + state : inner + 2 * state].astype(bf16)
    b_b = act_ref[:, inner + 2 * state : inner + 3 * state].astype(bf16)
    c_b = act_ref[:, inner + 3 * state :].astype(bf16)
    g = jnp.where(same & (col != row), jnp.where(lower, nt(c_f, b_f), nt(c_b, b_b)), 0.0)
    dt = dt_ref[...]
    cum = cum_ref[...]
    rate = -dt * rate_ref[...]
    cf, cb = cum[:, :heads], cum[:, heads:] - rate[:, heads:]
    dtf, dtb = dt[:, :heads], dt[:, heads:]
    total_f, total_b = cum[Q - 1 :, :heads], cum[Q - 1 :, heads:]
    ldt = jnp.log(jnp.maximum(dt, 1e-37))
    rows = jnp.transpose(
        jnp.concatenate(
            [cf - ldt[:, :heads], cb + ldt[:, heads:], jnp.zeros((Q, Q - 2 * heads), f32)], axis=1
        )
    )
    scales = split2(
        jnp.concatenate(
            [
                jnp.exp(cf) * aux[:, 6:7],
                jnp.exp(total_b - cb) * aux[:, 7:8],
                dtf * jnp.exp(total_f - cf) * aux[:, 4:5],
                dtb * jnp.exp(cb) * aux[:, 5:6],
                jnp.broadcast_to(jnp.exp(total_f) * aux[Q - 1 :, 6:7], (8, heads)),
                jnp.broadcast_to(jnp.exp(total_b) * aux[0:1, 7:8], (8, heads)),
            ],
            axis=0,
        )
    )
    lane = lax.broadcasted_iota(jnp.int32, (1, Q), 1)
    first = (lane < Q // 2).astype(bf16)
    second = (lane >= Q // 2).astype(bf16)

    def apart(x):
        return jnp.concatenate([x * first, x * second], axis=0)

    squares = jnp.zeros((Q, quad), f32)
    dots = jnp.zeros((Q, quad), f32)
    cot = cot_ref[...]
    for at in range(0, inner, quad):
        sl = slice(at, at + quad)
        wide_ref[:, sl] = nn(scales, x2_ref[:, sl])
        v = act_ref[:, sl]
        low = v.astype(bf16)
        yf = nn(c_f, state_ref[:, sl].astype(bf16)) * wide_ref[:Q, sl]
        yb = nn(c_b, sb_ref[0, :, sl]) * wide_ref[Q : 2 * Q, sl]
        yf_ref[:, sl] = yf
        yb_ref[:, sl] = yb
        parts = []
        for half in range(2):
            mixes = []
            for h in (at // 64 + 2 * half, at // 64 + 2 * half + 1):
                gap = jnp.where(
                    lower,
                    cf[:, h : h + 1] - rows[h : h + 1, :],
                    rows[heads + h : heads + h + 1, :] - cb[:, h : h + 1],
                )
                decay = jnp.exp(gap)
                decay_ref[h] = decay
                mix = (g * decay).astype(bf16)
                mix_ref[h * Q : (h + 1) * Q, :] = mix
                mixes.append(mix)
            parts.append(
                nn(jnp.concatenate(mixes, axis=1), apart(low[:, half * Q : (half + 1) * Q]))
            )
        ssm = jnp.concatenate(parts, axis=1) + yf + yb + skip_ref[:, sl] * v
        ssm_ref[:, sl] = ssm
        gate = gate_ref[:, sl]
        gated = ssm * (gate / (1.0 + jnp.exp(-gate)))
        gated_ref[:, sl] = gated
        dno = nn(cot, w_ref[:, sl])
        dno_ref[:, sl] = dno
        squares += gated * gated
        dots += dno * og_ref[:, sl] * gated

    inv = lax.rsqrt(jnp.sum(squares, axis=1, keepdims=True) / inner + eps)
    drag = inv * (inv * jnp.sum(dots, axis=1, keepdims=True) / inner)
    dg = jnp.zeros((Q, Q), f32)
    d_cf = jnp.zeros((Q, state), f32)
    d_cb = jnp.zeros((Q, state), f32)
    d_bb = jnp.zeros((Q, state), f32)
    heads_of = jnp.zeros((3 * Q, Q), f32)
    for at in range(0, inner, quad):
        sl = slice(at, at + quad)
        v = act_ref[:, sl]
        low = v.astype(bf16)
        low_f = low.astype(f32)
        ssm, gate, gated, dno = ssm_ref[:, sl], gate_ref[:, sl], gated_ref[:, sl], dno_ref[:, sl]
        og = og_ref[:, sl]
        unit = gated * inv
        nout_ref[:, sl] = (unit * og).astype(bf16)
        dog_ref[:, sl] += jnp.sum(dno * unit, axis=0, keepdims=True)
        d_gated = inv * (dno * og) - gated * (inv * drag)
        sig = 1.0 / (1.0 + jnp.exp(-gate))
        d_ssm = d_gated * (gate * sig)
        dgate_ref[:, sl] = (d_gated * ssm * (sig * (1.0 + gate * (1.0 - sig)))).astype(bf16)
        dsk_ref[:, sl] += jnp.sum(d_ssm * v, axis=0, keepdims=True)
        dy = d_ssm.astype(bf16)
        dy_ref[:, sl] = dy
        dy_f = dy.astype(f32)
        parts = []
        for half in range(2):
            h0 = at // 64 + 2 * half
            cut = slice(half * Q, (half + 1) * Q)
            d_mix = nt(dy[:, cut], apart(low[:, cut]))
            for i in range(2):
                h = h0 + i
                x = d_mix[:, i * Q : (i + 1) * Q] * decay_ref[h]
                dg += x
                full = x * g
                under = jnp.where(lower, full, 0.0)
                over = full - under
                q_ref[h : h + 1, :] = jnp.sum(under, axis=0, keepdims=True)
                q_ref[heads + h : heads + h + 1, :] = jnp.sum(over, axis=0, keepdims=True)
                p_ref[:, h : h + 1] = jnp.sum(under, axis=1, keepdims=True)
                p_ref[:, heads + h : heads + h + 1] = jnp.sum(over, axis=1, keepdims=True)
            parts.append(tn(mix_ref[h0 * Q : (h0 + 2) * Q, :], apart(dy[:, cut])))
        adj = adj_ref[:, sl]
        adj_low = adj.astype(bf16)
        sf_low = state_ref[:, sl].astype(bf16)
        sb_low = sb_ref[0, :, sl]
        wide_wb = wide_ref[3 * Q : 4 * Q, sl]
        dvb = wide_wb * nn(b_b, adj_low)
        dv_ref[:, sl] = d_ssm * skip_ref[:, sl] + jnp.concatenate(parts, axis=1) + dvb
        prods = jnp.concatenate(
            [
                (dy_f * yf_ref[:, sl]).astype(bf16),
                (dy_f * yb_ref[:, sl]).astype(bf16),
                (low_f * dvb).astype(bf16),
            ],
            axis=0,
        )
        heads_of += nn(prods, r_ref[sl, :])
        dye_f = (dy_f * wide_ref[:Q, sl]).astype(bf16)
        dye_b = (dy_f * wide_ref[Q : 2 * Q, sl]).astype(bf16)
        vs_f = (low_f * wide_ref[2 * Q : 3 * Q, sl]).astype(bf16)
        vs_b = (low_f * wide_wb).astype(bf16)
        d_cf += nt(dye_f, sf_low)
        d_cb += nt(dye_b, sb_low)
        d_bb += nt(vs_b, adj_low)
        across_b = wide_ref[4 * Q + 8 : 4 * Q + 9, sl]
        scal_ref[:, sl] = jnp.sum(adj * sb_low.astype(f32), axis=0, keepdims=True) * across_b
        adj_ref[:, sl] = adj * across_b + tn(c_b, dye_b)
        state_ref[:, sl] = state_ref[:, sl] * wide_ref[4 * Q : 4 * Q + 1, sl] + tn(b_f, vs_f)

    out_ref[...] = (tok_ref[...].astype(f32) + nt(nout_ref[...], w_ref[...])).astype(bf16)
    dg = jnp.where(same & (col != row), dg, 0.0)
    dg_f = jnp.where(lower, dg, 0.0)
    dg_b = (dg - dg_f).astype(bf16)
    dg_f = dg_f.astype(bf16)
    dbc_ref[...] = jnp.concatenate(
        [tn(dg_f, c_f), d_cf + nn(dg_f, b_f), d_bb + tn(dg_b, c_b), d_cb + nn(dg_b, b_b)], axis=1
    )
    q_cols = jnp.transpose(q_ref[...])[:, : 2 * heads]
    dots_f, dots_b, dots_v = heads_of[:Q, :heads], heads_of[Q : 2 * Q, :heads], heads_of[2 * Q :, :heads]
    through = nn(split_rows(jnp.broadcast_to(scal_ref[...], (8, inner))), r_ref[...])
    through = (through[0:1] + through[8:9])[:, :heads]
    diff = p_ref[:, : 2 * heads] - q_cols
    d_rate_f = nn_exact((col >= row).astype(bf16), diff[:, :heads] + dots_f)
    d_rate_b = (
        nn_exact((col <= row).astype(bf16), diff[:, heads:] + dots_b)
        + nn_exact((col > row).astype(bf16), dots_v)
        + through
    )
    drate_ref[...] = jnp.concatenate([d_rate_f, d_rate_b], axis=1)
    dq_ref[...] = jnp.concatenate([q_cols[:, :heads], q_cols[:, heads:] + dots_v], axis=1)


def middle(tokens, act, gate, dt, cum, aux, segrow, cot, sb, w_out_t, rate_row, skip_row, og_row, x2, r, sizes):
    inner, channels, heads, state = sizes
    t, d = tokens.shape
    n = t // Q
    fwd = lambda i: (i, 0)
    fixed = lambda i: (0, 0)
    cube = lambda i: (i, 0, 0)
    blk = lambda width: pl.BlockSpec((Q, width), fwd)
    whole = lambda a: pl.BlockSpec(a.shape, fixed)
    out = lambda width, dtype: jax.ShapeDtypeStruct((t, width), dtype)
    line = jax.ShapeDtypeStruct((1, inner), f32)
    return pl.pallas_call(
        functools.partial(middle_kernel, sizes),
        grid=(n,),
        in_specs=[
            blk(d), blk(channels), blk(inner), blk(2 * heads), blk(2 * heads), blk(aux.shape[1]),
            pl.BlockSpec((1, 1, Q), cube), blk(d), pl.BlockSpec((1, state, inner), cube),
            whole(w_out_t), whole(rate_row), whole(skip_row), whole(og_row), whole(x2), whole(r),
        ],
        out_specs=[
            blk(d), blk(inner), blk(inner), blk(inner), blk(inner), blk(4 * state),
            blk(2 * heads), blk(2 * heads), pl.BlockSpec((1, state, inner), cube),
            pl.BlockSpec((1, inner), fixed), pl.BlockSpec((1, inner), fixed),
        ],
        out_shape=[
            out(d, bf16), out(inner, bf16), out(inner, bf16), out(inner, bf16), out(inner, f32),
            out(4 * state, f32), out(2 * heads, f32), out(2 * heads, f32),
            jax.ShapeDtypeStruct((n, state, inner), bf16), line, line,
        ],
        scratch_shapes=[
            pltpu.VMEM((heads, Q, Q), f32),
            pltpu.VMEM((heads * Q, Q), bf16),
            pltpu.VMEM((state, inner), f32),
            pltpu.VMEM((state, inner), f32),
            pltpu.VMEM((Q, inner), f32),
            pltpu.VMEM((Q, inner), f32),
            pltpu.VMEM((Q, inner), f32),
            pltpu.VMEM((Q, inner), f32),
            pltpu.VMEM((Q, inner), f32),
            pltpu.VMEM((4 * Q + 16, inner), f32),
            pltpu.VMEM((Q, Q), f32),
            pltpu.VMEM((Q, Q), f32),
            pltpu.VMEM((1, inner), f32),
        ],
        compiler_params=pltpu.CompilerParams(
            dimension_semantics=("arbitrary",), vmem_limit_bytes=60 * 1024 * 1024
        ),
        cost_estimate=pl.CostEstimate(flops=30_000_000_000, bytes_accessed=60_000_000, transcendentals=0),
    )(tokens, act, gate, dt, cum, aux, segrow, cot, sb, w_out_t, rate_row, skip_row, og_row, x2, r)


def back_kernel(
    sizes,
    tok_ref, cot_ref, gain_ref, w_ref, cw_ref, dtb_ref, rate_ref, aux_ref, x2_ref, r_ref,
    low_ref, dsil_ref, conv_ref, dt_ref, cum_ref, dtraw_ref,
    dgate_ref, dy_ref, dv_ref, dbc_ref, drate_ref, dq_ref, sf_ref, dog_ref, dsk_ref,
    dproj_ref, dtok_ref, small_ref,
    adj_ref, dpre_ref, scal_ref,
):
    inner, channels, heads, state = sizes
    quad = 256
    step = pl.program_id(0)

    @pl.when(step == 0)
    def _():
        adj_ref[...] = jnp.zeros_like(adj_ref)
        dpre_ref[...] = jnp.zeros_like(dpre_ref)
        small_ref[...] = jnp.zeros_like(small_ref)
        small_ref[5:6, :inner] = dog_ref[...]
        skips = nn(split_rows(jnp.broadcast_to(dsk_ref[...], (8, inner))), r_ref[...])
        small_ref[6:7, SKIP_AT : SKIP_AT + Q] = skips[0:1] + skips[8:9]

    d = tok_ref.shape[1]

    dpre_ref[Q:, :] = dpre_ref[0:8, :]
    aux = aux_ref[...]
    dt = dt_ref[...]
    cum = cum_ref[...]
    cf, dtf = cum[:, :heads], dt[:, :heads]
    total_f = cf[Q - 1 :, :]
    scales = split2(
        jnp.concatenate(
            [
                jnp.exp(cf) * aux[:, 6:7],
                dtf * jnp.exp(total_f - cf) * aux[:, 4:5],
                jnp.broadcast_to(jnp.exp(total_f) * aux[Q - 1 :, 6:7], (8, heads)),
            ],
            axis=0,
        )
    )
    b_f = low_ref[:, inner : inner + state]
    c_f = low_ref[:, inner + state : inner + 2 * state]
    dots = jnp.zeros((Q, Q), f32)
    d_bf = jnp.zeros((Q, state), f32)
    for at in range(0, inner, quad):
        sl = slice(at, at + quad)
        wide = nn(scales, x2_ref[:, sl])
        low_f = low_ref[:, sl].astype(f32)
        adj = adj_ref[:, sl]
        adj_low = adj.astype(bf16)
        wide_wf = wide[Q : 2 * Q]
        dvf = wide_wf * nn(b_f, adj_low)
        dots += nn((low_f * dvf).astype(bf16), r_ref[sl, :])
        d_bf += nt((low_f * wide_wf).astype(bf16), adj_low)
        across = wide[2 * Q : 2 * Q + 1]
        scal_ref[:, sl] = jnp.sum(adj * sf_ref[0, :, sl].astype(f32), axis=0, keepdims=True) * across
        dye = (dy_ref[:, sl].astype(f32) * wide[:Q]).astype(bf16)
        adj_ref[:, sl] = adj * across + tn(c_f, dye)
        dpre_ref[:Q, sl] = (dv_ref[:, sl] + dvf) * dsil_ref[:, sl]
    d_bc = dbc_ref[...] + jnp.concatenate([d_bf, jnp.zeros((Q, 3 * state), f32)], axis=1)
    dpre_ref[:Q, inner:] = d_bc * dsil_ref[:, inner:]

    n1, n2, n3 = aux[:, 8:9], aux[:, 9:10], aux[:, 10:11]
    for at in range(0, channels, quad):
        sl = slice(at, at + quad)
        conv = conv_ref[:, sl]
        z = dpre_ref[:Q, sl]
        small_ref[4:5, sl] += jnp.sum(z, axis=0, keepdims=True)
        small_ref[0:1, sl] += jnp.sum(z * conv, axis=0, keepdims=True)
        total = cw_ref[0:1, sl] * z
        for k, mask in ((1, n1), (2, n2), (3, n3)):
            z = dpre_ref[k : Q + k, sl] * mask
            small_ref[k : k + 1, sl] += jnp.sum(z * conv, axis=0, keepdims=True)
            total += cw_ref[k : k + 1, sl] * z
        dproj_ref[:, inner + at : inner + at + quad] = total.astype(bf16)
    dproj_ref[:, :inner] = dgate_ref[...]

    row, col = iotas((Q, Q))
    through = nn(split_rows(jnp.broadcast_to(scal_ref[...], (8, inner))), r_ref[...])
    through = (through[0:1] + through[8:9])[:, :heads]
    dots = dots[:, :heads]
    extra = nn_exact((col < row).astype(bf16), dots) + through
    none = jnp.zeros((Q, heads), f32)
    d_rate = drate_ref[...] + jnp.concatenate([extra, none], axis=1)
    d_dt = dq_ref[...] + jnp.concatenate([dots, none], axis=1)
    d_dt = jnp.where(dt > 0.0, d_dt / jnp.maximum(dt, 1e-37), 0.0)
    a = rate_ref[...]
    v = dtraw_ref[...] + dtb_ref[...]
    d_v = (d_dt - d_rate * a) / (1.0 + jnp.exp(-v))
    small_ref[6:7, BIAS_AT : BIAS_AT + 2 * heads] += jnp.sum(d_v, axis=0, keepdims=True)
    small_ref[6:7, LOG_AT : LOG_AT + 2 * heads] += jnp.sum(d_rate * (-dt * a), axis=0, keepdims=True)
    dproj_ref[:, inner + channels :] = d_v.astype(bf16)

    d_normed = (
        nt(dproj_ref[:, :inner], w_ref[:, :inner])
        + nt(dproj_ref[:, inner : inner + channels], w_ref[:, inner : inner + channels])
        + nt(dproj_ref[:, inner + channels :], w_ref[:, inner + channels : inner + channels + 2 * heads])
    )
    x = tok_ref[...].astype(f32)
    inv = lax.rsqrt(jnp.mean(x * x, axis=1, keepdims=True) + eps)
    unit = x * inv
    small_ref[6:7, :d] += jnp.sum(d_normed * unit, axis=0, keepdims=True)
    a = d_normed * gain_ref[...]
    dtok_ref[...] = cot_ref[...].astype(f32) + inv * (a - unit * jnp.mean(a * unit, axis=1, keepdims=True))


def back(
    tokens, cot, gain_row, w_in, conv_w, dt_bias, rate_row, aux, x2, r, low, dsil, conv, dt, cum, dtraw,
    dgate, dy, dv, dbc, drate, dq, sf, dog, dsk, sizes,
):
    inner, channels, heads, state = sizes
    t, d = tokens.shape
    n = t // Q
    proj = inner + channels + 2 * heads
    rev = lambda i: (n - 1 - i, 0)
    fixed = lambda i: (0, 0)
    blk = lambda a: pl.BlockSpec((Q, a.shape[1]), rev)
    whole = lambda a: pl.BlockSpec(a.shape, fixed)
    return pl.pallas_call(
        functools.partial(back_kernel, sizes),
        grid=(n,),
        in_specs=[
            blk(tokens), blk(cot), whole(gain_row), whole(w_in), whole(conv_w), whole(dt_bias), whole(rate_row),
            blk(aux), whole(x2), whole(r), blk(low), blk(dsil), blk(conv), blk(dt), blk(cum), blk(dtraw),
            blk(dgate), blk(dy), blk(dv), blk(dbc), blk(drate), blk(dq),
            pl.BlockSpec((1, state, inner), lambda i: (n - 1 - i, 0, 0)), whole(dog), whole(dsk),
        ],
        out_specs=[pl.BlockSpec((Q, proj), rev), pl.BlockSpec((Q, d), rev), pl.BlockSpec((8, channels), fixed)],
        out_shape=[
            jax.ShapeDtypeStruct((t, proj), bf16),
            jax.ShapeDtypeStruct((t, d), f32),
            jax.ShapeDtypeStruct((8, channels), f32),
        ],
        scratch_shapes=[
            pltpu.VMEM((state, inner), f32),
            pltpu.VMEM((Q + 8, channels), f32),
            pltpu.VMEM((1, inner), f32),
        ],
        compiler_params=pltpu.CompilerParams(
            dimension_semantics=("arbitrary",), vmem_limit_bytes=60 * 1024 * 1024
        ),
        cost_estimate=pl.CostEstimate(flops=20_000_000_000, bytes_accessed=60_000_000, transcendentals=0),
    )(
        tokens, cot, gain_row, w_in, conv_w, dt_bias, rate_row, aux, x2, r, low, dsil, conv, dt, cum, dtraw,
        dgate, dy, dv, dbc, drate, dq, sf, dog, dsk,
    )


def features(segment_ids):
    t = segment_ids.shape[0]
    n = t // Q
    seg = segment_ids.astype(f32)
    earlier = [jnp.concatenate([jnp.full((k,), -1.0, f32), seg[: t - k]]) == seg for k in (1, 2, 3)]
    later = [jnp.concatenate([seg[k:], jnp.full((k,), -1.0, f32)]) == seg for k in (1, 2, 3)]
    chunks = seg.reshape(n, Q)
    ends, starts = chunks[:, -1:], chunks[:, :1]
    none = jnp.full((1, 1), -1.0, f32)
    like = lambda edge: (chunks == edge).reshape(t)
    columns = earlier + [
        seg,
        like(ends),
        like(starts),
        like(jnp.concatenate([none, ends[:-1]])),
        like(jnp.concatenate([starts[1:], none])),
    ] + later
    aux = jnp.stack([c.astype(f32) for c in columns], axis=1)
    return aux, chunks.reshape(n, 1, Q)


def local(tokens, segment_ids, w_in, w_out_t, gain, conv_w, conv_b, dt_bias, a_log, d_skip, out_gain, cotangent):
    heads = d_skip.shape[0]
    inner = out_gain.shape[0]
    channels = conv_w.shape[1]
    state = (channels - inner) // 4
    width = inner // heads
    sizes = (inner, channels, heads, state)
    aux, segrow = features(segment_ids)
    spread = np.arange(inner)[None, :] // width == np.arange(heads)[:, None]
    x2 = jnp.asarray(np.concatenate([spread, spread], axis=0), bf16)
    r = jnp.asarray(np.pad(spread.T, ((0, 0), (0, Q - heads))), bf16)
    gain_row = gain.astype(f32)[None, :]
    rate_row = jnp.exp(a_log)[None, :]
    dtb_row = dt_bias[None, :]
    skip_row = jnp.repeat(d_skip, width)[None, :]
    normed, gate, conv, act, low, dsil, dt, cum, dtraw, sb = front(
        tokens, gain_row, w_in, conv_w, conv_b[None, :], dtb_row, rate_row, aux, x2, sizes
    )
    output, nout, dgate, dy, dv, dbc, drate, dq, sf, d_og, d_sk = middle(
        tokens, act, gate, dt, cum, aux, segrow, cotangent, sb, w_out_t, rate_row, skip_row,
        out_gain[None, :], x2, r, sizes,
    )
    d_w_out_t = tn(cotangent, nout).astype(bf16)
    dproj, d_tokens, small = back(
        tokens, cotangent, gain_row, w_in, conv_w, dtb_row, rate_row, aux, x2, r, low, dsil, conv, dt, cum, dtraw,
        dgate, dy, dv, dbc, drate, dq, sf, d_og, d_sk, sizes,
    )
    d_w_in = tn(normed, dproj).astype(bf16)
    return output, d_tokens, d_w_in, d_w_out_t, small


def unpack(small, taps, inner, heads, d):
    return small[6, :d], (
        small[:taps],
        small[taps],
        small[6, BIAS_AT : BIAS_AT + 2 * heads],
        small[6, LOG_AT : LOG_AT + 2 * heads],
        small[6, SKIP_AT : SKIP_AT + heads],
        small[5, :inner],
    )


MESH = pl.DeviceIdType.MESH


def place():
    f = lax.axis_index("fsdp")
    return f // 4, (f // 2) % 2, f % 2, lax.axis_index("rep")


def flip(at, dy, dx, dc, k):
    y, x, c, z = at
    z_at = {0: z, 1: z + 1 - 2 * (z % 2), 2: (z + 2) % 4, 3: 3 - z}[k]
    return (1 - y if dy else y, 1 - x if dx else x, 1 - c if dc else c, z_at)


def device(at):
    y, x, c, z = at
    return ((y * 2 + x) * 2 + c, z)


def slot(at):
    y, x, c, z = at
    return ((y * 2 + x) * 2 + c) * 4 + z


def greet(me):
    barrier = pltpu.get_barrier_semaphore()
    others = [(0, 0, 1, 0), (0, 1, 0, 0), (1, 0, 0, 0), (0, 0, 0, 1), (0, 0, 0, 2), (0, 0, 0, 3)]
    for other in others:
        pl.semaphore_signal(barrier, inc=1, device_id=device(flip(me, *other)), device_id_type=MESH)
    pl.semaphore_wait(barrier, len(others))


def halves(width):
    cut = (width // 2 + 127) // 128 * 128
    return slice(0, cut), slice(cut, width)


class Gatherer:
    count = 39

    def __init__(self, me, own, full, send, recv):
        self.me, self.own, self.full, self.send, self.recv = me, own, full, send, recv
        self.left, self.right = halves(full.shape[2])
        self.copies = {}

    def copy(self, name, block, to, cols=None):
        i = len(self.copies)
        at = slot(flip(self.me, *block))
        dst = self.full.at[at] if cols is None else self.full.at[at, :, cols]
        src = dst
        if block == (0, 0, 0, 0):
            src = self.own if cols is None else self.own.at[:, cols]
        made = pltpu.make_async_remote_copy(
            src_ref=src, dst_ref=dst, send_sem=self.send.at[i], recv_sem=self.recv.at[i],
            device_id=device(flip(self.me, *to)), device_id_type=MESH,
        )
        made.start()
        self.copies[name] = made

    def arrived(self, name):
        self.copies[name].wait_recv()

    def start(self):
        for k in (1, 2, 3):
            self.copy(("z", k), (0, 0, 0, 0), (0, 0, 0, k))
        self.spread(0)

    def spread(self, k):
        self.copy(("x", k), (0, 0, 0, k), (0, 1, 0, 0))
        self.copy(("y", k), (0, 0, 0, k), (1, 0, 0, 0))
        self.copy(("c", k), (0, 0, 0, k), (0, 0, 1, 0))

    def column(self):
        for k in (1, 2, 3):
            self.arrived(("z", k))
            self.spread(k)

    def corner(self):
        for k in range(4):
            self.arrived(("x", k))
            self.copy(("left", k), (0, 1, 0, k), (1, 0, 0, 0), self.left)
            self.copy(("cx", k), (0, 1, 0, k), (0, 0, 1, 0))
            self.arrived(("y", k))
            self.copy(("right", k), (1, 0, 0, k), (0, 1, 0, 0), self.right)
            self.copy(("cy", k), (1, 0, 0, k), (0, 0, 1, 0))

    def last(self):
        for k in range(4):
            self.arrived(("left", k))
            self.copy(("cl", k), (1, 1, 0, k), (0, 0, 1, 0), self.left)
            self.arrived(("right", k))
            self.copy(("cr", k), (1, 1, 0, k), (0, 0, 1, 0), self.right)

    def finish(self):
        for name, made in self.copies.items():
            if name[0][0] == "c":
                made.wait_recv()
        for made in self.copies.values():
            made.wait_send()


def gather_kernel(*refs):
    n = (len(refs) - 3) // 2
    owns, fulls = refs[:n], refs[n : 2 * n]
    send, recv, here = refs[2 * n :]
    me = place()
    greet(me)
    work = [Gatherer(me, owns[i], fulls[i], send.at[i], recv.at[i]) for i in range(n)]
    for w in work:
        w.start()
    locals_ = [pltpu.make_async_copy(owns[i], fulls[i].at[slot(me)], here.at[i]) for i in range(n)]
    for made in locals_:
        made.start()
    for phase in ("column", "corner", "last", "finish"):
        for w in work:
            getattr(w, phase)()
    for made in locals_:
        made.wait()


def gather(*shards):
    n = len(shards)
    return pl.pallas_call(
        gather_kernel,
        in_specs=[pl.BlockSpec(memory_space=pl.ANY)] * n,
        out_specs=[pl.BlockSpec(memory_space=pl.ANY)] * n,
        out_shape=[jax.ShapeDtypeStruct((32,) + s.shape, s.dtype) for s in shards],
        scratch_shapes=[
            pltpu.SemaphoreType.DMA((n, Gatherer.count)),
            pltpu.SemaphoreType.DMA((n, Gatherer.count)),
            pltpu.SemaphoreType.DMA((n,)),
        ],
        compiler_params=pltpu.CompilerParams(collective_id=0, has_side_effects=True),
    )(*shards)


BLOCKS = ((1, 1), (0, 1), (1, 0), (0, 0))


class Scatterer:
    count = 43

    def __init__(self, me, part, out, mine, from_core, from_pair, from_far, from_line, send, recv, here):
        self.me, self.part, self.out = me, part, out
        self.mine, self.from_core, self.from_pair, self.from_far, self.from_line = (
            mine, from_core, from_pair, from_far, from_line,
        )
        self.send, self.recv, self.here = send, recv, here
        self.left, self.right = halves(part.shape[2])
        self.copies = {}

    def copy(self, name, src, dst, to):
        i = len(self.copies)
        made = pltpu.make_async_remote_copy(
            src_ref=src, dst_ref=dst, send_sem=self.send.at[i], recv_sem=self.recv.at[i],
            device_id=device(flip(self.me, *to)), device_id_type=MESH,
        )
        made.start()
        self.copies[name] = made

    def start(self):
        self.locals = {}
        for b, (dy, dx) in enumerate(BLOCKS):
            for k in range(4):
                other = slot(flip(self.me, dy, dx, 1, k))
                self.copy(("core", b, k), self.part.at[other], self.from_core.at[b, k], (0, 0, 1, 0))
                own = slot(flip(self.me, dy, dx, 0, k))
                made = pltpu.make_async_copy(self.part.at[own], self.mine.at[b, k], self.here.at[b * 4 + k])
                made.start()
                self.locals[b, k] = made

    def add(self, b, k, cols, others):
        total = self.mine[b, k, :, cols].astype(f32)
        for ref in others:
            total += ref.astype(f32)
        return total

    def pair(self):
        for b, (dy, dx) in enumerate(BLOCKS):
            for k in range(4):
                self.locals[b, k].wait()
                self.copies["core", b, k].wait_recv()
                self.mine[b, k] = (self.mine[b, k].astype(f32) + self.from_core[b, k].astype(f32)).astype(bf16)
                if dx:
                    self.copy(
                        ("x", b, k), self.mine.at[b, k, :, self.left], self.from_pair.at[b, k, :, self.left],
                        (0, 1, 0, 0),
                    )
                if dy:
                    self.copy(
                        ("y", b, k), self.mine.at[b, k, :, self.right], self.from_pair.at[b // 2, k, :, self.right],
                        (1, 0, 0, 0),
                    )

    def far(self):
        for k in range(4):
            self.copies["x", 0, k].wait_recv()
            self.mine[2, k, :, self.left] = self.add(
                2, k, self.left, [self.from_pair[0, k, :, self.left]]
            ).astype(bf16)
            self.copy(("fy", k), self.mine.at[2, k, :, self.left], self.from_far.at[k, :, self.left], (1, 0, 0, 0))
            self.copies["y", 0, k].wait_recv()
            self.mine[1, k, :, self.right] = self.add(
                1, k, self.right, [self.from_pair[0, k, :, self.right]]
            ).astype(bf16)
            self.copy(("fx", k), self.mine.at[1, k, :, self.right], self.from_far.at[k, :, self.right], (0, 1, 0, 0))

    def line(self):
        for k in (1, 2, 3, 0):
            for name in (("x", 1, k), ("y", 2, k), ("fy", k), ("fx", k)):
                self.copies[name].wait_recv()
            if k:
                self.mine[3, k] = self.add(3, k, slice(None), [self.from_pair[1, k], self.from_far[k]]).astype(bf16)
                self.copy(("z", k), self.mine.at[3, k], self.from_line.at[k - 1], (0, 0, 0, k))

    def finish(self):
        for k in (1, 2, 3):
            self.copies["z", k].wait_recv()
        self.out[...] = self.add(
            3, 0, slice(None),
            [self.from_pair[1, 0], self.from_far[0], self.from_line[0], self.from_line[1], self.from_line[2]],
        )
        for made in self.copies.values():
            made.wait_send()


def scatter_scratch(rows, width):
    vmem = lambda *lead: pltpu.VMEM(lead + (rows, width), bf16)
    return [
        vmem(4, 4), vmem(4, 4), vmem(2, 4), vmem(4), vmem(3),
        pltpu.SemaphoreType.DMA((Scatterer.count,)), pltpu.SemaphoreType.DMA((Scatterer.count,)),
        pltpu.SemaphoreType.DMA((16,)),
    ]


class Summer:
    def __init__(self, me, own, out, held, send, recv):
        self.me, self.own, self.out, self.held, self.send, self.recv = me, own, out, held, send, recv
        self.copies = []

    def copy(self, src, dst, to):
        i = len(self.copies)
        made = pltpu.make_async_remote_copy(
            src_ref=src, dst_ref=dst, send_sem=self.send.at[i], recv_sem=self.recv.at[i],
            device_id=device(flip(self.me, *to)), device_id_type=MESH,
        )
        made.start()
        self.copies.append(made)

    def start(self):
        self.copy(self.own, self.held.at[0], (0, 0, 1, 0))

    def second(self):
        self.copies[0].wait_recv()
        self.out[...] = self.own[...] + self.held[0]
        self.held[6] = self.out[...]
        self.copy(self.held.at[6], self.held.at[1], (0, 1, 0, 0))

    def third(self):
        self.copies[1].wait_recv()
        self.held[7] = self.held[6] + self.held[1]
        self.copy(self.held.at[7], self.held.at[2], (1, 0, 0, 0))

    def fourth(self):
        self.copies[2].wait_recv()
        self.held[8] = self.held[7] + self.held[2]
        for k in (1, 2, 3):
            self.copy(self.held.at[8], self.held.at[2 + k], (0, 0, 0, k))

    def finish(self):
        for made in self.copies[3:]:
            made.wait_recv()
        self.out[...] = (self.held[8] + self.held[3]) + (self.held[4] + self.held[5])
        for made in self.copies:
            made.wait_send()


def scatter_kernel(n, *refs):
    parts, small = refs[:n], refs[n]
    outs, small_out = refs[n + 1 : 2 * n + 1], refs[2 * n + 1]
    scratch = refs[2 * n + 2 :]
    me = place()
    greet(me)
    work = [Scatterer(me, parts[i], outs[i], *scratch[8 * i : 8 * i + 8]) for i in range(n)]
    tiny = Summer(me, small, small_out, *scratch[8 * n :])
    tiny.start()
    for w in work:
        w.start()
    tiny.second()
    for w in work:
        w.pair()
    tiny.third()
    for w in work:
        w.far()
    tiny.fourth()
    for w in work:
        w.line()
    for w in work:
        w.finish()
    tiny.finish()


def scatter(parts, small):
    n = len(parts)
    scratch = []
    for p in parts:
        scratch += scatter_scratch(p.shape[1], p.shape[2])
    scratch += [
        pltpu.VMEM((9,) + small.shape, f32), pltpu.SemaphoreType.DMA((6,)), pltpu.SemaphoreType.DMA((6,)),
    ]
    vmem = pl.BlockSpec(memory_space=pltpu.VMEM)
    return pl.pallas_call(
        functools.partial(scatter_kernel, n),
        in_specs=[pl.BlockSpec(memory_space=pl.ANY)] * n + [vmem],
        out_specs=[vmem] * (n + 1),
        out_shape=[jax.ShapeDtypeStruct(p.shape[1:], f32) for p in parts]
        + [jax.ShapeDtypeStruct(small.shape, f32)],
        scratch_shapes=scratch,
        compiler_params=pltpu.CompilerParams(
            collective_id=1, has_side_effects=True, vmem_limit_bytes=60 * 1024 * 1024
        ),
    )(*parts, small)


def body(here, tokens, segment_ids, w_in, w_out, norm_gain, conv_w, conv_b, dt_bias, a_log, d_skip, out_gain, cotangent):
    rows, proj = w_in.shape
    d, inner, heads = tokens.shape[1], out_gain.shape[0], d_skip.shape[0]
    parts = d // rows
    w_ext = jnp.concatenate([w_in, norm_gain[:, None]], axis=1)
    if here:
        full_in, full_out_t = gather(w_ext, w_out.T)
    else:
        full_in, full_out_t = lax.all_gather(w_ext, AXES), lax.all_gather(w_out.T, AXES)
    full_in = full_in.reshape(d, proj + 1)
    output, d_tokens, g_in, g_out_t, small = local(
        tokens, segment_ids, full_in, full_out_t.reshape(d, inner), full_in[:, proj], conv_w, conv_b, dt_bias, a_log,
        d_skip, out_gain, cotangent,
    )
    g_in, g_out_t = g_in.reshape(parts, rows, proj), g_out_t.reshape(parts, rows, inner)
    if here:
        d_w_in, d_w_out, small = scatter([g_in, g_out_t], small)
    else:
        d_w_in = lax.psum_scatter(g_in.astype(f32), AXES, scatter_dimension=0)
        d_w_out = lax.psum_scatter(g_out_t.astype(f32), AXES, scatter_dimension=0)
        small = lax.psum(small, AXES)
    d_gain, small = unpack(small, conv_w.shape[0], inner, heads, d)
    d_gain = lax.dynamic_slice_in_dim(d_gain, lax.axis_index(AXES) * rows, rows)
    return (output, d_tokens, d_w_in, d_w_out.T, d_gain) + small


def solution(mesh):
    rows, cols, line, none = P(AXES, None), P(None, AXES), P(AXES), P()
    here = dict(mesh.shape) == {"fsdp": 8, "rep": 4}
    return jax.shard_map(
        functools.partial(body, here),
        mesh=mesh,
        in_specs=(rows, line, rows, cols, line, none, none, none, none, none, none, rows),
        out_specs=(rows, rows, rows, cols, line, none, none, none, none, none, none),
        check_vma=False,
    )
```

```python
import functools

import jax
import jax.numpy as jnp
import numpy as np
from jax import lax
from jax.experimental import pallas as pl
from jax.experimental.pallas import tpu as pltpu
from jax.sharding import PartitionSpec as P

eps = 1e-05
Q = 128
HALO = 16
f32 = jnp.float32
bf16 = jnp.bfloat16
AXES = ("fsdp", "rep")
BIAS_AT, LOG_AT, SKIP_AT = 768, 896, 1024


def nn(a, b):
    return lax.dot_general(a, b, (((1,), (0,)), ((), ())), preferred_element_type=f32)


def nt(a, b):
    return lax.dot_general(a, b, (((1,), (1,)), ((), ())), preferred_element_type=f32)


def tn(a, b):
    return lax.dot_general(a, b, (((0,), (0,)), ((), ())), preferred_element_type=f32)


def split2(x):
    hi = x.astype(bf16)
    lo = (x - hi.astype(f32)).astype(bf16)
    return jnp.concatenate([hi, lo], axis=1)


def split_rows(x):
    hi = x.astype(bf16)
    return jnp.concatenate([hi, (x - hi.astype(f32)).astype(bf16)], axis=0)


def nn_exact(ones_mask, x):
    hi = x.astype(bf16)
    r = x - hi.astype(f32)
    mid = r.astype(bf16)
    lo = (r - mid.astype(f32)).astype(bf16)
    return nn(ones_mask, hi) + (nn(ones_mask, mid) + nn(ones_mask, lo))


def iotas(shape):
    return (
        lax.broadcasted_iota(jnp.int32, shape, 0),
        lax.broadcasted_iota(jnp.int32, shape, 1),
    )


MESH = pl.DeviceIdType.MESH
LINE = 4
STEPS = (0, -1, 1, -2, 2, -3, 3)
LAG = 2


def place():
    f = lax.axis_index("fsdp")
    return f // 4, (f // 2) % 2, f % 2, lax.axis_index("rep")


def flip(at, dy, dx, dc, dz):
    y, x, c, z = at
    return (1 - y if dy else y, 1 - x if dx else x, 1 - c if dc else c, z + dz)


def device(at):
    y, x, c, z = at
    return ((y * 2 + x) * 2 + c, z)


def slot(at):
    y, x, c, z = at
    return ((y * 2 + x) * 2 + c) * LINE + z


def on_line(me, dz):
    z = me[3]
    return z >= -dz if dz < 0 else z < LINE - dz


def when(condition, act):
    if condition is True:
        act()
    else:
        pl.when(condition)(act)


def greet(me):
    barrier = pltpu.get_barrier_semaphore()
    for other in ((0, 0, 1, 0), (0, 1, 0, 0), (1, 0, 0, 0)):
        pl.semaphore_signal(barrier, inc=1, device_id=device(flip(me, *other)), device_id_type=MESH)
    for dz in (-1, 1):

        @pl.when(on_line(me, dz))
        def _():
            pl.semaphore_signal(barrier, inc=1, device_id=device(flip(me, 0, 0, 0, dz)), device_id_type=MESH)

    inside = jnp.where((me[3] > 0) & (me[3] < LINE - 1), 1, 0)
    pl.semaphore_wait(barrier, 4 + inside)


def halves(width):
    cut = (width // 2 + 127) // 128 * 128
    return slice(0, cut), slice(cut, width)


class Gatherer:
    kinds = ("z", "x", "y", "c", "left", "right", "cx", "cy", "cl", "cr")
    count = len(kinds) * len(STEPS)

    def __init__(self, me, own, full, send, recv):
        self.me, self.own, self.full, self.send, self.recv = me, own, full, send, recv
        self.left, self.right = halves(full.shape[2])

    def made(self, kind, dz, block, to, cols=None):
        i = self.kinds.index(kind) * len(STEPS) + STEPS.index(dz)
        at = slot(flip(self.me, *block))
        dst = self.full.at[at] if cols is None else self.full.at[at, :, cols]
        src = dst
        if block == (0, 0, 0, 0):
            src = self.own if cols is None else self.own.at[:, cols]
        return pltpu.make_async_remote_copy(
            src_ref=src, dst_ref=dst, send_sem=self.send.at[i], recv_sem=self.recv.at[i],
            device_id=device(flip(self.me, *to)), device_id_type=MESH,
        )

    def copy(self, kind, dz):
        return {
            "x": lambda: self.made("x", dz, (0, 0, 0, dz), (0, 1, 0, 0)),
            "y": lambda: self.made("y", dz, (0, 0, 0, dz), (1, 0, 0, 0)),
            "c": lambda: self.made("c", dz, (0, 0, 0, dz), (0, 0, 1, 0)),
            "left": lambda: self.made("left", dz, (0, 1, 0, dz), (1, 0, 0, 0), self.left),
            "right": lambda: self.made("right", dz, (1, 0, 0, dz), (0, 1, 0, 0), self.right),
            "cx": lambda: self.made("cx", dz, (0, 1, 0, dz), (0, 0, 1, 0)),
            "cy": lambda: self.made("cy", dz, (1, 0, 0, dz), (0, 0, 1, 0)),
            "cl": lambda: self.made("cl", dz, (1, 1, 0, dz), (0, 0, 1, 0), self.left),
            "cr": lambda: self.made("cr", dz, (1, 1, 0, dz), (0, 0, 1, 0), self.right),
        }[kind]()

    def along(self, dz, way):
        i = self.kinds.index("z") * len(STEPS) + STEPS.index(dz - way)
        at = slot(flip(self.me, 0, 0, 0, dz))
        return pltpu.make_async_remote_copy(
            src_ref=self.full.at[at] if dz else self.own, dst_ref=self.full.at[at],
            send_sem=self.send.at[i], recv_sem=self.recv.at[i],
            device_id=device(flip(self.me, 0, 0, 0, way)), device_id_type=MESH,
        )

    def sent_along(self):
        for dz in STEPS:
            for way in (-1, 1):
                if dz * way <= 0 and abs(dz - way) < LINE:
                    yield dz, way, on_line(self.me, way) & (True if dz == 0 else on_line(self.me, dz))

    def each(self, act):
        for dz in STEPS:
            when(True if dz == 0 else on_line(self.me, dz), functools.partial(act, dz))

    def start(self):
        for dz, way, ok in self.sent_along():
            if dz == 0:
                when(ok, lambda dz=dz, way=way: self.along(dz, way).start())
        self.spread(0)

    def spread(self, dz):
        for kind in ("x", "y", "c"):
            self.copy(kind, dz).start()

    def column(self, dz):
        if dz == 0:
            return
        way = -1 if dz > 0 else 1
        self.along_arrived(dz)
        if abs(dz) < LINE - 1:
            when(on_line(self.me, way), lambda: self.along(dz, way).start())
        self.spread(dz)

    def along_arrived(self, dz):
        i = self.kinds.index("z") * len(STEPS) + STEPS.index(dz)
        ref = self.full.at[slot(flip(self.me, 0, 0, 0, dz))]
        pltpu.make_async_remote_copy(
            src_ref=ref, dst_ref=ref, send_sem=self.send.at[i], recv_sem=self.recv.at[i],
            device_id=device(flip(self.me, 0, 0, 0, 1 if dz > 0 else -1)), device_id_type=MESH,
        ).wait_recv()

    def corner(self, dz):
        self.copy("x", dz).wait_recv()
        self.copy("left", dz).start()
        self.copy("cx", dz).start()
        self.copy("y", dz).wait_recv()
        self.copy("right", dz).start()
        self.copy("cy", dz).start()

    def last(self, dz):
        self.copy("left", dz).wait_recv()
        self.copy("cl", dz).start()
        self.copy("right", dz).wait_recv()
        self.copy("cr", dz).start()

    def beat(self, t):
        for lag, act in ((0, self.column), (LAG, self.corner), (2 * LAG, self.last)):
            if 0 <= t - lag < len(STEPS):
                dz = STEPS[t - lag]
                when(True if dz == 0 else on_line(self.me, dz), functools.partial(act, dz))

    beats = len(STEPS) + 2 * LAG

    def finish(self):
        def act(dz):
            for kind in ("c", "cx", "cy", "cl", "cr"):
                self.copy(kind, dz).wait_recv()
            for kind in self.kinds[1:]:
                self.copy(kind, dz).wait_send()

        self.each(act)
        for dz, way, ok in self.sent_along():
            when(ok, lambda dz=dz, way=way: self.along(dz, way).wait_send())


def gather_kernel(*refs):
    n = (len(refs) - 3) // 2
    owns, fulls = refs[:n], refs[n : 2 * n]
    send, recv, here = refs[2 * n :]
    me = place()
    greet(me)
    work = [Gatherer(me, owns[i], fulls[i], send.at[i], recv.at[i]) for i in range(n)]
    for w in work:
        w.start()
    locals_ = [pltpu.make_async_copy(owns[i], fulls[i].at[slot(me)], here.at[i]) for i in range(n)]
    for made in locals_:
        made.start()
    for t in range(Gatherer.beats):
        for w in work:
            w.beat(t)
    for w in work:
        w.finish()
    for made in locals_:
        made.wait()


def gather(*shards):
    n = len(shards)
    return pl.pallas_call(
        gather_kernel,
        in_specs=[pl.BlockSpec(memory_space=pl.ANY)] * n,
        out_specs=[pl.BlockSpec(memory_space=pl.ANY)] * n,
        out_shape=[jax.ShapeDtypeStruct((32,) + s.shape, s.dtype) for s in shards],
        scratch_shapes=[
            pltpu.SemaphoreType.DMA((n, Gatherer.count)),
            pltpu.SemaphoreType.DMA((n, Gatherer.count)),
            pltpu.SemaphoreType.DMA((n,)),
        ],
        compiler_params=pltpu.CompilerParams(collective_id=0, has_side_effects=True),
    )(*shards)


def partner(at, dy, dx, dc, k):
    return flip(at, dy, dx, dc, 0)[:3] + ({0: at[3], 1: at[3] + 1 - 2 * (at[3] % 2), 2: (at[3] + 2) % 4, 3: 3 - at[3]}[k],)


def greet_all(me):
    barrier = pltpu.get_barrier_semaphore()
    others = [(0, 0, 1, 0), (0, 1, 0, 0), (1, 0, 0, 0), (0, 0, 0, 1), (0, 0, 0, 2), (0, 0, 0, 3)]
    for other in others:
        pl.semaphore_signal(barrier, inc=1, device_id=device(partner(me, *other)), device_id_type=MESH)
    pl.semaphore_wait(barrier, len(others))


BLOCKS = ((1, 1), (0, 1), (1, 0), (0, 0))


class Scatterer:
    count = 43

    def __init__(self, me, part, out, mine, from_core, from_pair, from_far, from_line, send, recv, here):
        self.me, self.part, self.out = me, part, out
        self.mine, self.from_core, self.from_pair, self.from_far, self.from_line = (
            mine, from_core, from_pair, from_far, from_line,
        )
        self.send, self.recv, self.here = send, recv, here
        self.left, self.right = halves(part.shape[2])
        self.copies = {}

    def copy(self, name, src, dst, to):
        i = len(self.copies)
        made = pltpu.make_async_remote_copy(
            src_ref=src, dst_ref=dst, send_sem=self.send.at[i], recv_sem=self.recv.at[i],
            device_id=device(partner(self.me, *to)), device_id_type=MESH,
        )
        made.start()
        self.copies[name] = made

    def start(self):
        self.locals = {}
        for b, (dy, dx) in enumerate(BLOCKS):
            for k in range(4):
                other = slot(partner(self.me, dy, dx, 1, k))
                self.copy(("core", b, k), self.part.at[other], self.from_core.at[b, k], (0, 0, 1, 0))
                own = slot(partner(self.me, dy, dx, 0, k))
                made = pltpu.make_async_copy(self.part.at[own], self.mine.at[b, k], self.here.at[b * 4 + k])
                made.start()
                self.locals[b, k] = made

    def add(self, b, k, cols, others):
        total = self.mine[b, k, :, cols].astype(f32)
        for ref in others:
            total += ref.astype(f32)
        return total

    def pair(self):
        for b, (dy, dx) in enumerate(BLOCKS):
            for k in range(4):
                self.locals[b, k].wait()
                self.copies["core", b, k].wait_recv()
                self.mine[b, k] = (self.mine[b, k].astype(f32) + self.from_core[b, k].astype(f32)).astype(bf16)
                if dx:
                    self.copy(
                        ("x", b, k), self.mine.at[b, k, :, self.left], self.from_pair.at[b, k, :, self.left],
                        (0, 1, 0, 0),
                    )
                if dy:
                    self.copy(
                        ("y", b, k), self.mine.at[b, k, :, self.right], self.from_pair.at[b // 2, k, :, self.right],
                        (1, 0, 0, 0),
                    )

    def far(self):
        for k in range(4):
            self.copies["x", 0, k].wait_recv()
            self.mine[2, k, :, self.left] = self.add(
                2, k, self.left, [self.from_pair[0, k, :, self.left]]
            ).astype(bf16)
            self.copy(("fy", k), self.mine.at[2, k, :, self.left], self.from_far.at[k, :, self.left], (1, 0, 0, 0))
            self.copies["y", 0, k].wait_recv()
            self.mine[1, k, :, self.right] = self.add(
                1, k, self.right, [self.from_pair[0, k, :, self.right]]
            ).astype(bf16)
            self.copy(("fx", k), self.mine.at[1, k, :, self.right], self.from_far.at[k, :, self.right], (0, 1, 0, 0))

    def line(self):
        for k in (1, 2, 3, 0):
            for name in (("x", 1, k), ("y", 2, k), ("fy", k), ("fx", k)):
                self.copies[name].wait_recv()
            if k:
                self.mine[3, k] = self.add(3, k, slice(None), [self.from_pair[1, k], self.from_far[k]]).astype(bf16)
                self.copy(("z", k), self.mine.at[3, k], self.from_line.at[k - 1], (0, 0, 0, k))

    def finish(self):
        for k in (1, 2, 3):
            self.copies["z", k].wait_recv()
        self.out[...] = self.add(
            3, 0, slice(None),
            [self.from_pair[1, 0], self.from_far[0], self.from_line[0], self.from_line[1], self.from_line[2]],
        )
        for made in self.copies.values():
            made.wait_send()


def scatter_scratch(rows, width):
    vmem = lambda *lead: pltpu.VMEM(lead + (rows, width), bf16)
    return [
        vmem(4, 4), vmem(4, 4), vmem(2, 4), vmem(4), vmem(3),
        pltpu.SemaphoreType.DMA((Scatterer.count,)), pltpu.SemaphoreType.DMA((Scatterer.count,)),
        pltpu.SemaphoreType.DMA((16,)),
    ]


class Summer:
    def __init__(self, me, own, out, held, send, recv):
        self.me, self.own, self.out, self.held, self.send, self.recv = me, own, out, held, send, recv
        self.copies = []

    def copy(self, src, dst, to):
        i = len(self.copies)
        made = pltpu.make_async_remote_copy(
            src_ref=src, dst_ref=dst, send_sem=self.send.at[i], recv_sem=self.recv.at[i],
            device_id=device(partner(self.me, *to)), device_id_type=MESH,
        )
        made.start()
        self.copies.append(made)

    def start(self):
        self.copy(self.own, self.held.at[0], (0, 0, 1, 0))

    def second(self):
        self.copies[0].wait_recv()
        self.out[...] = self.own[...] + self.held[0]
        self.held[6] = self.out[...]
        self.copy(self.held.at[6], self.held.at[1], (0, 1, 0, 0))

    def third(self):
        self.copies[1].wait_recv()
        self.held[7] = self.held[6] + self.held[1]
        self.copy(self.held.at[7], self.held.at[2], (1, 0, 0, 0))

    def fourth(self):
        self.copies[2].wait_recv()
        self.held[8] = self.held[7] + self.held[2]
        for k in (1, 2, 3):
            self.copy(self.held.at[8], self.held.at[2 + k], (0, 0, 0, k))

    def finish(self):
        for made in self.copies[3:]:
            made.wait_recv()
        self.out[...] = (self.held[8] + self.held[3]) + (self.held[4] + self.held[5])
        for made in self.copies:
            made.wait_send()


def scatter_kernel(n, *refs):
    parts, small = refs[:n], refs[n]
    outs, small_out = refs[n + 1 : 2 * n + 1], refs[2 * n + 1]
    scratch = refs[2 * n + 2 :]
    me = place()
    greet_all(me)
    work = [Scatterer(me, parts[i], outs[i], *scratch[8 * i : 8 * i + 8]) for i in range(n)]
    tiny = Summer(me, small, small_out, *scratch[8 * n :])
    tiny.start()
    for w in work:
        w.start()
    tiny.second()
    for w in work:
        w.pair()
    tiny.third()
    for w in work:
        w.far()
    tiny.fourth()
    for w in work:
        w.line()
    for w in work:
        w.finish()
    tiny.finish()


def scatter(parts, small):
    n = len(parts)
    scratch = []
    for p in parts:
        scratch += scatter_scratch(p.shape[1], p.shape[2])
    scratch += [
        pltpu.VMEM((9,) + small.shape, f32), pltpu.SemaphoreType.DMA((6,)), pltpu.SemaphoreType.DMA((6,)),
    ]
    vmem = pl.BlockSpec(memory_space=pltpu.VMEM)
    return pl.pallas_call(
        functools.partial(scatter_kernel, n),
        in_specs=[pl.BlockSpec(memory_space=pl.ANY)] * n + [vmem],
        out_specs=[vmem] * (n + 1),
        out_shape=[jax.ShapeDtypeStruct(p.shape[1:], f32) for p in parts]
        + [jax.ShapeDtypeStruct(small.shape, f32)],
        scratch_shapes=scratch,
        compiler_params=pltpu.CompilerParams(
            collective_id=2, has_side_effects=True, vmem_limit_bytes=60 * 1024 * 1024
        ),
    )(*parts, small)


def reaches(here, number):
    return dict(collective_id=number, has_side_effects=True) if here else {}


BEATS = (0, 2, 4, 5, 7, 8, 9, 10, 11)


def front_kernel(
    sizes, here,
    tok_ref, halo_ref, gain_ref, w_ref, cw_ref, cb_ref, dtb_ref, rate_ref, aux_ref, x2_ref, own_ref,
    normed_ref, conv_ref, act_ref, low_ref, dsil_ref, dt_ref, cum_ref, dtraw_ref, sb_ref, full_ref,
    ext_ref, state_ref, send_ref, recv_ref, copy_ref,
):
    inner, channels, heads, state = sizes
    step = pl.program_id(0)
    if here:
        me = place()
        others = Gatherer(me, own_ref, full_ref, send_ref, recv_ref)
        mine = pltpu.make_async_copy(own_ref, full_ref.at[slot(me)], copy_ref)

        @pl.when(step == 0)
        def _():
            greet(me)
            others.start()
            mine.start()

    @pl.when(step == 0)
    def _():
        state_ref[...] = jnp.zeros_like(state_ref)

    gain = gain_ref[...]

    def norm(x):
        x = x.astype(f32)
        inv = lax.rsqrt(jnp.mean(x * x, axis=1, keepdims=True) + eps)
        return (x * inv * gain).astype(bf16)

    normed = norm(tok_ref[...])
    normed_ref[...] = normed
    both = jnp.concatenate([norm(halo_ref[...]), normed], axis=0)
    dt_raw = nn(normed, w_ref[:, channels : channels + 2 * heads])
    dtraw_ref[...] = dt_raw
    aux = aux_ref[...]
    m1, m2, m3 = aux[:, 0:1], aux[:, 1:2], aux[:, 2:3]
    block = 256
    for at in range(0, channels, block):
        sl = slice(at, at + block)
        ext_ref[:, sl] = nn(both, w_ref[:, at : at + block])
        x0 = ext_ref[HALO : HALO + Q, sl]
        conv_ref[:, sl] = x0
        pre = cb_ref[:, sl] + cw_ref[0:1, sl] * x0
        pre += cw_ref[1:2, sl] * (ext_ref[HALO - 1 : HALO - 1 + Q, sl] * m1)
        pre += cw_ref[2:3, sl] * (ext_ref[HALO - 2 : HALO - 2 + Q, sl] * m2)
        pre += cw_ref[3:4, sl] * (ext_ref[HALO - 3 : HALO - 3 + Q, sl] * m3)
        sig = 1.0 / (1.0 + jnp.exp(-pre))
        act = pre * sig
        act_ref[:, sl] = act
        low_ref[:, sl] = act.astype(bf16)
        dsil_ref[:, sl] = sig * (1.0 + pre * (1.0 - sig))
    v = dt_raw + dtb_ref[...]
    dt = jnp.maximum(v, 0.0) + jnp.log1p(jnp.exp(-jnp.abs(v)))
    dt_ref[...] = dt
    rate = -dt * rate_ref[...]
    row, col = iotas((Q, Q))
    cum = nn_exact((col <= row).astype(bf16), rate)
    cum_ref[...] = cum
    sb_ref[0] = state_ref[...].astype(bf16)
    weight = dt[:, heads:] * jnp.exp(cum[:, heads:] - rate[:, heads:]) * aux[:, 5:6]
    whole = jnp.exp(cum[Q - 1 :, heads:]) * aux[0:1, 7:8]
    scales = split2(jnp.concatenate([weight, jnp.broadcast_to(whole, (8, heads))], axis=0))
    b_bwd = low_ref[:, inner + 2 * state : inner + 3 * state]
    for at in range(0, inner, block):
        sl = slice(at, at + block)
        wide = nn(scales, x2_ref[:, sl])
        vs = (low_ref[:, sl].astype(f32) * wide[:Q]).astype(bf16)
        state_ref[:, sl] = state_ref[:, sl] * wide[Q : Q + 1] + tn(b_bwd, vs)
    if here:
        steps = len(BEATS) - 1
        for i in range(steps):

            @pl.when(step == i)
            def _():
                for t in range(BEATS[i], BEATS[i + 1]):
                    others.beat(t)
                if i == steps - 1:
                    others.finish()
                    mine.wait()


def front(tokens, gain_row, w_in, conv_w, conv_b, dt_bias, rate_row, aux, x2, own, sizes, here):
    inner, channels, heads, state = sizes
    t, d = tokens.shape
    n = t // Q
    rows = own.shape[0]
    rev = lambda i: (n - 1 - i, 0)
    fixed = lambda i: (0, 0)
    blk = lambda width: pl.BlockSpec((Q, width), rev)
    whole = lambda a: pl.BlockSpec(a.shape, fixed)
    per = Q // HALO
    out = lambda width, dtype: jax.ShapeDtypeStruct((t, width), dtype)
    return pl.pallas_call(
        functools.partial(front_kernel, sizes, here),
        grid=(n,),
        in_specs=[
            blk(d),
            pl.BlockSpec((HALO, d), lambda i: (jnp.maximum((n - 1 - i) * per - 1, 0), 0)),
            whole(gain_row), whole(w_in), whole(conv_w), whole(conv_b), whole(dt_bias), whole(rate_row),
            blk(aux.shape[1]), whole(x2), pl.BlockSpec(memory_space=pl.ANY),
        ],
        out_specs=[
            blk(d), blk(channels), blk(channels), blk(channels), blk(channels),
            blk(2 * heads), blk(2 * heads), blk(2 * heads),
            pl.BlockSpec((1, state, inner), lambda i: (n - 1 - i, 0, 0)),
            pl.BlockSpec(memory_space=pl.ANY),
        ],
        out_shape=[
            out(d, bf16), out(channels, f32), out(channels, f32), out(channels, bf16), out(channels, f32),
            out(2 * heads, f32), out(2 * heads, f32), out(2 * heads, f32),
            jax.ShapeDtypeStruct((n, state, inner), bf16),
            jax.ShapeDtypeStruct((32 if here else 1,) + own.shape, bf16),
        ],
        scratch_shapes=[
            pltpu.VMEM((HALO + Q, channels), f32),
            pltpu.VMEM((state, inner), f32),
            pltpu.SemaphoreType.DMA((Gatherer.count,)),
            pltpu.SemaphoreType.DMA((Gatherer.count,)),
            pltpu.SemaphoreType.DMA,
        ],
        compiler_params=pltpu.CompilerParams(
            dimension_semantics=("arbitrary",), vmem_limit_bytes=60 * 1024 * 1024, **reaches(here, 1)
        ),
        cost_estimate=pl.CostEstimate(flops=5_000_000_000, bytes_accessed=50_000_000, transcendentals=0),
    )(tokens, tokens, gain_row, w_in, conv_w, conv_b, dt_bias, rate_row, aux, x2, own)


def middle_kernel(
    sizes,
    tok_ref, act_ref, normed_ref, dt_ref, cum_ref, aux_ref, segrow_ref, cot_ref, sb_ref, w_ref,
    rate_ref, skip_ref, og_ref, x2_ref, r_ref,
    out_ref, nout_ref, dgate_ref, dy_ref, dv_ref, dbc_ref, drate_ref, dq_ref, sf_ref, dog_ref, dsk_ref,
    decay_ref, mix_ref, state_ref, adj_ref, ssm_ref, gated_ref, dno_ref, yf_ref, yb_ref, wide_ref,
    p_ref, q_ref, scal_ref, gate_ref,
):
    inner, channels, heads, state = sizes
    quad = 256
    step = pl.program_id(0)

    @pl.when(step == 0)
    def _():
        state_ref[...] = jnp.zeros_like(state_ref)
        adj_ref[...] = jnp.zeros_like(adj_ref)
        dog_ref[...] = jnp.zeros_like(dog_ref)
        dsk_ref[...] = jnp.zeros_like(dsk_ref)
        q_ref[...] = jnp.zeros_like(q_ref)

    sf_ref[0] = state_ref[...].astype(bf16)
    aux = aux_ref[...]
    row, col = iotas((Q, Q))
    lower = col < row
    same = aux[:, 3:4] == segrow_ref[0]
    b_f = act_ref[:, inner : inner + state].astype(bf16)
    c_f = act_ref[:, inner + state : inner + 2 * state].astype(bf16)
    b_b = act_ref[:, inner + 2 * state : inner + 3 * state].astype(bf16)
    c_b = act_ref[:, inner + 3 * state :].astype(bf16)
    g = jnp.where(same & (col != row), jnp.where(lower, nt(c_f, b_f), nt(c_b, b_b)), 0.0)
    dt = dt_ref[...]
    cum = cum_ref[...]
    rate = -dt * rate_ref[...]
    cf, cb = cum[:, :heads], cum[:, heads:] - rate[:, heads:]
    dtf, dtb = dt[:, :heads], dt[:, heads:]
    total_f, total_b = cum[Q - 1 :, :heads], cum[Q - 1 :, heads:]
    ldt = jnp.log(jnp.maximum(dt, 1e-37))
    rows = jnp.transpose(
        jnp.concatenate(
            [cf - ldt[:, :heads], cb + ldt[:, heads:], jnp.zeros((Q, Q - 2 * heads), f32)], axis=1
        )
    )
    scales = split2(
        jnp.concatenate(
            [
                jnp.exp(cf) * aux[:, 6:7],
                jnp.exp(total_b - cb) * aux[:, 7:8],
                dtf * jnp.exp(total_f - cf) * aux[:, 4:5],
                dtb * jnp.exp(cb) * aux[:, 5:6],
                jnp.broadcast_to(jnp.exp(total_f) * aux[Q - 1 :, 6:7], (8, heads)),
                jnp.broadcast_to(jnp.exp(total_b) * aux[0:1, 7:8], (8, heads)),
            ],
            axis=0,
        )
    )
    lane = lax.broadcasted_iota(jnp.int32, (1, Q), 1)
    first = (lane < Q // 2).astype(bf16)
    second = (lane >= Q // 2).astype(bf16)

    def apart(x):
        return jnp.concatenate([x * first, x * second], axis=0)

    squares = jnp.zeros((Q, quad), f32)
    dots = jnp.zeros((Q, quad), f32)
    cot = cot_ref[...]
    for at in range(0, inner, quad):
        sl = slice(at, at + quad)
        wide_ref[:, sl] = nn(scales, x2_ref[:, sl])
        v = act_ref[:, sl]
        low = v.astype(bf16)
        yf = nn(c_f, state_ref[:, sl].astype(bf16)) * wide_ref[:Q, sl]
        yb = nn(c_b, sb_ref[0, :, sl]) * wide_ref[Q : 2 * Q, sl]
        yf_ref[:, sl] = yf
        yb_ref[:, sl] = yb
        parts = []
        for half in range(2):
            mixes = []
            for h in (at // 64 + 2 * half, at // 64 + 2 * half + 1):
                gap = jnp.where(
                    lower,
                    cf[:, h : h + 1] - rows[h : h + 1, :],
                    rows[heads + h : heads + h + 1, :] - cb[:, h : h + 1],
                )
                decay = jnp.exp(gap)
                decay_ref[h] = decay
                mix = (g * decay).astype(bf16)
                mix_ref[h * Q : (h + 1) * Q, :] = mix
                mixes.append(mix)
            parts.append(
                nn(jnp.concatenate(mixes, axis=1), apart(low[:, half * Q : (half + 1) * Q]))
            )
        ssm = jnp.concatenate(parts, axis=1) + yf + yb + skip_ref[:, sl] * v
        ssm_ref[:, sl] = ssm
        gate = nn(normed_ref[...], w_ref[:, sl])
        gate_ref[:, sl] = gate
        gated = ssm * (gate / (1.0 + jnp.exp(-gate)))
        gated_ref[:, sl] = gated
        dno = nn(cot, w_ref[:, inner + at : inner + at + quad])
        dno_ref[:, sl] = dno
        squares += gated * gated
        dots += dno * og_ref[:, sl] * gated

    inv = lax.rsqrt(jnp.sum(squares, axis=1, keepdims=True) / inner + eps)
    drag = inv * (inv * jnp.sum(dots, axis=1, keepdims=True) / inner)
    dg = jnp.zeros((Q, Q), f32)
    d_cf = jnp.zeros((Q, state), f32)
    d_cb = jnp.zeros((Q, state), f32)
    d_bb = jnp.zeros((Q, state), f32)
    heads_of = jnp.zeros((3 * Q, Q), f32)
    for at in range(0, inner, quad):
        sl = slice(at, at + quad)
        v = act_ref[:, sl]
        low = v.astype(bf16)
        low_f = low.astype(f32)
        ssm, gate, gated, dno = ssm_ref[:, sl], gate_ref[:, sl], gated_ref[:, sl], dno_ref[:, sl]
        og = og_ref[:, sl]
        unit = gated * inv
        nout_ref[:, sl] = (unit * og).astype(bf16)
        dog_ref[:, sl] += jnp.sum(dno * unit, axis=0, keepdims=True)
        d_gated = inv * (dno * og) - gated * (inv * drag)
        sig = 1.0 / (1.0 + jnp.exp(-gate))
        d_ssm = d_gated * (gate * sig)
        dgate_ref[:, sl] = (d_gated * ssm * (sig * (1.0 + gate * (1.0 - sig)))).astype(bf16)
        dsk_ref[:, sl] += jnp.sum(d_ssm * v, axis=0, keepdims=True)
        dy = d_ssm.astype(bf16)
        dy_ref[:, sl] = dy
        dy_f = dy.astype(f32)
        parts = []
        for half in range(2):
            h0 = at // 64 + 2 * half
            cut = slice(half * Q, (half + 1) * Q)
            d_mix = nt(dy[:, cut], apart(low[:, cut]))
            for i in range(2):
                h = h0 + i
                x = d_mix[:, i * Q : (i + 1) * Q] * decay_ref[h]
                dg += x
                full = x * g
                under = jnp.where(lower, full, 0.0)
                over = full - under
                q_ref[h : h + 1, :] = jnp.sum(under, axis=0, keepdims=True)
                q_ref[heads + h : heads + h + 1, :] = jnp.sum(over, axis=0, keepdims=True)
                p_ref[:, h : h + 1] = jnp.sum(under, axis=1, keepdims=True)
                p_ref[:, heads + h : heads + h + 1] = jnp.sum(over, axis=1, keepdims=True)
            parts.append(tn(mix_ref[h0 * Q : (h0 + 2) * Q, :], apart(dy[:, cut])))
        adj = adj_ref[:, sl]
        adj_low = adj.astype(bf16)
        sf_low = state_ref[:, sl].astype(bf16)
        sb_low = sb_ref[0, :, sl]
        wide_wb = wide_ref[3 * Q : 4 * Q, sl]
        dvb = wide_wb * nn(b_b, adj_low)
        dv_ref[:, sl] = d_ssm * skip_ref[:, sl] + jnp.concatenate(parts, axis=1) + dvb
        prods = jnp.concatenate(
            [
                (dy_f * yf_ref[:, sl]).astype(bf16),
                (dy_f * yb_ref[:, sl]).astype(bf16),
                (low_f * dvb).astype(bf16),
            ],
            axis=0,
        )
        heads_of += nn(prods, r_ref[sl, :])
        dye_f = (dy_f * wide_ref[:Q, sl]).astype(bf16)
        dye_b = (dy_f * wide_ref[Q : 2 * Q, sl]).astype(bf16)
        vs_f = (low_f * wide_ref[2 * Q : 3 * Q, sl]).astype(bf16)
        vs_b = (low_f * wide_wb).astype(bf16)
        d_cf += nt(dye_f, sf_low)
        d_cb += nt(dye_b, sb_low)
        d_bb += nt(vs_b, adj_low)
        across_b = wide_ref[4 * Q + 8 : 4 * Q + 9, sl]
        scal_ref[:, sl] = jnp.sum(adj * sb_low.astype(f32), axis=0, keepdims=True) * across_b
        adj_ref[:, sl] = adj * across_b + tn(c_b, dye_b)
        state_ref[:, sl] = state_ref[:, sl] * wide_ref[4 * Q : 4 * Q + 1, sl] + tn(b_f, vs_f)

    out_ref[...] = (tok_ref[...].astype(f32) + nt(nout_ref[...], w_ref[:, inner:])).astype(bf16)
    dg = jnp.where(same & (col != row), dg, 0.0)
    dg_f = jnp.where(lower, dg, 0.0)
    dg_b = (dg - dg_f).astype(bf16)
    dg_f = dg_f.astype(bf16)
    dbc_ref[...] = jnp.concatenate(
        [tn(dg_f, c_f), d_cf + nn(dg_f, b_f), d_bb + tn(dg_b, c_b), d_cb + nn(dg_b, b_b)], axis=1
    )
    q_cols = jnp.transpose(q_ref[...])[:, : 2 * heads]
    dots_f, dots_b, dots_v = heads_of[:Q, :heads], heads_of[Q : 2 * Q, :heads], heads_of[2 * Q :, :heads]
    through = nn(split_rows(jnp.broadcast_to(scal_ref[...], (8, inner))), r_ref[...])
    through = (through[0:1] + through[8:9])[:, :heads]
    diff = p_ref[:, : 2 * heads] - q_cols
    d_rate_f = nn_exact((col >= row).astype(bf16), diff[:, :heads] + dots_f)
    d_rate_b = (
        nn_exact((col <= row).astype(bf16), diff[:, heads:] + dots_b)
        + nn_exact((col > row).astype(bf16), dots_v)
        + through
    )
    drate_ref[...] = jnp.concatenate([d_rate_f, d_rate_b], axis=1)
    dq_ref[...] = jnp.concatenate([q_cols[:, :heads], q_cols[:, heads:] + dots_v], axis=1)


def middle(tokens, act, normed, dt, cum, aux, segrow, cot, sb, w_side, rate_row, skip_row, og_row, x2, r, sizes):
    inner, channels, heads, state = sizes
    t, d = tokens.shape
    n = t // Q
    fwd = lambda i: (i, 0)
    fixed = lambda i: (0, 0)
    cube = lambda i: (i, 0, 0)
    blk = lambda width: pl.BlockSpec((Q, width), fwd)
    whole = lambda a: pl.BlockSpec(a.shape, fixed)
    out = lambda width, dtype: jax.ShapeDtypeStruct((t, width), dtype)
    line = jax.ShapeDtypeStruct((1, inner), f32)
    return pl.pallas_call(
        functools.partial(middle_kernel, sizes),
        grid=(n,),
        in_specs=[
            blk(d), blk(channels), blk(d), blk(2 * heads), blk(2 * heads), blk(aux.shape[1]),
            pl.BlockSpec((1, 1, Q), cube), blk(d), pl.BlockSpec((1, state, inner), cube),
            whole(w_side), whole(rate_row), whole(skip_row), whole(og_row), whole(x2), whole(r),
        ],
        out_specs=[
            blk(d), blk(inner), blk(inner), blk(inner), blk(inner), blk(4 * state),
            blk(2 * heads), blk(2 * heads), pl.BlockSpec((1, state, inner), cube),
            pl.BlockSpec((1, inner), fixed), pl.BlockSpec((1, inner), fixed),
        ],
        out_shape=[
            out(d, bf16), out(inner, bf16), out(inner, bf16), out(inner, bf16), out(inner, f32),
            out(4 * state, f32), out(2 * heads, f32), out(2 * heads, f32),
            jax.ShapeDtypeStruct((n, state, inner), bf16), line, line,
        ],
        scratch_shapes=[
            pltpu.VMEM((heads, Q, Q), f32),
            pltpu.VMEM((heads * Q, Q), bf16),
            pltpu.VMEM((state, inner), f32),
            pltpu.VMEM((state, inner), f32),
            pltpu.VMEM((Q, inner), f32),
            pltpu.VMEM((Q, inner), f32),
            pltpu.VMEM((Q, inner), f32),
            pltpu.VMEM((Q, inner), f32),
            pltpu.VMEM((Q, inner), f32),
            pltpu.VMEM((4 * Q + 16, inner), f32),
            pltpu.VMEM((Q, Q), f32),
            pltpu.VMEM((Q, Q), f32),
            pltpu.VMEM((1, inner), f32),
            pltpu.VMEM((Q, inner), f32),
        ],
        compiler_params=pltpu.CompilerParams(
            dimension_semantics=("arbitrary",), vmem_limit_bytes=60 * 1024 * 1024
        ),
        cost_estimate=pl.CostEstimate(flops=30_000_000_000, bytes_accessed=60_000_000, transcendentals=0),
    )(tokens, act, normed, dt, cum, aux, segrow, cot, sb, w_side, rate_row, skip_row, og_row, x2, r)


def back_kernel(
    sizes,
    tok_ref, cot_ref, gain_ref, w_ref, side_ref, cw_ref, dtb_ref, rate_ref, aux_ref, x2_ref, r_ref,
    low_ref, dsil_ref, conv_ref, dt_ref, cum_ref, dtraw_ref,
    dgate_ref, dy_ref, dv_ref, dbc_ref, drate_ref, dq_ref, sf_ref, dog_ref, dsk_ref,
    dproj_ref, dtok_ref, small_ref,
    adj_ref, dpre_ref, scal_ref,
):
    inner, channels, heads, state = sizes
    quad = 256
    step = pl.program_id(0)

    @pl.when(step == 0)
    def _():
        adj_ref[...] = jnp.zeros_like(adj_ref)
        dpre_ref[...] = jnp.zeros_like(dpre_ref)
        small_ref[...] = jnp.zeros_like(small_ref)
        small_ref[5:6, :inner] = dog_ref[...]
        skips = nn(split_rows(jnp.broadcast_to(dsk_ref[...], (8, inner))), r_ref[...])
        small_ref[6:7, SKIP_AT : SKIP_AT + Q] = skips[0:1] + skips[8:9]

    d = tok_ref.shape[1]

    dpre_ref[Q:, :] = dpre_ref[0:8, :]
    aux = aux_ref[...]
    dt = dt_ref[...]
    cum = cum_ref[...]
    cf, dtf = cum[:, :heads], dt[:, :heads]
    total_f = cf[Q - 1 :, :]
    scales = split2(
        jnp.concatenate(
            [
                jnp.exp(cf) * aux[:, 6:7],
                dtf * jnp.exp(total_f - cf) * aux[:, 4:5],
                jnp.broadcast_to(jnp.exp(total_f) * aux[Q - 1 :, 6:7], (8, heads)),
            ],
            axis=0,
        )
    )
    b_f = low_ref[:, inner : inner + state]
    c_f = low_ref[:, inner + state : inner + 2 * state]
    dots = jnp.zeros((Q, Q), f32)
    d_bf = jnp.zeros((Q, state), f32)
    for at in range(0, inner, quad):
        sl = slice(at, at + quad)
        wide = nn(scales, x2_ref[:, sl])
        low_f = low_ref[:, sl].astype(f32)
        adj = adj_ref[:, sl]
        adj_low = adj.astype(bf16)
        wide_wf = wide[Q : 2 * Q]
        dvf = wide_wf * nn(b_f, adj_low)
        dots += nn((low_f * dvf).astype(bf16), r_ref[sl, :])
        d_bf += nt((low_f * wide_wf).astype(bf16), adj_low)
        across = wide[2 * Q : 2 * Q + 1]
        scal_ref[:, sl] = jnp.sum(adj * sf_ref[0, :, sl].astype(f32), axis=0, keepdims=True) * across
        dye = (dy_ref[:, sl].astype(f32) * wide[:Q]).astype(bf16)
        adj_ref[:, sl] = adj * across + tn(c_f, dye)
        dpre_ref[:Q, sl] = (dv_ref[:, sl] + dvf) * dsil_ref[:, sl]
    d_bc = dbc_ref[...] + jnp.concatenate([d_bf, jnp.zeros((Q, 3 * state), f32)], axis=1)
    dpre_ref[:Q, inner:] = d_bc * dsil_ref[:, inner:]

    n1, n2, n3 = aux[:, 8:9], aux[:, 9:10], aux[:, 10:11]
    for at in range(0, channels, quad):
        sl = slice(at, at + quad)
        conv = conv_ref[:, sl]
        z = dpre_ref[:Q, sl]
        small_ref[4:5, sl] += jnp.sum(z, axis=0, keepdims=True)
        small_ref[0:1, sl] += jnp.sum(z * conv, axis=0, keepdims=True)
        total = cw_ref[0:1, sl] * z
        for k, mask in ((1, n1), (2, n2), (3, n3)):
            z = dpre_ref[k : Q + k, sl] * mask
            small_ref[k : k + 1, sl] += jnp.sum(z * conv, axis=0, keepdims=True)
            total += cw_ref[k : k + 1, sl] * z
        dproj_ref[:, inner + at : inner + at + quad] = total.astype(bf16)
    dproj_ref[:, :inner] = dgate_ref[...]

    row, col = iotas((Q, Q))
    through = nn(split_rows(jnp.broadcast_to(scal_ref[...], (8, inner))), r_ref[...])
    through = (through[0:1] + through[8:9])[:, :heads]
    dots = dots[:, :heads]
    extra = nn_exact((col < row).astype(bf16), dots) + through
    none = jnp.zeros((Q, heads), f32)
    d_rate = drate_ref[...] + jnp.concatenate([extra, none], axis=1)
    d_dt = dq_ref[...] + jnp.concatenate([dots, none], axis=1)
    d_dt = jnp.where(dt > 0.0, d_dt / jnp.maximum(dt, 1e-37), 0.0)
    a = rate_ref[...]
    v = dtraw_ref[...] + dtb_ref[...]
    d_v = (d_dt - d_rate * a) / (1.0 + jnp.exp(-v))
    small_ref[6:7, BIAS_AT : BIAS_AT + 2 * heads] += jnp.sum(d_v, axis=0, keepdims=True)
    small_ref[6:7, LOG_AT : LOG_AT + 2 * heads] += jnp.sum(d_rate * (-dt * a), axis=0, keepdims=True)
    dproj_ref[:, inner + channels :] = d_v.astype(bf16)

    d_normed = (
        nt(dproj_ref[:, :inner], side_ref[:, :inner])
        + nt(dproj_ref[:, inner : inner + channels], w_ref[:, :channels])
        + nt(dproj_ref[:, inner + channels :], w_ref[:, channels : channels + 2 * heads])
    )
    x = tok_ref[...].astype(f32)
    inv = lax.rsqrt(jnp.mean(x * x, axis=1, keepdims=True) + eps)
    unit = x * inv
    small_ref[6:7, :d] += jnp.sum(d_normed * unit, axis=0, keepdims=True)
    a = d_normed * gain_ref[...]
    dtok_ref[...] = cot_ref[...].astype(f32) + inv * (a - unit * jnp.mean(a * unit, axis=1, keepdims=True))


def back(
    tokens, cot, gain_row, w_in, w_side, conv_w, dt_bias, rate_row, aux, x2, r, low, dsil, conv, dt, cum, dtraw,
    dgate, dy, dv, dbc, drate, dq, sf, dog, dsk, sizes,
):
    inner, channels, heads, state = sizes
    t, d = tokens.shape
    n = t // Q
    proj = inner + channels + 2 * heads
    rev = lambda i: (n - 1 - i, 0)
    fixed = lambda i: (0, 0)
    blk = lambda a: pl.BlockSpec((Q, a.shape[1]), rev)
    whole = lambda a: pl.BlockSpec(a.shape, fixed)
    return pl.pallas_call(
        functools.partial(back_kernel, sizes),
        grid=(n,),
        in_specs=[
            blk(tokens), blk(cot), whole(gain_row), whole(w_in), pl.BlockSpec((w_side.shape[0], inner), fixed), whole(conv_w), whole(dt_bias), whole(rate_row),
            blk(aux), whole(x2), whole(r), blk(low), blk(dsil), blk(conv), blk(dt), blk(cum), blk(dtraw),
            blk(dgate), blk(dy), blk(dv), blk(dbc), blk(drate), blk(dq),
            pl.BlockSpec((1, state, inner), lambda i: (n - 1 - i, 0, 0)), whole(dog), whole(dsk),
        ],
        out_specs=[pl.BlockSpec((Q, proj), rev), pl.BlockSpec((Q, d), rev), pl.BlockSpec((8, channels), fixed)],
        out_shape=[
            jax.ShapeDtypeStruct((t, proj), bf16),
            jax.ShapeDtypeStruct((t, d), f32),
            jax.ShapeDtypeStruct((8, channels), f32),
        ],
        scratch_shapes=[
            pltpu.VMEM((state, inner), f32),
            pltpu.VMEM((Q + 8, channels), f32),
            pltpu.VMEM((1, inner), f32),
        ],
        compiler_params=pltpu.CompilerParams(
            dimension_semantics=("arbitrary",), vmem_limit_bytes=60 * 1024 * 1024
        ),
        cost_estimate=pl.CostEstimate(flops=20_000_000_000, bytes_accessed=60_000_000, transcendentals=0),
    )(
        tokens, cot, gain_row, w_in, w_side, conv_w, dt_bias, rate_row, aux, x2, r, low, dsil, conv, dt, cum, dtraw,
        dgate, dy, dv, dbc, drate, dq, sf, dog, dsk,
    )


def features(segment_ids):
    t = segment_ids.shape[0]
    n = t // Q
    seg = segment_ids.astype(f32)
    earlier = [jnp.concatenate([jnp.full((k,), -1.0, f32), seg[: t - k]]) == seg for k in (1, 2, 3)]
    later = [jnp.concatenate([seg[k:], jnp.full((k,), -1.0, f32)]) == seg for k in (1, 2, 3)]
    chunks = seg.reshape(n, Q)
    ends, starts = chunks[:, -1:], chunks[:, :1]
    none = jnp.full((1, 1), -1.0, f32)
    like = lambda edge: (chunks == edge).reshape(t)
    columns = earlier + [
        seg,
        like(ends),
        like(starts),
        like(jnp.concatenate([none, ends[:-1]])),
        like(jnp.concatenate([starts[1:], none])),
    ] + later
    aux = jnp.stack([c.astype(f32) for c in columns], axis=1)
    return aux, chunks.reshape(n, 1, Q)


def local(here, tokens, segment_ids, w_in, own_side, gain, conv_w, conv_b, dt_bias, a_log, d_skip, out_gain, cotangent):
    heads = d_skip.shape[0]
    inner = out_gain.shape[0]
    channels = conv_w.shape[1]
    state = (channels - inner) // 4
    width = inner // heads
    sizes = (inner, channels, heads, state)
    aux, segrow = features(segment_ids)
    spread = np.arange(inner)[None, :] // width == np.arange(heads)[:, None]
    x2 = jnp.asarray(np.concatenate([spread, spread], axis=0), bf16)
    r = jnp.asarray(np.pad(spread.T, ((0, 0), (0, Q - heads))), bf16)
    gain_row = gain.astype(f32)[None, :]
    rate_row = jnp.exp(a_log)[None, :]
    dtb_row = dt_bias[None, :]
    skip_row = jnp.repeat(d_skip, width)[None, :]
    normed, conv, act, low, dsil, dt, cum, dtraw, sb, w_side = front(
        tokens, gain_row, w_in, conv_w, conv_b[None, :], dtb_row, rate_row, aux, x2, own_side, sizes, here
    )
    if not here:
        w_side = lax.all_gather(own_side, AXES)
    w_side = w_side.reshape(-1, 2 * inner)
    output, nout, dgate, dy, dv, dbc, drate, dq, sf, d_og, d_sk = middle(
        tokens, act, normed, dt, cum, aux, segrow, cotangent, sb, w_side, rate_row, skip_row,
        out_gain[None, :], x2, r, sizes,
    )
    d_w_out_t = tn(cotangent, nout).astype(bf16)
    dproj, d_tokens, small = back(
        tokens, cotangent, gain_row, w_in, w_side, conv_w, dtb_row, rate_row, aux, x2, r, low, dsil, conv, dt, cum, dtraw,
        dgate, dy, dv, dbc, drate, dq, sf, d_og, d_sk, sizes,
    )
    d_w_in = tn(normed, dproj).astype(bf16)
    return output, d_tokens, d_w_in, d_w_out_t, small


def unpack(small, taps, inner, heads, d):
    return small[6, :d], (
        small[:taps],
        small[taps],
        small[6, BIAS_AT : BIAS_AT + 2 * heads],
        small[6, LOG_AT : LOG_AT + 2 * heads],
        small[6, SKIP_AT : SKIP_AT + heads],
        small[5, :inner],
    )


def body(here, tokens, segment_ids, w_in, w_out, norm_gain, conv_w, conv_b, dt_bias, a_log, d_skip, out_gain, cotangent):
    rows, proj = w_in.shape
    d, inner, heads = tokens.shape[1], out_gain.shape[0], d_skip.shape[0]
    parts = d // rows
    own_first = jnp.concatenate([w_in[:, inner:], norm_gain[:, None]], axis=1)
    own_side = jnp.concatenate([w_in[:, :inner], w_out.T], axis=1)
    first = gather(own_first)[0] if here else lax.all_gather(own_first, AXES)
    first = first.reshape(d, proj - inner + 1)
    output, d_tokens, g_in, g_out_t, small = local(
        here, tokens, segment_ids, first, own_side, first[:, proj - inner], conv_w, conv_b, dt_bias, a_log, d_skip,
        out_gain, cotangent,
    )
    g_in, g_out_t = g_in.reshape(parts, rows, proj), g_out_t.reshape(parts, rows, inner)
    if here:
        d_w_in, d_w_out, small = scatter([g_in, g_out_t], small)
    else:
        d_w_in = lax.psum_scatter(g_in.astype(f32), AXES, scatter_dimension=0)
        d_w_out = lax.psum_scatter(g_out_t.astype(f32), AXES, scatter_dimension=0)
        small = lax.psum(small, AXES)
    d_gain, small = unpack(small, conv_w.shape[0], inner, heads, d)
    d_gain = lax.dynamic_slice_in_dim(d_gain, lax.axis_index(AXES) * rows, rows)
    return (output, d_tokens, d_w_in, d_w_out.T, d_gain) + small


def solution(mesh):
    rows, cols, line, none = P(AXES, None), P(None, AXES), P(AXES), P()
    here = dict(mesh.shape) == {"fsdp": 8, "rep": 4}
    return jax.shard_map(
        functools.partial(body, here),
        mesh=mesh,
        in_specs=(rows, line, rows, cols, line, none, none, none, none, none, none, rows),
        out_specs=(rows, rows, rows, cols, line, none, none, none, none, none, none),
        check_vma=False,
    )
```

```python
import functools

import jax
import jax.numpy as jnp
import numpy as np
from jax import lax
from jax.experimental import pallas as pl
from jax.experimental.pallas import tpu as pltpu
from jax.sharding import PartitionSpec as P

eps = 1e-05
Q = 128
HALO = 16
f32 = jnp.float32
bf16 = jnp.bfloat16
AXES = ("fsdp", "rep")
BIAS_AT, LOG_AT, SKIP_AT = 768, 896, 1024


def nn(a, b):
    return lax.dot_general(a, b, (((1,), (0,)), ((), ())), preferred_element_type=f32)


def nt(a, b):
    return lax.dot_general(a, b, (((1,), (1,)), ((), ())), preferred_element_type=f32)


def tn(a, b):
    return lax.dot_general(a, b, (((0,), (0,)), ((), ())), preferred_element_type=f32)


def split2(x):
    hi = x.astype(bf16)
    lo = (x - hi.astype(f32)).astype(bf16)
    return jnp.concatenate([hi, lo], axis=1)


def split_rows(x):
    hi = x.astype(bf16)
    return jnp.concatenate([hi, (x - hi.astype(f32)).astype(bf16)], axis=0)


def nn_exact(ones_mask, x):
    hi = x.astype(bf16)
    r = x - hi.astype(f32)
    mid = r.astype(bf16)
    lo = (r - mid.astype(f32)).astype(bf16)
    return nn(ones_mask, hi) + (nn(ones_mask, mid) + nn(ones_mask, lo))


def iotas(shape):
    return (
        lax.broadcasted_iota(jnp.int32, shape, 0),
        lax.broadcasted_iota(jnp.int32, shape, 1),
    )


MESH = pl.DeviceIdType.MESH
LINE = 4
STEPS = (0, -1, 1, -2, 2, -3, 3)
LAG = 2


def place():
    f = lax.axis_index("fsdp")
    return f // 4, (f // 2) % 2, f % 2, lax.axis_index("rep")


def flip(at, dy, dx, dc, dz):
    y, x, c, z = at
    return (1 - y if dy else y, 1 - x if dx else x, 1 - c if dc else c, z + dz)


def device(at):
    y, x, c, z = at
    return ((y * 2 + x) * 2 + c, z)


def slot(at):
    y, x, c, z = at
    return ((y * 2 + x) * 2 + c) * LINE + z


def on_line(me, dz):
    z = me[3]
    return z >= -dz if dz < 0 else z < LINE - dz


def when(condition, act):
    if condition is True:
        act()
    else:
        pl.when(condition)(act)


def greet(me):
    barrier = pltpu.get_barrier_semaphore()
    for other in ((0, 0, 1, 0), (0, 1, 0, 0), (1, 0, 0, 0)):
        pl.semaphore_signal(barrier, inc=1, device_id=device(flip(me, *other)), device_id_type=MESH)
    for dz in (-1, 1):

        @pl.when(on_line(me, dz))
        def _():
            pl.semaphore_signal(barrier, inc=1, device_id=device(flip(me, 0, 0, 0, dz)), device_id_type=MESH)

    inside = jnp.where((me[3] > 0) & (me[3] < LINE - 1), 1, 0)
    pl.semaphore_wait(barrier, 4 + inside)


def halves(width):
    cut = (width // 2 + 127) // 128 * 128
    return slice(0, cut), slice(cut, width)


class Gatherer:
    kinds = ("z", "x", "y", "c", "left", "right", "cx", "cy", "cl", "cr")
    count = len(kinds) * len(STEPS)

    def __init__(self, me, own, full, send, recv):
        self.me, self.own, self.full, self.send, self.recv = me, own, full, send, recv
        self.left, self.right = halves(full.shape[2])

    def made(self, kind, dz, block, to, cols=None):
        i = self.kinds.index(kind) * len(STEPS) + STEPS.index(dz)
        at = slot(flip(self.me, *block))
        dst = self.full.at[at] if cols is None else self.full.at[at, :, cols]
        src = dst
        if block == (0, 0, 0, 0):
            src = self.own if cols is None else self.own.at[:, cols]
        return pltpu.make_async_remote_copy(
            src_ref=src, dst_ref=dst, send_sem=self.send.at[i], recv_sem=self.recv.at[i],
            device_id=device(flip(self.me, *to)), device_id_type=MESH,
        )

    def copy(self, kind, dz):
        return {
            "x": lambda: self.made("x", dz, (0, 0, 0, dz), (0, 1, 0, 0)),
            "y": lambda: self.made("y", dz, (0, 0, 0, dz), (1, 0, 0, 0)),
            "c": lambda: self.made("c", dz, (0, 0, 0, dz), (0, 0, 1, 0)),
            "left": lambda: self.made("left", dz, (0, 1, 0, dz), (1, 0, 0, 0), self.left),
            "right": lambda: self.made("right", dz, (1, 0, 0, dz), (0, 1, 0, 0), self.right),
            "cx": lambda: self.made("cx", dz, (0, 1, 0, dz), (0, 0, 1, 0)),
            "cy": lambda: self.made("cy", dz, (1, 0, 0, dz), (0, 0, 1, 0)),
            "cl": lambda: self.made("cl", dz, (1, 1, 0, dz), (0, 0, 1, 0), self.left),
            "cr": lambda: self.made("cr", dz, (1, 1, 0, dz), (0, 0, 1, 0), self.right),
        }[kind]()

    def along(self, dz, way):
        i = self.kinds.index("z") * len(STEPS) + STEPS.index(dz - way)
        at = slot(flip(self.me, 0, 0, 0, dz))
        return pltpu.make_async_remote_copy(
            src_ref=self.full.at[at] if dz else self.own, dst_ref=self.full.at[at],
            send_sem=self.send.at[i], recv_sem=self.recv.at[i],
            device_id=device(flip(self.me, 0, 0, 0, way)), device_id_type=MESH,
        )

    def sent_along(self):
        for dz in STEPS:
            for way in (-1, 1):
                if dz * way <= 0 and abs(dz - way) < LINE:
                    yield dz, way, on_line(self.me, way) & (True if dz == 0 else on_line(self.me, dz))

    def each(self, act):
        for dz in STEPS:
            when(True if dz == 0 else on_line(self.me, dz), functools.partial(act, dz))

    def start(self):
        for dz, way, ok in self.sent_along():
            if dz == 0:
                when(ok, lambda dz=dz, way=way: self.along(dz, way).start())
        self.spread(0)

    def spread(self, dz):
        for kind in ("x", "y", "c"):
            self.copy(kind, dz).start()

    def column(self, dz):
        if dz == 0:
            return
        way = -1 if dz > 0 else 1
        self.along_arrived(dz)
        if abs(dz) < LINE - 1:
            when(on_line(self.me, way), lambda: self.along(dz, way).start())
        self.spread(dz)

    def along_arrived(self, dz):
        i = self.kinds.index("z") * len(STEPS) + STEPS.index(dz)
        ref = self.full.at[slot(flip(self.me, 0, 0, 0, dz))]
        pltpu.make_async_remote_copy(
            src_ref=ref, dst_ref=ref, send_sem=self.send.at[i], recv_sem=self.recv.at[i],
            device_id=device(flip(self.me, 0, 0, 0, 1 if dz > 0 else -1)), device_id_type=MESH,
        ).wait_recv()

    def corner(self, dz):
        self.copy("x", dz).wait_recv()
        self.copy("left", dz).start()
        self.copy("cx", dz).start()
        self.copy("y", dz).wait_recv()
        self.copy("right", dz).start()
        self.copy("cy", dz).start()

    def last(self, dz):
        self.copy("left", dz).wait_recv()
        self.copy("cl", dz).start()
        self.copy("right", dz).wait_recv()
        self.copy("cr", dz).start()

    def beat(self, t):
        for lag, act in ((0, self.column), (LAG, self.corner), (2 * LAG, self.last)):
            if 0 <= t - lag < len(STEPS):
                dz = STEPS[t - lag]
                when(True if dz == 0 else on_line(self.me, dz), functools.partial(act, dz))

    beats = len(STEPS) + 2 * LAG

    def finish(self):
        def act(dz):
            for kind in ("c", "cx", "cy", "cl", "cr"):
                self.copy(kind, dz).wait_recv()
            for kind in self.kinds[1:]:
                self.copy(kind, dz).wait_send()

        self.each(act)
        for dz, way, ok in self.sent_along():
            when(ok, lambda dz=dz, way=way: self.along(dz, way).wait_send())


def partner(at, dy, dx, dc, k):
    return flip(at, dy, dx, dc, 0)[:3] + ({0: at[3], 1: at[3] + 1 - 2 * (at[3] % 2), 2: (at[3] + 2) % 4, 3: 3 - at[3]}[k],)


def greet_all(me):
    barrier = pltpu.get_barrier_semaphore()
    others = [(0, 0, 1, 0), (0, 1, 0, 0), (1, 0, 0, 0), (0, 0, 0, 1), (0, 0, 0, 2), (0, 0, 0, 3)]
    for other in others:
        pl.semaphore_signal(barrier, inc=1, device_id=device(partner(me, *other)), device_id_type=MESH)
    pl.semaphore_wait(barrier, len(others))


BLOCKS = ((1, 1), (0, 1), (1, 0), (0, 0))


ORDER = (3, 2, 1, 0)


class Scatterer:
    count = 59

    def __init__(self, me, part, out, mine, from_core, from_pair, from_far, from_line, send, recv, here=None):
        self.me, self.part, self.out = me, part, out
        self.mine, self.from_core, self.from_pair, self.from_far, self.from_line = (
            mine, from_core, from_pair, from_far, from_line,
        )
        self.send, self.recv, self.here = send, recv, here
        self.left, self.right = halves(part.shape[2])

    def copy(self, name, index):
        if name == "core":
            b, k, half = index // 8, index // 2 % 4, index % 2
            cols = self.right if half else self.left
            src = self.part.at[slot(partner(self.me, *BLOCKS[b], 1, k)), :, cols]
            dst, to, i = self.from_core.at[b, k, :, cols], (0, 0, 1, 0), index
        elif name == "x":
            b, k = index // 4, index % 4
            src, dst = self.mine.at[b, k, :, self.left], self.from_pair.at[b, k, :, self.left]
            to, i = (0, 1, 0, 0), 32 + index
        elif name == "y":
            b, k = index // 4, index % 4
            src, dst = self.mine.at[2 * b, k, :, self.right], self.from_pair.at[b, k, :, self.right]
            to, i = (1, 0, 0, 0), 40 + index
        elif name == "fy":
            src, dst = self.mine.at[2, index, :, self.left], self.from_far.at[index, :, self.left]
            to, i = (1, 0, 0, 0), 48 + index
        elif name == "fx":
            src, dst = self.mine.at[1, index, :, self.right], self.from_far.at[index, :, self.right]
            to, i = (0, 1, 0, 0), 52 + index
        else:
            src, dst, to, i = self.mine.at[3, index], self.from_line.at[index - 1], (0, 0, 0, index), 55 + index
        return pltpu.make_async_remote_copy(
            src_ref=src, dst_ref=dst, send_sem=self.send.at[i], recv_sem=self.recv.at[i],
            device_id=device(partner(self.me, *to)), device_id_type=MESH,
        )

    def local(self, b, k):
        own = slot(partner(self.me, *BLOCKS[b], 0, k))
        return pltpu.make_async_copy(self.part.at[own], self.mine.at[b, k], self.here.at[b * 4 + k])

    def start(self, *cuts):
        for k in ORDER:
            for b in range(4):
                for half in cuts or (0, 1):
                    self.copy("core", b * 8 + k * 2 + half).start()
                if self.here is not None:
                    self.local(b, k).start()

    def add(self, b, k, cols, others):
        total = self.mine[b, k, :, cols].astype(f32)
        for ref in others:
            total += ref.astype(f32)
        return total

    def pair(self, k):
        for b in range(4):
            for half in (0, 1):
                self.copy("core", b * 8 + k * 2 + half).wait_recv()
            if self.here is not None:
                self.local(b, k).wait()
                own = self.mine[b, k]
            else:
                own = self.part[slot(partner(self.me, *BLOCKS[b], 0, k))]
            self.mine[b, k] = (own.astype(f32) + self.from_core[b, k].astype(f32)).astype(bf16)
            if b < 2:
                self.copy("x", b * 4 + k).start()
            if b % 2 == 0:
                self.copy("y", b * 2 + k).start()

    def far(self, k):
        self.copy("x", k).wait_recv()
        self.mine[2, k, :, self.left] = self.add(2, k, self.left, [self.from_pair[0, k, :, self.left]]).astype(bf16)
        self.copy("fy", k).start()
        self.copy("y", k).wait_recv()
        self.mine[1, k, :, self.right] = self.add(1, k, self.right, [self.from_pair[0, k, :, self.right]]).astype(bf16)
        self.copy("fx", k).start()

    def line(self, k):
        for made in (self.copy("x", 4 + k), self.copy("y", 4 + k), self.copy("fy", k), self.copy("fx", k)):
            made.wait_recv()
        if k:
            self.mine[3, k] = self.add(3, k, slice(None), [self.from_pair[1, k], self.from_far[k]]).astype(bf16)
            self.copy("z", k).start()

    def finish(self):
        for k in (1, 2, 3):
            self.copy("z", k).wait_recv()
        self.out[...] = self.add(
            3, 0, slice(None),
            [self.from_pair[1, 0], self.from_far[0], self.from_line[0], self.from_line[1], self.from_line[2]],
        )
        for name, indices in (
            ("core", range(32)), ("x", range(8)), ("y", range(8)), ("fy", range(4)), ("fx", range(4)), ("z", (1, 2, 3)),
        ):
            for i in indices:
                self.copy(name, i).wait_send()


def scatter_scratch(rows, width):
    vmem = lambda *lead: pltpu.VMEM(lead + (rows, width), bf16)
    return [
        vmem(4, 4), vmem(4, 4), vmem(2, 4), vmem(4), vmem(3),
        pltpu.SemaphoreType.DMA((Scatterer.count,)), pltpu.SemaphoreType.DMA((Scatterer.count,)),
    ]


class Summer:
    def __init__(self, me, own, out, held, send, recv):
        self.me, self.own, self.out, self.held, self.send, self.recv = me, own, out, held, send, recv

    def copy(self, i):
        src = self.own if i == 0 else self.held.at[5 + min(i, 3)]
        to = ((0, 0, 1, 0), (0, 1, 0, 0), (1, 0, 0, 0), (0, 0, 0, 1), (0, 0, 0, 2), (0, 0, 0, 3))[i]
        return pltpu.make_async_remote_copy(
            src_ref=src, dst_ref=self.held.at[i], send_sem=self.send.at[i], recv_sem=self.recv.at[i],
            device_id=device(partner(self.me, *to)), device_id_type=MESH,
        )

    def start(self):
        self.copy(0).start()

    def next(self, i):
        self.copy(i - 1).wait_recv()
        before = self.own[...] if i == 1 else self.held[4 + i]
        self.held[5 + i] = before + self.held[i - 1]
        for j in (i,) if i < 3 else (3, 4, 5):
            self.copy(j).start()

    def finish(self):
        for j in (3, 4, 5):
            self.copy(j).wait_recv()
        self.out[...] = (self.held[8] + self.held[3]) + (self.held[4] + self.held[5])
        for j in range(6):
            self.copy(j).wait_send()


AUX = 16


def features(seg_ref, at):
    last = seg_ref.shape[0] - 1
    line = lambda i: jnp.broadcast_to(seg_ref[pl.ds(i, 1), :].astype(f32), (8, Q))
    seg = line(at)
    before = jnp.where(at > 0, line(jnp.maximum(at - 1, 0)), -1.0)
    after = jnp.where(at < last, line(jnp.minimum(at + 1, last)), -1.0)
    lane = lax.broadcasted_iota(jnp.int32, (8, Q), 1)
    earlier = [jnp.where(lane < k, pltpu.roll(before, k, 1), pltpu.roll(seg, k, 1)) == seg for k in (1, 2, 3)]
    later = [
        jnp.where(lane < Q - k, pltpu.roll(seg, Q - k, 1), pltpu.roll(after, Q - k, 1)) == seg for k in (1, 2, 3)
    ]
    edges = [seg == x for x in (seg[:, Q - 1 :], seg[:, :1], before[:, Q - 1 :], after[:, :1])]
    one = lambda mask: jnp.where(mask, 1.0, 0.0)
    lines = [one(m) for m in earlier] + [seg] + [one(m) for m in edges + later]
    row = lax.broadcasted_iota(jnp.int32, (8, Q), 0)
    blocks = []
    for i in range(0, AUX, 8):
        block = jnp.zeros((8, Q), f32)
        for j, x in enumerate(lines[i : i + 8]):
            block = jnp.where(row == j, x, block)
        blocks.append(block)
    return jnp.transpose(jnp.concatenate(blocks + [jnp.zeros((Q - AUX, Q), f32)], axis=0))


def reaches(here, number):
    return dict(collective_id=number, has_side_effects=True) if here else {}


OTHERS_AT = 3
OTHERS_LAG = 4
BEATS = (5, 6, 7, 8, 9, 10, 11, 11, 11)


def front_kernel(
    sizes, here,
    tok_ref, halo_ref, seg_ref, cw_ref, cb_ref, dtb_ref, alog_ref, x2_ref, first_ref, own_ref, gain_in_ref,
    normed_ref, turned_ref, conv_ref, act_ref, low_ref, dsil_ref, dt_ref, cum_ref, dtraw_ref, aux_ref, sb_ref, w_ref, gain_ref,
    full_ref,
    ext_ref, column_ref, state_ref, land_ref, near_ref, side_ref, send_ref, recv_ref, copy_ref,
):
    inner, channels, heads, state = sizes
    step = pl.program_id(0)
    taken = channels + 2 * heads
    if here:
        me = place()
        urgent = Gatherer(me, near_ref, land_ref, send_ref.at[0], recv_ref.at[0])
        others = Gatherer(me, side_ref, full_ref, send_ref.at[1], recv_ref.at[1])
        mine = [
            pltpu.make_async_copy(near_ref, land_ref.at[slot(me)], copy_ref.at[0]),
            pltpu.make_async_copy(side_ref, full_ref.at[slot(me)], copy_ref.at[1]),
        ]

    @pl.when(step == 0)
    def _():
        state_ref[...] = jnp.zeros_like(state_ref)
        if here:
            near_ref[:, :taken] = first_ref[:, inner:]
            gain_in = gain_in_ref[...]
            gain_in = jnp.concatenate([gain_in, jnp.zeros((1, Q - gain_in.shape[1]), f32)], axis=1)
            gain_in = jnp.transpose(jnp.broadcast_to(gain_in, (Q, Q)))
            near_ref[:, taken:] = gain_in[: near_ref.shape[0], 0:1].astype(bf16)
            side_ref[:, :inner] = first_ref[:, :inner]
            side_ref[:, inner:] = own_ref[...]
            greet(me)
            urgent.start()
            mine[0].start()
            for t in range(Gatherer.beats):
                if t == OTHERS_AT:
                    others.start()
                    mine[1].start()
                urgent.beat(t)
                if 0 <= t - OTHERS_LAG < BEATS[0]:
                    others.beat(t - OTHERS_LAG)
            mine[0].wait()
            urgent.finish()
            source = land_ref
        else:
            source = first_ref
        rows = source.shape[1]
        group = 1 if rows % 16 == 0 else 48 // rows
        for j in range(0, source.shape[0], group):
            block = jnp.concatenate([source[j + i].astype(f32) for i in range(group)], axis=0)
            at = slice(j * rows, (j + group) * rows)
            w_ref[at, :] = block[:, :taken].astype(bf16)
            column_ref[at, :] = jnp.broadcast_to(block[:, taken:], (block.shape[0], Q))
        for at in range(0, gain_ref.shape[1], Q):
            gain_ref[:, at : at + Q] = jnp.transpose(column_ref[at : at + Q, :])[0:1, :]

    gain = gain_ref[...]

    def norm(x):
        x = x.astype(f32)
        inv = lax.rsqrt(jnp.mean(x * x, axis=1, keepdims=True) + eps)
        return (x * inv * gain).astype(bf16)

    normed = norm(tok_ref[...])
    normed_ref[...] = normed
    turned_ref[...] = jnp.transpose(normed)
    both = jnp.concatenate([norm(halo_ref[...]), normed], axis=0)
    dt_raw = nn(normed, w_ref[:, channels : channels + 2 * heads])
    dtraw_ref[...] = dt_raw
    aux = features(seg_ref, pl.num_programs(0) - 1 - step)
    aux_ref[...] = aux[:, : aux_ref.shape[1]]
    m1, m2, m3 = aux[:, 0:1], aux[:, 1:2], aux[:, 2:3]
    block = 256
    for at in range(0, channels, block):
        sl = slice(at, at + block)
        ext_ref[:, sl] = nn(both, w_ref[:, at : at + block])
        x0 = ext_ref[HALO : HALO + Q, sl]
        conv_ref[:, sl] = x0
        pre = cb_ref[sl][None, :] + cw_ref[0:1, sl] * x0
        pre += cw_ref[1:2, sl] * (ext_ref[HALO - 1 : HALO - 1 + Q, sl] * m1)
        pre += cw_ref[2:3, sl] * (ext_ref[HALO - 2 : HALO - 2 + Q, sl] * m2)
        pre += cw_ref[3:4, sl] * (ext_ref[HALO - 3 : HALO - 3 + Q, sl] * m3)
        sig = 1.0 / (1.0 + jnp.exp(-pre))
        act = pre * sig
        act_ref[:, sl] = act
        low_ref[:, sl] = act.astype(bf16)
        dsil_ref[:, sl] = sig * (1.0 + pre * (1.0 - sig))
    v = dt_raw + dtb_ref[...]
    dt = jnp.maximum(v, 0.0) + jnp.log1p(jnp.exp(-jnp.abs(v)))
    dt_ref[...] = dt
    rate = -dt * jnp.exp(alog_ref[...])
    row, col = iotas((Q, Q))
    cum = nn_exact((col <= row).astype(bf16), rate)
    cum_ref[...] = cum
    sb_ref[0] = state_ref[...].astype(bf16)
    weight = dt[:, heads:] * jnp.exp(cum[:, heads:] - rate[:, heads:]) * aux[:, 5:6]
    whole = jnp.exp(cum[Q - 1 :, heads:]) * aux[0:1, 7:8]
    scales = split2(jnp.concatenate([weight, jnp.broadcast_to(whole, (8, heads))], axis=0))
    b_bwd = low_ref[:, inner + 2 * state : inner + 3 * state]
    for at in range(0, inner, block):
        sl = slice(at, at + block)
        wide = nn(scales, x2_ref[:, sl])
        vs = (low_ref[:, sl].astype(f32) * wide[:Q]).astype(bf16)
        state_ref[:, sl] = state_ref[:, sl] * wide[Q : Q + 1] + tn(b_bwd, vs)
    if here:
        steps = len(BEATS) - 1
        for i in range(steps):

            @pl.when(step == i)
            def _():
                for t in range(BEATS[i], BEATS[i + 1]):
                    others.beat(t)
                if i == steps - 1:
                    mine[1].wait()
                    others.finish()


def front(tokens, seg, conv_w, conv_b, dt_bias, a_log, x2, first, own, gain, sizes, here):
    inner, channels, heads, state = sizes
    t, d = tokens.shape
    n = t // Q
    rev = lambda i: (n - 1 - i, 0)
    fixed = lambda i: (0, 0)
    blk = lambda width: pl.BlockSpec((Q, width), rev)
    whole = lambda a: pl.BlockSpec(a.shape, lambda i: (0,) * a.ndim)
    anywhere = pl.BlockSpec(memory_space=pl.ANY)
    per = Q // HALO
    out = lambda width, dtype: jax.ShapeDtypeStruct((t, width), dtype)
    taken = channels + 2 * heads
    rows = own.shape[0]
    return pl.pallas_call(
        functools.partial(front_kernel, sizes, here),
        grid=(n,),
        in_specs=[
            blk(d),
            pl.BlockSpec((HALO, d), lambda i: (jnp.maximum((n - 1 - i) * per - 1, 0), 0)),
            whole(seg), whole(conv_w), whole(conv_b), whole(dt_bias), whole(a_log), whole(x2), whole(first), whole(own),
            whole(gain),
        ],
        out_specs=[
            blk(d), pl.BlockSpec((d, Q), lambda i: (0, n - 1 - i)), blk(channels), blk(channels), blk(channels), blk(channels),
            blk(2 * heads), blk(2 * heads), blk(2 * heads), blk(AUX),
            pl.BlockSpec((1, state, inner), lambda i: (n - 1 - i, 0, 0)),
            pl.BlockSpec((d, taken), fixed), pl.BlockSpec((1, d), fixed),
            anywhere,
        ],
        out_shape=[
            out(d, bf16), jax.ShapeDtypeStruct((d, t), bf16),
            out(channels, f32), out(channels, f32), out(channels, bf16), out(channels, f32),
            out(2 * heads, f32), out(2 * heads, f32), out(2 * heads, f32), out(AUX, f32),
            jax.ShapeDtypeStruct((n, state, inner), bf16),
            jax.ShapeDtypeStruct((d, taken), bf16), jax.ShapeDtypeStruct((1, d), f32),
            jax.ShapeDtypeStruct((32, rows, 2 * inner) if here else (1, 8, Q), bf16),
        ],
        scratch_shapes=[
            pltpu.VMEM((HALO + Q, channels), f32),
            pltpu.VMEM((d, Q), f32),
            pltpu.VMEM((state, inner), f32),
            pltpu.VMEM((32, rows, taken + 1) if here else (1, 8, Q), bf16),
            pltpu.VMEM((rows, taken + 1), bf16),
            pltpu.VMEM((rows, 2 * inner), bf16),
            pltpu.SemaphoreType.DMA((2, Gatherer.count)),
            pltpu.SemaphoreType.DMA((2, Gatherer.count)),
            pltpu.SemaphoreType.DMA((2,)),
        ],
        compiler_params=pltpu.CompilerParams(
            dimension_semantics=("arbitrary",), vmem_limit_bytes=60 * 1024 * 1024, **reaches(here, 0)
        ),
        cost_estimate=pl.CostEstimate(flops=5_000_000_000, bytes_accessed=50_000_000, transcendentals=0),
    )(tokens, tokens, seg, conv_w, conv_b, dt_bias, a_log, x2, first, own, gain)


def middle_kernel(
    sizes,
    tok_ref, act_ref, normed_ref, dt_ref, cum_ref, aux_ref, seg_ref, cot_ref, sb_ref, w_ref,
    alog_ref, skip_in_ref, og_ref, x2_ref, r_ref,
    out_ref, turned_ref, nout_ref, dgate_ref, dy_ref, dv_ref, dbc_ref, drate_ref, dq_ref, sf_ref, dog_ref, dsk_ref,
    decay_ref, mix_ref, state_ref, adj_ref, ssm_ref, gated_ref, dno_ref, yf_ref, yb_ref, wide_ref,
    p_ref, q_ref, scal_ref, gate_ref, skip_ref,
):
    inner, channels, heads, state = sizes
    quad = 256
    step = pl.program_id(0)

    @pl.when(step == 0)
    def _():
        state_ref[...] = jnp.zeros_like(state_ref)
        adj_ref[...] = jnp.zeros_like(adj_ref)
        dog_ref[...] = jnp.zeros_like(dog_ref)
        dsk_ref[...] = jnp.zeros_like(dsk_ref)
        q_ref[...] = jnp.zeros_like(q_ref)
        skip_ref[...] = nn(split2(jnp.broadcast_to(skip_in_ref[...], (8, heads))), x2_ref[...])[0:1]

    sf_ref[0] = state_ref[...].astype(bf16)
    aux = aux_ref[...]
    row, col = iotas((Q, Q))
    lower = col < row
    same = aux[:, 3:4] == seg_ref[pl.ds(step, 1), :].astype(f32)
    b_f = act_ref[:, inner : inner + state].astype(bf16)
    c_f = act_ref[:, inner + state : inner + 2 * state].astype(bf16)
    b_b = act_ref[:, inner + 2 * state : inner + 3 * state].astype(bf16)
    c_b = act_ref[:, inner + 3 * state :].astype(bf16)
    g = jnp.where(same & (col != row), jnp.where(lower, nt(c_f, b_f), nt(c_b, b_b)), 0.0)
    dt = dt_ref[...]
    cum = cum_ref[...]
    rate = -dt * jnp.exp(alog_ref[...])
    cf, cb = cum[:, :heads], cum[:, heads:] - rate[:, heads:]
    dtf, dtb = dt[:, :heads], dt[:, heads:]
    total_f, total_b = cum[Q - 1 :, :heads], cum[Q - 1 :, heads:]
    ldt = jnp.log(jnp.maximum(dt, 1e-37))
    rows = jnp.transpose(
        jnp.concatenate(
            [cf - ldt[:, :heads], cb + ldt[:, heads:], jnp.zeros((Q, Q - 2 * heads), f32)], axis=1
        )
    )
    scales = split2(
        jnp.concatenate(
            [
                jnp.exp(cf) * aux[:, 6:7],
                jnp.exp(total_b - cb) * aux[:, 7:8],
                dtf * jnp.exp(total_f - cf) * aux[:, 4:5],
                dtb * jnp.exp(cb) * aux[:, 5:6],
                jnp.broadcast_to(jnp.exp(total_f) * aux[Q - 1 :, 6:7], (8, heads)),
                jnp.broadcast_to(jnp.exp(total_b) * aux[0:1, 7:8], (8, heads)),
            ],
            axis=0,
        )
    )
    lane = lax.broadcasted_iota(jnp.int32, (1, Q), 1)
    first = (lane < Q // 2).astype(bf16)
    second = (lane >= Q // 2).astype(bf16)

    def apart(x):
        return jnp.concatenate([x * first, x * second], axis=0)

    squares = jnp.zeros((Q, quad), f32)
    dots = jnp.zeros((Q, quad), f32)
    cot = cot_ref[...]
    turned_ref[...] = jnp.transpose(cot)
    for at in range(0, inner, quad):
        sl = slice(at, at + quad)
        wide_ref[:, sl] = nn(scales, x2_ref[:, sl])
        v = act_ref[:, sl]
        low = v.astype(bf16)
        yf = nn(c_f, state_ref[:, sl].astype(bf16)) * wide_ref[:Q, sl]
        yb = nn(c_b, sb_ref[0, :, sl]) * wide_ref[Q : 2 * Q, sl]
        yf_ref[:, sl] = yf
        yb_ref[:, sl] = yb
        parts = []
        for half in range(2):
            mixes = []
            for h in (at // 64 + 2 * half, at // 64 + 2 * half + 1):
                gap = jnp.where(
                    lower,
                    cf[:, h : h + 1] - rows[h : h + 1, :],
                    rows[heads + h : heads + h + 1, :] - cb[:, h : h + 1],
                )
                decay = jnp.exp(gap)
                decay_ref[h] = decay
                mix = (g * decay).astype(bf16)
                mix_ref[h * Q : (h + 1) * Q, :] = mix
                mixes.append(mix)
            parts.append(
                nn(jnp.concatenate(mixes, axis=1), apart(low[:, half * Q : (half + 1) * Q]))
            )
        ssm = jnp.concatenate(parts, axis=1) + yf + yb + skip_ref[:, sl] * v
        ssm_ref[:, sl] = ssm
        gate = nn(normed_ref[...], w_ref[:, sl])
        gate_ref[:, sl] = gate
        gated = ssm * (gate / (1.0 + jnp.exp(-gate)))
        gated_ref[:, sl] = gated
        dno = nn(cot, w_ref[:, inner + at : inner + at + quad])
        dno_ref[:, sl] = dno
        squares += gated * gated
        dots += dno * og_ref[sl][None, :] * gated

    inv = lax.rsqrt(jnp.sum(squares, axis=1, keepdims=True) / inner + eps)
    drag = inv * (inv * jnp.sum(dots, axis=1, keepdims=True) / inner)
    dg = jnp.zeros((Q, Q), f32)
    d_cf = jnp.zeros((Q, state), f32)
    d_cb = jnp.zeros((Q, state), f32)
    d_bb = jnp.zeros((Q, state), f32)
    heads_of = jnp.zeros((3 * Q, Q), f32)
    for at in range(0, inner, quad):
        sl = slice(at, at + quad)
        v = act_ref[:, sl]
        low = v.astype(bf16)
        low_f = low.astype(f32)
        ssm, gate, gated, dno = ssm_ref[:, sl], gate_ref[:, sl], gated_ref[:, sl], dno_ref[:, sl]
        og = og_ref[sl][None, :]
        unit = gated * inv
        nout_ref[:, sl] = (unit * og).astype(bf16)
        dog_ref[:, sl] += jnp.sum(dno * unit, axis=0, keepdims=True)
        d_gated = inv * (dno * og) - gated * (inv * drag)
        sig = 1.0 / (1.0 + jnp.exp(-gate))
        d_ssm = d_gated * (gate * sig)
        dgate_ref[:, sl] = (d_gated * ssm * (sig * (1.0 + gate * (1.0 - sig)))).astype(bf16)
        dsk_ref[:, sl] += jnp.sum(d_ssm * v, axis=0, keepdims=True)
        dy = d_ssm.astype(bf16)
        dy_ref[:, sl] = dy
        dy_f = dy.astype(f32)
        parts = []
        for half in range(2):
            h0 = at // 64 + 2 * half
            cut = slice(half * Q, (half + 1) * Q)
            d_mix = nt(dy[:, cut], apart(low[:, cut]))
            for i in range(2):
                h = h0 + i
                x = d_mix[:, i * Q : (i + 1) * Q] * decay_ref[h]
                dg += x
                full = x * g
                under = jnp.where(lower, full, 0.0)
                over = full - under
                q_ref[h : h + 1, :] = jnp.sum(under, axis=0, keepdims=True)
                q_ref[heads + h : heads + h + 1, :] = jnp.sum(over, axis=0, keepdims=True)
                p_ref[:, h : h + 1] = jnp.sum(under, axis=1, keepdims=True)
                p_ref[:, heads + h : heads + h + 1] = jnp.sum(over, axis=1, keepdims=True)
            parts.append(tn(mix_ref[h0 * Q : (h0 + 2) * Q, :], apart(dy[:, cut])))
        adj = adj_ref[:, sl]
        adj_low = adj.astype(bf16)
        sf_low = state_ref[:, sl].astype(bf16)
        sb_low = sb_ref[0, :, sl]
        wide_wb = wide_ref[3 * Q : 4 * Q, sl]
        dvb = wide_wb * nn(b_b, adj_low)
        dv_ref[:, sl] = d_ssm * skip_ref[:, sl] + jnp.concatenate(parts, axis=1) + dvb
        prods = jnp.concatenate(
            [
                (dy_f * yf_ref[:, sl]).astype(bf16),
                (dy_f * yb_ref[:, sl]).astype(bf16),
                (low_f * dvb).astype(bf16),
            ],
            axis=0,
        )
        heads_of += nn(prods, r_ref[sl, :])
        dye_f = (dy_f * wide_ref[:Q, sl]).astype(bf16)
        dye_b = (dy_f * wide_ref[Q : 2 * Q, sl]).astype(bf16)
        vs_f = (low_f * wide_ref[2 * Q : 3 * Q, sl]).astype(bf16)
        vs_b = (low_f * wide_wb).astype(bf16)
        d_cf += nt(dye_f, sf_low)
        d_cb += nt(dye_b, sb_low)
        d_bb += nt(vs_b, adj_low)
        across_b = wide_ref[4 * Q + 8 : 4 * Q + 9, sl]
        scal_ref[:, sl] = jnp.sum(adj * sb_low.astype(f32), axis=0, keepdims=True) * across_b
        adj_ref[:, sl] = adj * across_b + tn(c_b, dye_b)
        state_ref[:, sl] = state_ref[:, sl] * wide_ref[4 * Q : 4 * Q + 1, sl] + tn(b_f, vs_f)

    out_ref[...] = (tok_ref[...].astype(f32) + nt(nout_ref[...], w_ref[:, inner:])).astype(bf16)
    dg = jnp.where(same & (col != row), dg, 0.0)
    dg_f = jnp.where(lower, dg, 0.0)
    dg_b = (dg - dg_f).astype(bf16)
    dg_f = dg_f.astype(bf16)
    dbc_ref[...] = jnp.concatenate(
        [tn(dg_f, c_f), d_cf + nn(dg_f, b_f), d_bb + tn(dg_b, c_b), d_cb + nn(dg_b, b_b)], axis=1
    )
    q_cols = jnp.transpose(q_ref[...])[:, : 2 * heads]
    dots_f, dots_b, dots_v = heads_of[:Q, :heads], heads_of[Q : 2 * Q, :heads], heads_of[2 * Q :, :heads]
    through = nn(split_rows(jnp.broadcast_to(scal_ref[...], (8, inner))), r_ref[...])
    through = (through[0:1] + through[8:9])[:, :heads]
    diff = p_ref[:, : 2 * heads] - q_cols
    d_rate_f = nn_exact((col >= row).astype(bf16), diff[:, :heads] + dots_f)
    d_rate_b = (
        nn_exact((col <= row).astype(bf16), diff[:, heads:] + dots_b)
        + nn_exact((col > row).astype(bf16), dots_v)
        + through
    )
    drate_ref[...] = jnp.concatenate([d_rate_f, d_rate_b], axis=1)
    dq_ref[...] = jnp.concatenate([q_cols[:, :heads], q_cols[:, heads:] + dots_v], axis=1)


def middle(tokens, act, normed, dt, cum, aux, seg, cot, sb, w_side, a_log, skip, og, x2, r, sizes):
    inner, channels, heads, state = sizes
    t, d = tokens.shape
    n = t // Q
    fwd = lambda i: (i, 0)
    fixed = lambda i: (0, 0)
    cube = lambda i: (i, 0, 0)
    blk = lambda width: pl.BlockSpec((Q, width), fwd)
    whole = lambda a: pl.BlockSpec(a.shape, fixed)
    out = lambda width, dtype: jax.ShapeDtypeStruct((t, width), dtype)
    line = jax.ShapeDtypeStruct((1, inner), f32)
    return pl.pallas_call(
        functools.partial(middle_kernel, sizes),
        grid=(n,),
        in_specs=[
            blk(d), blk(channels), blk(d), blk(2 * heads), blk(2 * heads), blk(aux.shape[1]),
            whole(seg), blk(d), pl.BlockSpec((1, state, inner), cube),
            whole(w_side), whole(a_log), whole(skip), pl.BlockSpec(og.shape, lambda i: (0,)), whole(x2), whole(r),
        ],
        out_specs=[
            blk(d), pl.BlockSpec((d, Q), lambda i: (0, i)), blk(inner), blk(inner), blk(inner), blk(inner), blk(4 * state),
            blk(2 * heads), blk(2 * heads), pl.BlockSpec((1, state, inner), cube),
            pl.BlockSpec((1, inner), fixed), pl.BlockSpec((1, inner), fixed),
        ],
        out_shape=[
            out(d, bf16), jax.ShapeDtypeStruct((d, t), bf16),
            out(inner, bf16), out(inner, bf16), out(inner, bf16), out(inner, f32),
            out(4 * state, f32), out(2 * heads, f32), out(2 * heads, f32),
            jax.ShapeDtypeStruct((n, state, inner), bf16), line, line,
        ],
        scratch_shapes=[
            pltpu.VMEM((heads, Q, Q), f32),
            pltpu.VMEM((heads * Q, Q), bf16),
            pltpu.VMEM((state, inner), f32),
            pltpu.VMEM((state, inner), f32),
            pltpu.VMEM((Q, inner), f32),
            pltpu.VMEM((Q, inner), f32),
            pltpu.VMEM((Q, inner), f32),
            pltpu.VMEM((Q, inner), f32),
            pltpu.VMEM((Q, inner), f32),
            pltpu.VMEM((4 * Q + 16, inner), f32),
            pltpu.VMEM((Q, Q), f32),
            pltpu.VMEM((Q, Q), f32),
            pltpu.VMEM((1, inner), f32),
            pltpu.VMEM((Q, inner), f32),
            pltpu.VMEM((1, inner), f32),
        ],
        compiler_params=pltpu.CompilerParams(
            dimension_semantics=("arbitrary",), vmem_limit_bytes=60 * 1024 * 1024
        ),
        cost_estimate=pl.CostEstimate(flops=30_000_000_000, bytes_accessed=60_000_000, transcendentals=0),
    )(tokens, act, normed, dt, cum, aux, seg, cot, sb, w_side, a_log, skip, og, x2, r)


def side_kernel(half, a_ref, b_ref, u_ref, v_ref, out_ref):
    step = pl.program_id(0)

    @pl.when(step < half)
    def _():
        out_ref[...] = nn(a_ref[...], u_ref[...]).astype(bf16)

    @pl.when(step >= half)
    def _():
        out_ref[...] = nn(b_ref[...], v_ref[...]).astype(bf16)


def side(a, b, u, v):
    d, t = a.shape
    block = 768
    half = u.shape[1] // block
    fixed = lambda i: (0, 0)
    return pl.pallas_call(
        functools.partial(side_kernel, half),
        grid=(2 * half,),
        in_specs=[
            pl.BlockSpec((d, t), fixed), pl.BlockSpec((d, t), fixed),
            pl.BlockSpec((t, block), lambda i: (0, jnp.minimum(i, half - 1))),
            pl.BlockSpec((t, block), lambda i: (0, jnp.maximum(i - half, 0))),
        ],
        out_specs=pl.BlockSpec((d, block), lambda i: (0, i)),
        out_shape=jax.ShapeDtypeStruct((d, 2 * u.shape[1]), bf16),
        compiler_params=pltpu.CompilerParams(
            dimension_semantics=("arbitrary",), vmem_limit_bytes=60 * 1024 * 1024
        ),
        cost_estimate=pl.CostEstimate(flops=4 * d * t * u.shape[1], bytes_accessed=14_000_000, transcendentals=0),
    )(a, b, u, v)


def back_kernel(
    sizes, here,
    side_ref, cw_ref, dtb_ref, alog_ref, aux_ref, x2_ref, r_ref,
    low_ref, dsil_ref, conv_ref, dt_ref, cum_ref, dtraw_ref,
    dgate_ref, dy_ref, dv_ref, dbc_ref, drate_ref, dq_ref, sf_ref, dog_ref, dsk_ref, part_ref,
    dproj_ref, dnorm_ref, small_ref, sum_ref,
    adj_ref, dpre_ref, scal_ref, *exchange,
):
    inner, channels, heads, state = sizes
    quad = 256
    step = pl.program_id(0)

    @pl.when(step == 0)
    def _():
        adj_ref[...] = jnp.zeros_like(adj_ref)
        dpre_ref[...] = jnp.zeros_like(dpre_ref)
        small_ref[...] = jnp.zeros_like(small_ref)
        small_ref[5:6, :inner] = dog_ref[...]
        skips = nn(split_rows(jnp.broadcast_to(dsk_ref[...], (8, inner))), r_ref[...])
        small_ref[6:7, SKIP_AT : SKIP_AT + Q] = skips[0:1] + skips[8:9]

    if here:
        me = place()
        sums = Scatterer(me, part_ref, sum_ref, *exchange)

        @pl.when(step == 0)
        def _():
            greet_all(me)
            sums.start()

    dnorm_ref[...] = nt(dgate_ref[...], side_ref[...])
    dpre_ref[Q:, :] = dpre_ref[0:8, :]
    aux = aux_ref[...]
    dt = dt_ref[...]
    cum = cum_ref[...]
    cf, dtf = cum[:, :heads], dt[:, :heads]
    total_f = cf[Q - 1 :, :]
    scales = split2(
        jnp.concatenate(
            [
                jnp.exp(cf) * aux[:, 6:7],
                dtf * jnp.exp(total_f - cf) * aux[:, 4:5],
                jnp.broadcast_to(jnp.exp(total_f) * aux[Q - 1 :, 6:7], (8, heads)),
            ],
            axis=0,
        )
    )
    b_f = low_ref[:, inner : inner + state]
    c_f = low_ref[:, inner + state : inner + 2 * state]
    dots = jnp.zeros((Q, Q), f32)
    d_bf = jnp.zeros((Q, state), f32)
    for at in range(0, inner, quad):
        sl = slice(at, at + quad)
        wide = nn(scales, x2_ref[:, sl])
        low_f = low_ref[:, sl].astype(f32)
        adj = adj_ref[:, sl]
        adj_low = adj.astype(bf16)
        wide_wf = wide[Q : 2 * Q]
        dvf = wide_wf * nn(b_f, adj_low)
        dots += nn((low_f * dvf).astype(bf16), r_ref[sl, :])
        d_bf += nt((low_f * wide_wf).astype(bf16), adj_low)
        across = wide[2 * Q : 2 * Q + 1]
        scal_ref[:, sl] = jnp.sum(adj * sf_ref[0, :, sl].astype(f32), axis=0, keepdims=True) * across
        dye = (dy_ref[:, sl].astype(f32) * wide[:Q]).astype(bf16)
        adj_ref[:, sl] = adj * across + tn(c_f, dye)
        dpre_ref[:Q, sl] = (dv_ref[:, sl] + dvf) * dsil_ref[:, sl]
    d_bc = dbc_ref[...] + jnp.concatenate([d_bf, jnp.zeros((Q, 3 * state), f32)], axis=1)
    dpre_ref[:Q, inner:] = d_bc * dsil_ref[:, inner:]

    n1, n2, n3 = aux[:, 8:9], aux[:, 9:10], aux[:, 10:11]
    for at in range(0, channels, quad):
        sl = slice(at, at + quad)
        conv = conv_ref[:, sl]
        z = dpre_ref[:Q, sl]
        small_ref[4:5, sl] += jnp.sum(z, axis=0, keepdims=True)
        small_ref[0:1, sl] += jnp.sum(z * conv, axis=0, keepdims=True)
        total = cw_ref[0:1, sl] * z
        for k, mask in ((1, n1), (2, n2), (3, n3)):
            z = dpre_ref[k : Q + k, sl] * mask
            small_ref[k : k + 1, sl] += jnp.sum(z * conv, axis=0, keepdims=True)
            total += cw_ref[k : k + 1, sl] * z
        dproj_ref[:, at : at + quad] = total.astype(bf16)

    row, col = iotas((Q, Q))
    through = nn(split_rows(jnp.broadcast_to(scal_ref[...], (8, inner))), r_ref[...])
    through = (through[0:1] + through[8:9])[:, :heads]
    dots = dots[:, :heads]
    extra = nn_exact((col < row).astype(bf16), dots) + through
    none = jnp.zeros((Q, heads), f32)
    d_rate = drate_ref[...] + jnp.concatenate([extra, none], axis=1)
    d_dt = dq_ref[...] + jnp.concatenate([dots, none], axis=1)
    d_dt = jnp.where(dt > 0.0, d_dt / jnp.maximum(dt, 1e-37), 0.0)
    a = jnp.exp(alog_ref[...])
    v = dtraw_ref[...] + dtb_ref[...]
    d_v = (d_dt - d_rate * a) / (1.0 + jnp.exp(-v))
    small_ref[6:7, BIAS_AT : BIAS_AT + 2 * heads] += jnp.sum(d_v, axis=0, keepdims=True)
    small_ref[6:7, LOG_AT : LOG_AT + 2 * heads] += jnp.sum(d_rate * (-dt * a), axis=0, keepdims=True)
    dproj_ref[:, channels:] = d_v.astype(bf16)
    if here:
        for i, acts in enumerate(SUM_BEATS):

            @pl.when(step == i)
            def _():
                for name, *index in acts:
                    getattr(sums, name)(*index)


SUM_BEATS = (
    (("pair", 3),),
    (("pair", 2), ("far", 3)),
    (("pair", 1), ("far", 2), ("line", 3)),
    (("pair", 0), ("far", 1), ("line", 2)),
    (("far", 0), ("line", 1)),
    (),
    (("line", 0),),
    (("finish",),),
)


def back(
    w_side, conv_w, dt_bias, rate_row, aux, x2, r, low, dsil, conv, dt, cum, dtraw,
    dgate, dy, dv, dbc, drate, dq, sf, dog, dsk, part, sizes, here,
):
    inner, channels, heads, state = sizes
    t, d = low.shape[0], w_side.shape[0]
    n = t // Q
    taken = channels + 2 * heads
    rev = lambda i: (n - 1 - i, 0)
    fixed = lambda i: (0, 0)
    blk = lambda a: pl.BlockSpec((Q, a.shape[1]), rev)
    whole = lambda a: pl.BlockSpec(a.shape, fixed)
    summed = part.shape[1:]
    return pl.pallas_call(
        functools.partial(back_kernel, sizes, here),
        grid=(n,),
        in_specs=[
            pl.BlockSpec((d, inner), fixed), whole(conv_w), whole(dt_bias), whole(rate_row),
            blk(aux), whole(x2), whole(r), blk(low), blk(dsil), blk(conv), blk(dt), blk(cum), blk(dtraw),
            blk(dgate), blk(dy), blk(dv), blk(dbc), blk(drate), blk(dq),
            pl.BlockSpec((1, state, inner), lambda i: (n - 1 - i, 0, 0)), whole(dog), whole(dsk),
            pl.BlockSpec(memory_space=pl.ANY),
        ],
        out_specs=[
            pl.BlockSpec((Q, taken), rev), pl.BlockSpec((Q, d), rev), pl.BlockSpec((8, channels), fixed),
            pl.BlockSpec(summed, fixed),
        ],
        out_shape=[
            jax.ShapeDtypeStruct((t, taken), bf16),
            jax.ShapeDtypeStruct((t, d), f32),
            jax.ShapeDtypeStruct((8, channels), f32),
            jax.ShapeDtypeStruct(summed, f32),
        ],
        scratch_shapes=[
            pltpu.VMEM((state, inner), f32),
            pltpu.VMEM((Q + 8, channels), f32),
            pltpu.VMEM((1, inner), f32),
        ]
        + (scatter_scratch(*summed) + [pltpu.SemaphoreType.DMA((16,))] if here else []),
        compiler_params=pltpu.CompilerParams(
            dimension_semantics=("arbitrary",), vmem_limit_bytes=60 * 1024 * 1024, **reaches(here, 1)
        ),
        cost_estimate=pl.CostEstimate(flops=20_000_000_000, bytes_accessed=60_000_000, transcendentals=0),
    )(
        w_side, conv_w, dt_bias, rate_row, aux, x2, r, low, dsil, conv, dt, cum, dtraw,
        dgate, dy, dv, dbc, drate, dq, sf, dog, dsk, part,
    )


def tail_kernel(
    here,
    turned_ref, dproj_ref, w_ref, dnorm_ref, tok_ref, cot_ref, gain_ref, small_ref,
    dtok_ref, sum_ref, total_ref,
    own_ref, *exchange,
):
    step = pl.program_id(0)
    last = pl.num_programs(0) - 1
    d = tok_ref.shape[1]
    if here:
        me = place()
        part_ref, *rest = exchange
        sums = Scatterer(me, part_ref, sum_ref, *rest[:7])
        tiny = Summer(me, own_ref, total_ref, *rest[7:])

    @pl.when(step == 0)
    def _():
        own_ref[...] = small_ref[...]
        if here:
            greet_all(me)
            for half, cols in enumerate((sums.left, sums.right)):
                block = nn(turned_ref[...], dproj_ref[:, cols])
                part_ref[:, :, cols] = block.reshape(part_ref.shape[:2] + block.shape[1:]).astype(bf16)
                sums.start(half)

    rows = pl.ds(pl.multiple_of(step * TAIL, TAIL), TAIL)
    d_normed = dnorm_ref[...] + nt(dproj_ref[rows, :], w_ref[...])
    x = tok_ref[...].astype(f32)
    inv = lax.rsqrt(jnp.mean(x * x, axis=1, keepdims=True) + eps)
    unit = x * inv
    own_ref[6:7, :d] += jnp.sum(d_normed * unit, axis=0, keepdims=True)
    a = d_normed * gain_ref[...]
    dtok_ref[...] = cot_ref[...].astype(f32) + inv * (a - unit * jnp.mean(a * unit, axis=1, keepdims=True))
    if here:
        for i, acts in enumerate(TAIL_BEATS):

            @pl.when(step == i)
            def _():
                for name, *index in acts:
                    getattr(tiny if name in ("first", "next") else sums, "start" if name == "first" else name)(*index)
                if i == len(TAIL_BEATS) - 1:
                    tiny.finish()
    else:

        @pl.when(step == last)
        def _():
            total_ref[...] = own_ref[...]


TAIL = 256
TAIL_BEATS = (
    (("pair", 3),),
    (("pair", 2), ("far", 3)),
    (("pair", 1), ("far", 2), ("line", 3)),
    (
        ("first",), ("pair", 0), ("far", 1), ("line", 2), ("next", 1), ("far", 0), ("line", 1), ("next", 2), ("line", 0),
        ("next", 3), ("finish",),
    ),
)


def tail(turned, dproj, w_first, dnorm, tokens, cot, gain_row, small, rows, here):
    d, t = turned.shape
    n = t // TAIL
    taken = dproj.shape[1]
    fwd = lambda i: (i, 0)
    fixed = lambda i: (0, 0)
    blk = pl.BlockSpec((TAIL, d), fwd)
    whole = lambda a: pl.BlockSpec(a.shape, fixed)
    exchange = []
    if here:
        exchange = [pltpu.VMEM((d // rows, rows, taken), bf16)] + scatter_scratch(rows, taken)
        exchange += [
            pltpu.VMEM((9,) + small.shape, f32), pltpu.SemaphoreType.DMA((6,)), pltpu.SemaphoreType.DMA((6,)),
        ]
    return pl.pallas_call(
        functools.partial(tail_kernel, here),
        grid=(n,),
        in_specs=[whole(turned), whole(dproj), whole(w_first), blk, blk, blk, whole(gain_row), whole(small)],
        out_specs=[blk, pl.BlockSpec((rows, taken), fixed), whole(small)],
        out_shape=[
            jax.ShapeDtypeStruct((t, d), f32),
            jax.ShapeDtypeStruct((rows, taken), f32),
            jax.ShapeDtypeStruct(small.shape, f32),
        ],
        scratch_shapes=[pltpu.VMEM(small.shape, f32)] + exchange,
        compiler_params=pltpu.CompilerParams(
            dimension_semantics=("arbitrary",), vmem_limit_bytes=60 * 1024 * 1024, **reaches(here, 2)
        ),
        cost_estimate=pl.CostEstimate(flops=10_000_000_000, bytes_accessed=30_000_000, transcendentals=0),
    )(turned, dproj, w_first, dnorm, tokens, cot, gain_row, small)


def unpack(small, taps, inner, heads, d):
    return small[6, :d], (
        small[:taps],
        small[taps],
        small[6, BIAS_AT : BIAS_AT + 2 * heads],
        small[6, LOG_AT : LOG_AT + 2 * heads],
        small[6, SKIP_AT : SKIP_AT + heads],
        small[5, :inner],
    )


def finish_kernel(
    sizes, side_ref, first_ref, small_ref,
    din_ref, dout_ref, dgain_ref, dcw_ref, dcb_ref, ddtb_ref, dalog_ref, dsk_ref, dog_ref,
):
    inner, channels, heads, rows = sizes
    din_ref[:, :inner] = side_ref[:, :inner]
    din_ref[:, inner:] = first_ref[...]
    dout_ref[...] = side_ref[:, inner:]
    taps = dcw_ref.shape[0]
    dcw_ref[...] = small_ref[:taps, :]
    dcb_ref[...] = small_ref[taps, :]
    dog_ref[...] = small_ref[5, :inner]
    ddtb_ref[...] = small_ref[6:7, BIAS_AT : BIAS_AT + 2 * heads]
    dalog_ref[...] = small_ref[6:7, LOG_AT : LOG_AT + 2 * heads]
    dsk_ref[...] = small_ref[6:7, SKIP_AT : SKIP_AT + heads]
    d = BIAS_AT
    row, col = iotas((d, Q))
    own = (row == col + slot(place()) * rows) & (col < rows)
    parts = jnp.broadcast_to(small_ref[6:7, :d], (8, d))
    hi = parts.astype(bf16)
    mid = (parts - hi.astype(f32)).astype(bf16)
    lo = (parts - hi.astype(f32) - mid.astype(f32)).astype(bf16)
    pick = jnp.where(own, 1.0, 0.0).astype(bf16)
    dgain_ref[...] = (nn(hi, pick) + nn(mid, pick) + nn(lo, pick))[0:1, :rows]


def finish(sides, firsts, small, taps, sizes):
    inner, channels, heads, rows = sizes
    shapes = [
        (rows, inner + firsts.shape[1]), (rows, inner), (1, rows), (taps, channels), (channels,), (1, 2 * heads),
        (1, 2 * heads), (1, heads), (inner,),
    ]
    return pl.pallas_call(
        functools.partial(finish_kernel, sizes),
        out_shape=[jax.ShapeDtypeStruct(shape, f32) for shape in shapes],
    )(sides, firsts, small)


def body(here, tokens, segment_ids, w_in, w_out, norm_gain, conv_w, conv_b, dt_bias, a_log, d_skip, out_gain, cotangent):
    rows = w_in.shape[0]
    d, inner, heads = tokens.shape[1], out_gain.shape[0], d_skip.shape[0]
    parts = d // rows
    channels = conv_w.shape[1]
    state = (channels - inner) // 4
    width = inner // heads
    sizes = (inner, channels, heads, state)
    seg = segment_ids.reshape(-1, Q)
    spread = np.arange(inner)[None, :] // width == np.arange(heads)[:, None]
    x2 = jnp.asarray(np.concatenate([spread, spread], axis=0), bf16)
    r = jnp.asarray(np.pad(spread.T, ((0, 0), (0, Q - heads))), bf16)
    first, own = w_in, w_out.T
    if not here:
        first = lax.all_gather(jnp.concatenate([w_in[:, inner:], norm_gain[:, None]], axis=1), AXES)
    alog_row, dtb_row = a_log[None, :], dt_bias[None, :]
    normed, turned, conv, act, low, dsil, dt, cum, dtraw, aux, sb, w_first, gain_row, w_side = front(
        tokens, seg, conv_w, conv_b, dtb_row, alog_row, x2, first, own, norm_gain.astype(f32)[None, :], sizes, here
    )
    if not here:
        w_side = lax.all_gather(jnp.concatenate([w_in[:, :inner], own], axis=1), AXES)
    w_side = w_side.reshape(d, 2 * inner)
    output, cot_turned, nout, dgate, dy, dv, dbc, drate, dq, sf, d_og, d_sk = middle(
        tokens, act, normed, dt, cum, aux, seg, cotangent, sb, w_side, alog_row, d_skip[None, :], out_gain, x2, r, sizes,
    )
    if here:
        g_side = side(turned, cot_turned, dgate, nout)
    else:
        g_side = jnp.concatenate([nn(turned, dgate), nn(cot_turned, nout)], axis=1)
    g_side = g_side.reshape(parts, rows, 2 * inner)
    dproj, dnorm, small, sides = back(
        w_side, conv_w, dtb_row, alog_row, aux, x2, r, low, dsil, conv, dt, cum, dtraw,
        dgate, dy, dv, dbc, drate, dq, sf, d_og, d_sk, g_side, sizes, here,
    )
    d_tokens, firsts, small = tail(turned, dproj, w_first, dnorm, tokens, cotangent, gain_row, small, rows, here)
    if here:
        d_w_in, d_w_out, d_gain, *small = finish(sides, firsts, small, conv_w.shape[0], (inner, channels, heads, rows))
        d_gain = d_gain[0]
        small = tuple(a[0] if a.ndim == 2 and a.shape[0] == 1 else a for a in small)
    else:
        g_first = nn(turned, dproj).reshape(parts, rows, dproj.shape[1])
        firsts = lax.psum_scatter(g_first, AXES, scatter_dimension=0)
        sides = lax.psum_scatter(g_side, AXES, scatter_dimension=0)
        d_w_in, d_w_out = jnp.concatenate([sides[:, :inner], firsts], axis=1), sides[:, inner:]
        d_gain, small = unpack(lax.psum(small, AXES), conv_w.shape[0], inner, heads, d)
        d_gain = lax.dynamic_slice_in_dim(d_gain, lax.axis_index(AXES) * rows, rows)
    return (output, d_tokens, d_w_in, d_w_out.T, d_gain) + small


def solution(mesh):
    rows, cols, line, none = P(AXES, None), P(None, AXES), P(AXES), P()
    here = dict(mesh.shape) == {"fsdp": 8, "rep": 4}
    return jax.shard_map(
        functools.partial(body, here),
        mesh=mesh,
        in_specs=(rows, line, rows, cols, line, none, none, none, none, none, none, rows),
        out_specs=(rows, rows, rows, cols, line, none, none, none, none, none, none),
        check_vma=False,
    )
```

```python
import functools

import jax
import jax.numpy as jnp
import numpy as np
from jax import lax
from jax.experimental import pallas as pl
from jax.experimental.pallas import tpu as pltpu
from jax.sharding import PartitionSpec as P

eps = 1e-05
Q = 128
HALO = 16
f32 = jnp.float32
bf16 = jnp.bfloat16
AXES = ("fsdp", "rep")
BIAS_AT, LOG_AT, SKIP_AT = 768, 896, 1024


def nn(a, b):
    return lax.dot_general(a, b, (((1,), (0,)), ((), ())), preferred_element_type=f32)


def nt(a, b):
    return lax.dot_general(a, b, (((1,), (1,)), ((), ())), preferred_element_type=f32)


def tn(a, b):
    return lax.dot_general(a, b, (((0,), (0,)), ((), ())), preferred_element_type=f32)


def split2(x):
    hi = x.astype(bf16)
    lo = (x - hi.astype(f32)).astype(bf16)
    return jnp.concatenate([hi, lo], axis=1)


def split_rows(x):
    hi = x.astype(bf16)
    return jnp.concatenate([hi, (x - hi.astype(f32)).astype(bf16)], axis=0)


def nn_exact(ones_mask, x):
    hi = x.astype(bf16)
    r = x - hi.astype(f32)
    mid = r.astype(bf16)
    lo = (r - mid.astype(f32)).astype(bf16)
    return nn(ones_mask, hi) + (nn(ones_mask, mid) + nn(ones_mask, lo))


def iotas(shape):
    return (
        lax.broadcasted_iota(jnp.int32, shape, 0),
        lax.broadcasted_iota(jnp.int32, shape, 1),
    )


MESH = pl.DeviceIdType.MESH
LINE = 4
STEPS = (0, -1, 1, -2, 2, -3, 3)
LAG = 2


def place():
    f = lax.axis_index("fsdp")
    return f // 4, (f // 2) % 2, f % 2, lax.axis_index("rep")


def flip(at, dy, dx, dc, dz):
    y, x, c, z = at
    return (1 - y if dy else y, 1 - x if dx else x, 1 - c if dc else c, z + dz)


def device(at):
    y, x, c, z = at
    return ((y * 2 + x) * 2 + c, z)


def slot(at):
    y, x, c, z = at
    return ((y * 2 + x) * 2 + c) * LINE + z


def on_line(me, dz):
    z = me[3]
    return z >= -dz if dz < 0 else z < LINE - dz


def when(condition, act):
    if condition is True:
        act()
    else:
        pl.when(condition)(act)


def greet(me):
    barrier = pltpu.get_barrier_semaphore()
    for other in ((0, 0, 1, 0), (0, 1, 0, 0), (1, 0, 0, 0)):
        pl.semaphore_signal(barrier, inc=1, device_id=device(flip(me, *other)), device_id_type=MESH)
    for dz in (-1, 1):

        @pl.when(on_line(me, dz))
        def _():
            pl.semaphore_signal(barrier, inc=1, device_id=device(flip(me, 0, 0, 0, dz)), device_id_type=MESH)

    inside = jnp.where((me[3] > 0) & (me[3] < LINE - 1), 1, 0)
    pl.semaphore_wait(barrier, 4 + inside)


def halves(width):
    cut = (width // 2 + 127) // 128 * 128
    return slice(0, cut), slice(cut, width)


class Gatherer:
    kinds = ("z", "x", "y", "c", "left", "right", "cx", "cy", "cl", "cr")
    count = len(kinds) * len(STEPS)

    def __init__(self, me, own, full, send, recv):
        self.me, self.own, self.full, self.send, self.recv = me, own, full, send, recv
        self.left, self.right = halves(full.shape[2])

    def made(self, kind, dz, block, to, cols=None):
        i = self.kinds.index(kind) * len(STEPS) + STEPS.index(dz)
        at = slot(flip(self.me, *block))
        dst = self.full.at[at] if cols is None else self.full.at[at, :, cols]
        src = dst
        if block == (0, 0, 0, 0):
            src = self.own if cols is None else self.own.at[:, cols]
        return pltpu.make_async_remote_copy(
            src_ref=src, dst_ref=dst, send_sem=self.send.at[i], recv_sem=self.recv.at[i],
            device_id=device(flip(self.me, *to)), device_id_type=MESH,
        )

    def copy(self, kind, dz):
        return {
            "x": lambda: self.made("x", dz, (0, 0, 0, dz), (0, 1, 0, 0)),
            "y": lambda: self.made("y", dz, (0, 0, 0, dz), (1, 0, 0, 0)),
            "c": lambda: self.made("c", dz, (0, 0, 0, dz), (0, 0, 1, 0)),
            "left": lambda: self.made("left", dz, (0, 1, 0, dz), (1, 0, 0, 0), self.left),
            "right": lambda: self.made("right", dz, (1, 0, 0, dz), (0, 1, 0, 0), self.right),
            "cx": lambda: self.made("cx", dz, (0, 1, 0, dz), (0, 0, 1, 0)),
            "cy": lambda: self.made("cy", dz, (1, 0, 0, dz), (0, 0, 1, 0)),
            "cl": lambda: self.made("cl", dz, (1, 1, 0, dz), (0, 0, 1, 0), self.left),
            "cr": lambda: self.made("cr", dz, (1, 1, 0, dz), (0, 0, 1, 0), self.right),
        }[kind]()

    def along(self, dz, way):
        i = self.kinds.index("z") * len(STEPS) + STEPS.index(dz - way)
        at = slot(flip(self.me, 0, 0, 0, dz))
        return pltpu.make_async_remote_copy(
            src_ref=self.full.at[at] if dz else self.own, dst_ref=self.full.at[at],
            send_sem=self.send.at[i], recv_sem=self.recv.at[i],
            device_id=device(flip(self.me, 0, 0, 0, way)), device_id_type=MESH,
        )

    def sent_along(self):
        for dz in STEPS:
            for way in (-1, 1):
                if dz * way <= 0 and abs(dz - way) < LINE:
                    yield dz, way, on_line(self.me, way) & (True if dz == 0 else on_line(self.me, dz))

    def each(self, act):
        for dz in STEPS:
            when(True if dz == 0 else on_line(self.me, dz), functools.partial(act, dz))

    def start(self):
        for dz, way, ok in self.sent_along():
            if dz == 0:
                when(ok, lambda dz=dz, way=way: self.along(dz, way).start())
        self.spread(0)

    def spread(self, dz):
        for kind in ("x", "y", "c"):
            self.copy(kind, dz).start()

    def column(self, dz):
        if dz == 0:
            return
        way = -1 if dz > 0 else 1
        self.along_arrived(dz)
        if abs(dz) < LINE - 1:
            when(on_line(self.me, way), lambda: self.along(dz, way).start())
        self.spread(dz)

    def along_arrived(self, dz):
        i = self.kinds.index("z") * len(STEPS) + STEPS.index(dz)
        ref = self.full.at[slot(flip(self.me, 0, 0, 0, dz))]
        pltpu.make_async_remote_copy(
            src_ref=ref, dst_ref=ref, send_sem=self.send.at[i], recv_sem=self.recv.at[i],
            device_id=device(flip(self.me, 0, 0, 0, 1 if dz > 0 else -1)), device_id_type=MESH,
        ).wait_recv()

    def corner(self, dz):
        self.copy("x", dz).wait_recv()
        self.copy("left", dz).start()
        self.copy("cx", dz).start()
        self.copy("y", dz).wait_recv()
        self.copy("right", dz).start()
        self.copy("cy", dz).start()

    def last(self, dz):
        self.copy("left", dz).wait_recv()
        self.copy("cl", dz).start()
        self.copy("right", dz).wait_recv()
        self.copy("cr", dz).start()

    def beat(self, t):
        for lag, act in ((0, self.column), (LAG, self.corner), (2 * LAG, self.last)):
            if 0 <= t - lag < len(STEPS):
                dz = STEPS[t - lag]
                when(True if dz == 0 else on_line(self.me, dz), functools.partial(act, dz))

    beats = len(STEPS) + 2 * LAG

    def finish(self):
        def act(dz):
            for kind in ("c", "cx", "cy", "cl", "cr"):
                self.copy(kind, dz).wait_recv()
            for kind in self.kinds[1:]:
                self.copy(kind, dz).wait_send()

        self.each(act)
        for dz, way, ok in self.sent_along():
            when(ok, lambda dz=dz, way=way: self.along(dz, way).wait_send())


def partner(at, dy, dx, dc, k):
    return flip(at, dy, dx, dc, 0)[:3] + ({0: at[3], 1: at[3] + 1 - 2 * (at[3] % 2), 2: (at[3] + 2) % 4, 3: 3 - at[3]}[k],)


CUBE = [(0, 0, 1, 0), (0, 1, 0, 0), (1, 0, 0, 0), (0, 1, 1, 0), (1, 0, 1, 0), (1, 1, 0, 0), (1, 1, 1, 0)]


def greet_all(me):
    barrier = pltpu.get_barrier_semaphore()
    others = CUBE + [(0, 0, 0, 1), (0, 0, 0, 2), (0, 0, 0, 3)]
    for other in others:
        pl.semaphore_signal(barrier, inc=1, device_id=device(partner(me, *other)), device_id_type=MESH)
    pl.semaphore_wait(barrier, len(others))


BLOCKS = ((1, 1), (0, 1), (1, 0), (0, 0))


ORDER = (3, 2, 1, 0)


class Scatterer:
    count = 59

    def __init__(self, me, part, out, mine, from_core, from_pair, from_far, from_line, send, recv, here=None):
        self.me, self.part, self.out = me, part, out
        self.mine, self.from_core, self.from_pair, self.from_far, self.from_line = (
            mine, from_core, from_pair, from_far, from_line,
        )
        self.send, self.recv, self.here = send, recv, here
        self.left, self.right = halves(part.shape[2])

    def copy(self, name, index):
        if name == "core":
            b, k, half = index // 8, index // 2 % 4, index % 2
            cols = self.right if half else self.left
            src = self.part.at[slot(partner(self.me, *BLOCKS[b], 1, k)), :, cols]
            dst, to, i = self.from_core.at[b, k, :, cols], (0, 0, 1, 0), index
        elif name == "x":
            b, k = index // 4, index % 4
            src, dst = self.mine.at[b, k, :, self.left], self.from_pair.at[b, k, :, self.left]
            to, i = (0, 1, 0, 0), 32 + index
        elif name == "y":
            b, k = index // 4, index % 4
            src, dst = self.mine.at[2 * b, k, :, self.right], self.from_pair.at[b, k, :, self.right]
            to, i = (1, 0, 0, 0), 40 + index
        elif name == "fy":
            src, dst = self.mine.at[2, index, :, self.left], self.from_far.at[index, :, self.left]
            to, i = (1, 0, 0, 0), 48 + index
        elif name == "fx":
            src, dst = self.mine.at[1, index, :, self.right], self.from_far.at[index, :, self.right]
            to, i = (0, 1, 0, 0), 52 + index
        else:
            src, dst, to, i = self.mine.at[3, index], self.from_line.at[index - 1], (0, 0, 0, index), 55 + index
        return pltpu.make_async_remote_copy(
            src_ref=src, dst_ref=dst, send_sem=self.send.at[i], recv_sem=self.recv.at[i],
            device_id=device(partner(self.me, *to)), device_id_type=MESH,
        )

    def local(self, b, k):
        own = slot(partner(self.me, *BLOCKS[b], 0, k))
        return pltpu.make_async_copy(self.part.at[own], self.mine.at[b, k], self.here.at[b * 4 + k])

    def start(self, *cuts):
        for k in ORDER:
            for b in range(4):
                for half in cuts or (0, 1):
                    self.copy("core", b * 8 + k * 2 + half).start()
                if self.here is not None:
                    self.local(b, k).start()

    def add(self, b, k, cols, others):
        total = self.mine[b, k, :, cols].astype(f32)
        for ref in others:
            total += ref.astype(f32)
        return total

    def pair(self, k):
        for b in range(4):
            for half in (0, 1):
                self.copy("core", b * 8 + k * 2 + half).wait_recv()
            if self.here is not None:
                self.local(b, k).wait()
                own = self.mine[b, k]
            else:
                own = self.part[slot(partner(self.me, *BLOCKS[b], 0, k))]
            self.mine[b, k] = own + self.from_core[b, k]
            if b < 2:
                self.copy("x", b * 4 + k).start()
            if b % 2 == 0:
                self.copy("y", b * 2 + k).start()

    def far(self, k):
        self.copy("x", k).wait_recv()
        self.mine[2, k, :, self.left] = self.mine[2, k, :, self.left] + self.from_pair[0, k, :, self.left]
        self.copy("fy", k).start()
        self.copy("y", k).wait_recv()
        self.mine[1, k, :, self.right] = self.mine[1, k, :, self.right] + self.from_pair[0, k, :, self.right]
        self.copy("fx", k).start()

    def line(self, k):
        for made in (self.copy("x", 4 + k), self.copy("y", 4 + k), self.copy("fy", k), self.copy("fx", k)):
            made.wait_recv()
        if k:
            self.mine[3, k] = self.add(3, k, slice(None), [self.from_pair[1, k], self.from_far[k]]).astype(bf16)
            self.copy("z", k).start()

    def finish(self):
        for k in (1, 2, 3):
            self.copy("z", k).wait_recv()
        self.out[...] = self.add(
            3, 0, slice(None),
            [self.from_pair[1, 0], self.from_far[0], self.from_line[0], self.from_line[1], self.from_line[2]],
        )
        for name, indices in (
            ("core", range(32)), ("x", range(8)), ("y", range(8)), ("fy", range(4)), ("fx", range(4)), ("z", (1, 2, 3)),
        ):
            for i in indices:
                self.copy(name, i).wait_send()


def scatter_scratch(rows, width):
    vmem = lambda *lead: pltpu.VMEM(lead + (rows, width), bf16)
    return [
        vmem(4, 4), vmem(4, 4), vmem(2, 4), vmem(4), vmem(3),
        pltpu.SemaphoreType.DMA((Scatterer.count,)), pltpu.SemaphoreType.DMA((Scatterer.count,)),
    ]


class Summer:
    def __init__(self, me, own, out, held, send, recv):
        self.me, self.own, self.out, self.held, self.send, self.recv = me, own, out, held, send, recv

    def copy(self, i):
        src = self.own if i == 0 else self.held.at[5 + min(i, 3)]
        to = ((0, 0, 1, 0), (0, 1, 0, 0), (1, 0, 0, 0), (0, 0, 0, 1), (0, 0, 0, 2), (0, 0, 0, 3))[i]
        return pltpu.make_async_remote_copy(
            src_ref=src, dst_ref=self.held.at[i], send_sem=self.send.at[i], recv_sem=self.recv.at[i],
            device_id=device(partner(self.me, *to)), device_id_type=MESH,
        )

    def start(self):
        self.copy(0).start()

    def next(self, i):
        self.copy(i - 1).wait_recv()
        before = self.own[...] if i == 1 else self.held[4 + i]
        self.held[5 + i] = before + self.held[i - 1]
        for j in (i,) if i < 3 else (3, 4, 5):
            self.copy(j).start()

    def finish(self):
        for j in (3, 4, 5):
            self.copy(j).wait_recv()
        self.out[...] = (self.held[8] + self.held[3]) + (self.held[4] + self.held[5])
        for j in range(6):
            self.copy(j).wait_send()


class Quick:
    def __init__(self, me, own, out, held, send, recv):
        self.me, self.own, self.out, self.held, self.send, self.recv = me, own, out, held, send, recv

    def copy(self, i):
        near = i < len(CUBE)
        to = CUBE[i] if near else (0, 0, 0, i - len(CUBE) + 1)
        return pltpu.make_async_remote_copy(
            src_ref=self.own if near else self.held.at[10], dst_ref=self.held.at[i],
            send_sem=self.send.at[i], recv_sem=self.recv.at[i],
            device_id=device(partner(self.me, *to)), device_id_type=MESH,
        )

    def start(self):
        for i in range(7):
            self.copy(i).start()

    def finish(self):
        for i in range(7):
            self.copy(i).wait_recv()
        self.held[10] = self.own[...] + functools.reduce(jnp.add, [self.held[i] for i in range(7)])
        for i in (7, 8, 9):
            self.copy(i).start()
        for i in (7, 8, 9):
            self.copy(i).wait_recv()
        self.out[...] = (self.held[10] + self.held[7]) + (self.held[8] + self.held[9])
        for i in range(10):
            self.copy(i).wait_send()


AUX = 16


def features(seg_ref, at):
    last = seg_ref.shape[0] - 1
    line = lambda i: jnp.broadcast_to(seg_ref[pl.ds(i, 1), :].astype(f32), (8, Q))
    seg = line(at)
    before = jnp.where(at > 0, line(jnp.maximum(at - 1, 0)), -1.0)
    after = jnp.where(at < last, line(jnp.minimum(at + 1, last)), -1.0)
    lane = lax.broadcasted_iota(jnp.int32, (8, Q), 1)
    earlier = [jnp.where(lane < k, pltpu.roll(before, k, 1), pltpu.roll(seg, k, 1)) == seg for k in (1, 2, 3)]
    later = [
        jnp.where(lane < Q - k, pltpu.roll(seg, Q - k, 1), pltpu.roll(after, Q - k, 1)) == seg for k in (1, 2, 3)
    ]
    edges = [seg == x for x in (seg[:, Q - 1 :], seg[:, :1], before[:, Q - 1 :], after[:, :1])]
    one = lambda mask: jnp.where(mask, 1.0, 0.0)
    lines = [one(m) for m in earlier] + [seg] + [one(m) for m in edges + later]
    row = lax.broadcasted_iota(jnp.int32, (8, Q), 0)
    blocks = []
    for i in range(0, AUX, 8):
        block = jnp.zeros((8, Q), f32)
        for j, x in enumerate(lines[i : i + 8]):
            block = jnp.where(row == j, x, block)
        blocks.append(block)
    return jnp.transpose(jnp.concatenate(blocks + [jnp.zeros((Q - AUX, Q), f32)], axis=0))


def reaches(here, number):
    return dict(collective_id=number, has_side_effects=True) if here else {}


OTHERS_AT = 3
OTHERS_LAG = 4
BEATS = (5, 6, 7, 8, 9, 10, 11, 11, 11)


def front_kernel(
    sizes, here,
    tok_ref, halo_ref, seg_ref, cw_ref, cb_ref, dtb_ref, alog_ref, x2_ref, first_ref, own_ref, gain_in_ref,
    normed_ref, turned_ref, conv_ref, act_ref, low_ref, dsil_ref, dt_ref, cum_ref, dtraw_ref, aux_ref, sb_ref, w_ref, gain_ref,
    full_ref,
    ext_ref, column_ref, state_ref, land_ref, near_ref, side_ref, send_ref, recv_ref, copy_ref,
):
    inner, channels, heads, state = sizes
    step = pl.program_id(0)
    taken = channels + 2 * heads
    if here:
        me = place()
        urgent = Gatherer(me, near_ref, land_ref, send_ref.at[0], recv_ref.at[0])
        others = Gatherer(me, side_ref, full_ref, send_ref.at[1], recv_ref.at[1])
        mine = [
            pltpu.make_async_copy(near_ref, land_ref.at[slot(me)], copy_ref.at[0]),
            pltpu.make_async_copy(side_ref, full_ref.at[slot(me)], copy_ref.at[1]),
        ]

    @pl.when(step == 0)
    def _():
        state_ref[...] = jnp.zeros_like(state_ref)
        if here:
            near_ref[:, :taken] = first_ref[:, inner:]
            gain_in = gain_in_ref[...]
            gain_in = jnp.concatenate([gain_in, jnp.zeros((1, Q - gain_in.shape[1]), f32)], axis=1)
            gain_in = jnp.transpose(jnp.broadcast_to(gain_in, (Q, Q)))
            near_ref[:, taken:] = gain_in[: near_ref.shape[0], 0:1].astype(bf16)
            side_ref[:, :inner] = first_ref[:, :inner]
            side_ref[:, inner:] = own_ref[...]
            greet(me)
            urgent.start()
            mine[0].start()
            for t in range(Gatherer.beats):
                if t == OTHERS_AT:
                    others.start()
                    mine[1].start()
                urgent.beat(t)
                if 0 <= t - OTHERS_LAG < BEATS[0]:
                    others.beat(t - OTHERS_LAG)
            mine[0].wait()
            urgent.finish()
            source = land_ref
        else:
            source = first_ref
        rows = source.shape[1]
        group = 1 if rows % 16 == 0 else 48 // rows
        for j in range(0, source.shape[0], group):
            block = jnp.concatenate([source[j + i].astype(f32) for i in range(group)], axis=0)
            at = slice(j * rows, (j + group) * rows)
            w_ref[at, :] = block[:, :taken].astype(bf16)
            column_ref[at, :] = jnp.broadcast_to(block[:, taken:], (block.shape[0], Q))
        for at in range(0, gain_ref.shape[1], Q):
            gain_ref[:, at : at + Q] = jnp.transpose(column_ref[at : at + Q, :])[0:1, :]

    gain = gain_ref[...]

    def norm(x):
        x = x.astype(f32)
        inv = lax.rsqrt(jnp.mean(x * x, axis=1, keepdims=True) + eps)
        return (x * inv * gain).astype(bf16)

    normed = norm(tok_ref[...])
    normed_ref[...] = normed
    turned_ref[...] = jnp.transpose(normed)
    both = jnp.concatenate([norm(halo_ref[...]), normed], axis=0)
    dt_raw = nn(normed, w_ref[:, channels : channels + 2 * heads])
    dtraw_ref[...] = dt_raw
    aux = features(seg_ref, pl.num_programs(0) - 1 - step)
    aux_ref[...] = aux[:, : aux_ref.shape[1]]
    m1, m2, m3 = aux[:, 0:1], aux[:, 1:2], aux[:, 2:3]
    block = 256
    for at in range(0, channels, block):
        sl = slice(at, at + block)
        ext_ref[:, sl] = nn(both, w_ref[:, at : at + block])
        x0 = ext_ref[HALO : HALO + Q, sl]
        conv_ref[:, sl] = x0
        pre = cb_ref[sl][None, :] + cw_ref[0:1, sl] * x0
        pre += cw_ref[1:2, sl] * (ext_ref[HALO - 1 : HALO - 1 + Q, sl] * m1)
        pre += cw_ref[2:3, sl] * (ext_ref[HALO - 2 : HALO - 2 + Q, sl] * m2)
        pre += cw_ref[3:4, sl] * (ext_ref[HALO - 3 : HALO - 3 + Q, sl] * m3)
        sig = 1.0 / (1.0 + jnp.exp(-pre))
        act = pre * sig
        act_ref[:, sl] = act
        low_ref[:, sl] = act.astype(bf16)
        dsil_ref[:, sl] = sig * (1.0 + pre * (1.0 - sig))
    v = dt_raw + dtb_ref[...]
    dt = jnp.maximum(v, 0.0) + jnp.log1p(jnp.exp(-jnp.abs(v)))
    dt_ref[...] = dt
    rate = -dt * jnp.exp(alog_ref[...])
    row, col = iotas((Q, Q))
    cum = nn_exact((col <= row).astype(bf16), rate)
    cum_ref[...] = cum
    sb_ref[0] = state_ref[...].astype(bf16)
    weight = dt[:, heads:] * jnp.exp(cum[:, heads:] - rate[:, heads:]) * aux[:, 5:6]
    whole = jnp.exp(cum[Q - 1 :, heads:]) * aux[0:1, 7:8]
    scales = split2(jnp.concatenate([weight, jnp.broadcast_to(whole, (8, heads))], axis=0))
    b_bwd = low_ref[:, inner + 2 * state : inner + 3 * state]
    for at in range(0, inner, block):
        sl = slice(at, at + block)
        wide = nn(scales, x2_ref[:, sl])
        vs = (low_ref[:, sl].astype(f32) * wide[:Q]).astype(bf16)
        state_ref[:, sl] = state_ref[:, sl] * wide[Q : Q + 1] + tn(b_bwd, vs)
    if here:
        steps = len(BEATS) - 1
        for i in range(steps):

            @pl.when(step == i)
            def _():
                for t in range(BEATS[i], BEATS[i + 1]):
                    others.beat(t)
                if i == steps - 1:
                    mine[1].wait()
                    others.finish()


def front(tokens, seg, conv_w, conv_b, dt_bias, a_log, x2, first, own, gain, sizes, here):
    inner, channels, heads, state = sizes
    t, d = tokens.shape
    n = t // Q
    rev = lambda i: (n - 1 - i, 0)
    fixed = lambda i: (0, 0)
    blk = lambda width: pl.BlockSpec((Q, width), rev)
    whole = lambda a: pl.BlockSpec(a.shape, lambda i: (0,) * a.ndim)
    anywhere = pl.BlockSpec(memory_space=pl.ANY)
    per = Q // HALO
    out = lambda width, dtype: jax.ShapeDtypeStruct((t, width), dtype)
    taken = channels + 2 * heads
    rows = own.shape[0]
    return pl.pallas_call(
        functools.partial(front_kernel, sizes, here),
        grid=(n,),
        in_specs=[
            blk(d),
            pl.BlockSpec((HALO, d), lambda i: (jnp.maximum((n - 1 - i) * per - 1, 0), 0)),
            whole(seg), whole(conv_w), whole(conv_b), whole(dt_bias), whole(a_log), whole(x2), whole(first), whole(own),
            whole(gain),
        ],
        out_specs=[
            blk(d), pl.BlockSpec((d, Q), lambda i: (0, n - 1 - i)), blk(channels), blk(channels), blk(channels), blk(channels),
            blk(2 * heads), blk(2 * heads), blk(2 * heads), blk(AUX),
            pl.BlockSpec((1, state, inner), lambda i: (n - 1 - i, 0, 0)),
            pl.BlockSpec((d, taken), fixed), pl.BlockSpec((1, d), fixed),
            anywhere,
        ],
        out_shape=[
            out(d, bf16), jax.ShapeDtypeStruct((d, t), bf16),
            out(channels, f32), out(channels, f32), out(channels, bf16), out(channels, f32),
            out(2 * heads, f32), out(2 * heads, f32), out(2 * heads, f32), out(AUX, f32),
            jax.ShapeDtypeStruct((n, state, inner), bf16),
            jax.ShapeDtypeStruct((d, taken), bf16), jax.ShapeDtypeStruct((1, d), f32),
            jax.ShapeDtypeStruct((32, rows, 2 * inner) if here else (1, 8, Q), bf16),
        ],
        scratch_shapes=[
            pltpu.VMEM((HALO + Q, channels), f32),
            pltpu.VMEM((d, Q), f32),
            pltpu.VMEM((state, inner), f32),
            pltpu.VMEM((32, rows, taken + 1) if here else (1, 8, Q), bf16),
            pltpu.VMEM((rows, taken + 1), bf16),
            pltpu.VMEM((rows, 2 * inner), bf16),
            pltpu.SemaphoreType.DMA((2, Gatherer.count)),
            pltpu.SemaphoreType.DMA((2, Gatherer.count)),
            pltpu.SemaphoreType.DMA((2,)),
        ],
        compiler_params=pltpu.CompilerParams(
            dimension_semantics=("arbitrary",), vmem_limit_bytes=60 * 1024 * 1024, **reaches(here, 0)
        ),
        cost_estimate=pl.CostEstimate(flops=5_000_000_000, bytes_accessed=50_000_000, transcendentals=0),
    )(tokens, tokens, seg, conv_w, conv_b, dt_bias, a_log, x2, first, own, gain)


def middle_kernel(
    sizes,
    tok_ref, act_ref, normed_ref, dt_ref, cum_ref, aux_ref, seg_ref, cot_ref, sb_ref, w_ref,
    alog_ref, skip_in_ref, og_ref, x2_ref, r_ref,
    out_ref, turned_ref, nout_ref, dgate_ref, dy_ref, dv_ref, dbc_ref, drate_ref, dq_ref, sf_ref, dog_ref, dsk_ref,
    decay_ref, mix_ref, state_ref, adj_ref, ssm_ref, gated_ref, dno_ref, yf_ref, yb_ref, wide_ref,
    p_ref, q_ref, scal_ref, gate_ref, skip_ref,
):
    inner, channels, heads, state = sizes
    quad = 256
    step = pl.program_id(0)

    @pl.when(step == 0)
    def _():
        state_ref[...] = jnp.zeros_like(state_ref)
        adj_ref[...] = jnp.zeros_like(adj_ref)
        dog_ref[...] = jnp.zeros_like(dog_ref)
        dsk_ref[...] = jnp.zeros_like(dsk_ref)
        q_ref[...] = jnp.zeros_like(q_ref)
        skip_ref[...] = nn(split2(jnp.broadcast_to(skip_in_ref[...], (8, heads))), x2_ref[...])[0:1]

    sf_ref[0] = state_ref[...].astype(bf16)
    aux = aux_ref[...]
    row, col = iotas((Q, Q))
    lower = col < row
    same = aux[:, 3:4] == seg_ref[pl.ds(step, 1), :].astype(f32)
    b_f = act_ref[:, inner : inner + state].astype(bf16)
    c_f = act_ref[:, inner + state : inner + 2 * state].astype(bf16)
    b_b = act_ref[:, inner + 2 * state : inner + 3 * state].astype(bf16)
    c_b = act_ref[:, inner + 3 * state :].astype(bf16)
    g = jnp.where(same & (col != row), jnp.where(lower, nt(c_f, b_f), nt(c_b, b_b)), 0.0)
    dt = dt_ref[...]
    cum = cum_ref[...]
    rate = -dt * jnp.exp(alog_ref[...])
    cf, cb = cum[:, :heads], cum[:, heads:] - rate[:, heads:]
    dtf, dtb = dt[:, :heads], dt[:, heads:]
    total_f, total_b = cum[Q - 1 :, :heads], cum[Q - 1 :, heads:]
    ldt = jnp.log(jnp.maximum(dt, 1e-37))
    rows = jnp.transpose(
        jnp.concatenate(
            [cf - ldt[:, :heads], cb + ldt[:, heads:], jnp.zeros((Q, Q - 2 * heads), f32)], axis=1
        )
    )
    scales = split2(
        jnp.concatenate(
            [
                jnp.exp(cf) * aux[:, 6:7],
                jnp.exp(total_b - cb) * aux[:, 7:8],
                dtf * jnp.exp(total_f - cf) * aux[:, 4:5],
                dtb * jnp.exp(cb) * aux[:, 5:6],
                jnp.broadcast_to(jnp.exp(total_f) * aux[Q - 1 :, 6:7], (8, heads)),
                jnp.broadcast_to(jnp.exp(total_b) * aux[0:1, 7:8], (8, heads)),
            ],
            axis=0,
        )
    )
    lane = lax.broadcasted_iota(jnp.int32, (1, Q), 1)
    first = (lane < Q // 2).astype(bf16)
    second = (lane >= Q // 2).astype(bf16)

    def apart(x):
        return jnp.concatenate([x * first, x * second], axis=0)

    squares = jnp.zeros((Q, quad), f32)
    dots = jnp.zeros((Q, quad), f32)
    cot = cot_ref[...]
    turned_ref[...] = jnp.transpose(cot)
    for at in range(0, inner, quad):
        sl = slice(at, at + quad)
        wide_ref[:, sl] = nn(scales, x2_ref[:, sl])
        v = act_ref[:, sl]
        low = v.astype(bf16)
        yf = nn(c_f, state_ref[:, sl].astype(bf16)) * wide_ref[:Q, sl]
        yb = nn(c_b, sb_ref[0, :, sl]) * wide_ref[Q : 2 * Q, sl]
        yf_ref[:, sl] = yf
        yb_ref[:, sl] = yb
        parts = []
        for half in range(2):
            mixes = []
            for h in (at // 64 + 2 * half, at // 64 + 2 * half + 1):
                gap = jnp.where(
                    lower,
                    cf[:, h : h + 1] - rows[h : h + 1, :],
                    rows[heads + h : heads + h + 1, :] - cb[:, h : h + 1],
                )
                decay = jnp.exp(gap)
                decay_ref[h] = decay
                mix = (g * decay).astype(bf16)
                mix_ref[h * Q : (h + 1) * Q, :] = mix
                mixes.append(mix)
            parts.append(
                nn(jnp.concatenate(mixes, axis=1), apart(low[:, half * Q : (half + 1) * Q]))
            )
        ssm = jnp.concatenate(parts, axis=1) + yf + yb + skip_ref[:, sl] * v
        ssm_ref[:, sl] = ssm
        gate = nn(normed_ref[...], w_ref[:, sl])
        gate_ref[:, sl] = gate
        gated = ssm * (gate / (1.0 + jnp.exp(-gate)))
        gated_ref[:, sl] = gated
        dno = nn(cot, w_ref[:, inner + at : inner + at + quad])
        dno_ref[:, sl] = dno
        squares += gated * gated
        dots += dno * og_ref[sl][None, :] * gated

    inv = lax.rsqrt(jnp.sum(squares, axis=1, keepdims=True) / inner + eps)
    drag = inv * (inv * jnp.sum(dots, axis=1, keepdims=True) / inner)
    dg = jnp.zeros((Q, Q), f32)
    d_cf = jnp.zeros((Q, state), f32)
    d_cb = jnp.zeros((Q, state), f32)
    d_bb = jnp.zeros((Q, state), f32)
    heads_of = jnp.zeros((3 * Q, Q), f32)
    for at in range(0, inner, quad):
        sl = slice(at, at + quad)
        v = act_ref[:, sl]
        low = v.astype(bf16)
        low_f = low.astype(f32)
        ssm, gate, gated, dno = ssm_ref[:, sl], gate_ref[:, sl], gated_ref[:, sl], dno_ref[:, sl]
        og = og_ref[sl][None, :]
        unit = gated * inv
        nout_ref[:, sl] = (unit * og).astype(bf16)
        dog_ref[:, sl] += jnp.sum(dno * unit, axis=0, keepdims=True)
        d_gated = inv * (dno * og) - gated * (inv * drag)
        sig = 1.0 / (1.0 + jnp.exp(-gate))
        d_ssm = d_gated * (gate * sig)
        dgate_ref[:, sl] = (d_gated * ssm * (sig * (1.0 + gate * (1.0 - sig)))).astype(bf16)
        dsk_ref[:, sl] += jnp.sum(d_ssm * v, axis=0, keepdims=True)
        dy = d_ssm.astype(bf16)
        dy_ref[:, sl] = dy
        dy_f = dy.astype(f32)
        parts = []
        for half in range(2):
            h0 = at // 64 + 2 * half
            cut = slice(half * Q, (half + 1) * Q)
            d_mix = nt(dy[:, cut], apart(low[:, cut]))
            for i in range(2):
                h = h0 + i
                x = d_mix[:, i * Q : (i + 1) * Q] * decay_ref[h]
                dg += x
                full = x * g
                under = jnp.where(lower, full, 0.0)
                over = full - under
                q_ref[h : h + 1, :] = jnp.sum(under, axis=0, keepdims=True)
                q_ref[heads + h : heads + h + 1, :] = jnp.sum(over, axis=0, keepdims=True)
                p_ref[:, h : h + 1] = jnp.sum(under, axis=1, keepdims=True)
                p_ref[:, heads + h : heads + h + 1] = jnp.sum(over, axis=1, keepdims=True)
            parts.append(tn(mix_ref[h0 * Q : (h0 + 2) * Q, :], apart(dy[:, cut])))
        adj = adj_ref[:, sl]
        adj_low = adj.astype(bf16)
        sf_low = state_ref[:, sl].astype(bf16)
        sb_low = sb_ref[0, :, sl]
        wide_wb = wide_ref[3 * Q : 4 * Q, sl]
        dvb = wide_wb * nn(b_b, adj_low)
        dv_ref[:, sl] = d_ssm * skip_ref[:, sl] + jnp.concatenate(parts, axis=1) + dvb
        prods = jnp.concatenate(
            [
                (dy_f * yf_ref[:, sl]).astype(bf16),
                (dy_f * yb_ref[:, sl]).astype(bf16),
                (low_f * dvb).astype(bf16),
            ],
            axis=0,
        )
        heads_of += nn(prods, r_ref[sl, :])
        dye_f = (dy_f * wide_ref[:Q, sl]).astype(bf16)
        dye_b = (dy_f * wide_ref[Q : 2 * Q, sl]).astype(bf16)
        vs_f = (low_f * wide_ref[2 * Q : 3 * Q, sl]).astype(bf16)
        vs_b = (low_f * wide_wb).astype(bf16)
        d_cf += nt(dye_f, sf_low)
        d_cb += nt(dye_b, sb_low)
        d_bb += nt(vs_b, adj_low)
        across_b = wide_ref[4 * Q + 8 : 4 * Q + 9, sl]
        scal_ref[:, sl] = jnp.sum(adj * sb_low.astype(f32), axis=0, keepdims=True) * across_b
        adj_ref[:, sl] = adj * across_b + tn(c_b, dye_b)
        state_ref[:, sl] = state_ref[:, sl] * wide_ref[4 * Q : 4 * Q + 1, sl] + tn(b_f, vs_f)

    out_ref[...] = (tok_ref[...].astype(f32) + nt(nout_ref[...], w_ref[:, inner:])).astype(bf16)
    dg = jnp.where(same & (col != row), dg, 0.0)
    dg_f = jnp.where(lower, dg, 0.0)
    dg_b = (dg - dg_f).astype(bf16)
    dg_f = dg_f.astype(bf16)
    dbc_ref[...] = jnp.concatenate(
        [tn(dg_f, c_f), d_cf + nn(dg_f, b_f), d_bb + tn(dg_b, c_b), d_cb + nn(dg_b, b_b)], axis=1
    )
    q_cols = jnp.transpose(q_ref[...])[:, : 2 * heads]
    dots_f, dots_b, dots_v = heads_of[:Q, :heads], heads_of[Q : 2 * Q, :heads], heads_of[2 * Q :, :heads]
    through = nn(split_rows(jnp.broadcast_to(scal_ref[...], (8, inner))), r_ref[...])
    through = (through[0:1] + through[8:9])[:, :heads]
    diff = p_ref[:, : 2 * heads] - q_cols
    d_rate_f = nn_exact((col >= row).astype(bf16), diff[:, :heads] + dots_f)
    d_rate_b = (
        nn_exact((col <= row).astype(bf16), diff[:, heads:] + dots_b)
        + nn_exact((col > row).astype(bf16), dots_v)
        + through
    )
    drate_ref[...] = jnp.concatenate([d_rate_f, d_rate_b], axis=1)
    dq_ref[...] = jnp.concatenate([q_cols[:, :heads], q_cols[:, heads:] + dots_v], axis=1)


def middle(tokens, act, normed, dt, cum, aux, seg, cot, sb, w_side, a_log, skip, og, x2, r, sizes):
    inner, channels, heads, state = sizes
    t, d = tokens.shape
    n = t // Q
    fwd = lambda i: (i, 0)
    fixed = lambda i: (0, 0)
    cube = lambda i: (i, 0, 0)
    blk = lambda width: pl.BlockSpec((Q, width), fwd)
    whole = lambda a: pl.BlockSpec(a.shape, fixed)
    out = lambda width, dtype: jax.ShapeDtypeStruct((t, width), dtype)
    line = jax.ShapeDtypeStruct((1, inner), f32)
    return pl.pallas_call(
        functools.partial(middle_kernel, sizes),
        grid=(n,),
        in_specs=[
            blk(d), blk(channels), blk(d), blk(2 * heads), blk(2 * heads), blk(aux.shape[1]),
            whole(seg), blk(d), pl.BlockSpec((1, state, inner), cube),
            whole(w_side), whole(a_log), whole(skip), pl.BlockSpec(og.shape, lambda i: (0,)), whole(x2), whole(r),
        ],
        out_specs=[
            blk(d), pl.BlockSpec((d, Q), lambda i: (0, i)), blk(inner), blk(inner), blk(inner), blk(inner), blk(4 * state),
            blk(2 * heads), blk(2 * heads), pl.BlockSpec((1, state, inner), cube),
            pl.BlockSpec((1, inner), fixed), pl.BlockSpec((1, inner), fixed),
        ],
        out_shape=[
            out(d, bf16), jax.ShapeDtypeStruct((d, t), bf16),
            out(inner, bf16), out(inner, bf16), out(inner, bf16), out(inner, f32),
            out(4 * state, f32), out(2 * heads, f32), out(2 * heads, f32),
            jax.ShapeDtypeStruct((n, state, inner), bf16), line, line,
        ],
        scratch_shapes=[
            pltpu.VMEM((heads, Q, Q), f32),
            pltpu.VMEM((heads * Q, Q), bf16),
            pltpu.VMEM((state, inner), f32),
            pltpu.VMEM((state, inner), f32),
            pltpu.VMEM((Q, inner), f32),
            pltpu.VMEM((Q, inner), f32),
            pltpu.VMEM((Q, inner), f32),
            pltpu.VMEM((Q, inner), f32),
            pltpu.VMEM((Q, inner), f32),
            pltpu.VMEM((4 * Q + 16, inner), f32),
            pltpu.VMEM((Q, Q), f32),
            pltpu.VMEM((Q, Q), f32),
            pltpu.VMEM((1, inner), f32),
            pltpu.VMEM((Q, inner), f32),
            pltpu.VMEM((1, inner), f32),
        ],
        compiler_params=pltpu.CompilerParams(
            dimension_semantics=("arbitrary",), vmem_limit_bytes=60 * 1024 * 1024
        ),
        cost_estimate=pl.CostEstimate(flops=30_000_000_000, bytes_accessed=60_000_000, transcendentals=0),
    )(tokens, act, normed, dt, cum, aux, seg, cot, sb, w_side, a_log, skip, og, x2, r)


def side_kernel(half, a_ref, b_ref, u_ref, v_ref, out_ref):
    step = pl.program_id(0)

    @pl.when(step < half)
    def _():
        out_ref[...] = nn(a_ref[...], u_ref[...]).astype(bf16)

    @pl.when(step >= half)
    def _():
        out_ref[...] = nn(b_ref[...], v_ref[...]).astype(bf16)


def side(a, b, u, v):
    d, t = a.shape
    block = 768
    half = u.shape[1] // block
    fixed = lambda i: (0, 0)
    return pl.pallas_call(
        functools.partial(side_kernel, half),
        grid=(2 * half,),
        in_specs=[
            pl.BlockSpec((d, t), fixed), pl.BlockSpec((d, t), fixed),
            pl.BlockSpec((t, block), lambda i: (0, jnp.minimum(i, half - 1))),
            pl.BlockSpec((t, block), lambda i: (0, jnp.maximum(i - half, 0))),
        ],
        out_specs=pl.BlockSpec((d, block), lambda i: (0, i)),
        out_shape=jax.ShapeDtypeStruct((d, 2 * u.shape[1]), bf16),
        compiler_params=pltpu.CompilerParams(
            dimension_semantics=("arbitrary",), vmem_limit_bytes=60 * 1024 * 1024
        ),
        cost_estimate=pl.CostEstimate(flops=4 * d * t * u.shape[1], bytes_accessed=14_000_000, transcendentals=0),
    )(a, b, u, v)


BLOCK = 256
ROWS = 256
PIECES = (3, 3)


def rear_kernel(
    sizes, here,
    low_ref, dsil_ref, conv_ref, dy_ref, dv_ref, sf_ref, cw_ref, x2_ref, r_ref, dog_ref, dsk_ref,
    bc_ref, dt_ref, cum_ref, dtraw_ref, aux_ref, dbc_ref, drate_ref, dq_ref, dtb_ref, alog_ref,
    turned_ref, w_ref, side_ref, gain_ref,
    dgate_ref, tok_ref, cot_ref, given_ref,
    *rest,
):
    inner, channels, heads, state = sizes
    blocks = inner // BLOCK
    step = pl.program_id(0)
    t, d = low_ref.shape[0], turned_ref.shape[0]
    n = t // Q
    taken = channels + 2 * heads
    if here:
        dtok_ref, total_ref, gains_ref, *sum_refs = rest[:7]
        (
            dproj_ref, own_ref, dgain_ref, scales_ref, ct_ref, dpre_ref, dots_ref, dbf_ref, scal_ref, through_ref, *exchange,
        ) = rest[7:]
        me = place()
        sums = [Scatterer(me, given_ref, sum_refs[0], *exchange[:8])]
        for i in range(3):
            part_ref, *held = exchange[8 + 8 * i : 16 + 8 * i]
            sums.append(Scatterer(me, part_ref, sum_refs[1 + i], *held))
        sums.append(Summer(me, own_ref, total_ref, *exchange[32:35]))
        sums.append(Quick(me, dgain_ref, gains_ref, *exchange[35:]))
    else:
        dtok_ref, own_ref, dgain_ref, dproj_ref = rest[:4]
        scales_ref, ct_ref, dpre_ref, dots_ref, dbf_ref, scal_ref, through_ref = rest[4:]

    chunk = lambda c: slice(c * Q, (c + 1) * Q)

    @pl.when(step == 0)
    def _():
        if here:
            greet_all(me)
            sums[0].start()
        own_ref[...] = jnp.zeros_like(own_ref)
        dgain_ref[...] = jnp.zeros_like(dgain_ref)
        dots_ref[...] = jnp.zeros_like(dots_ref)
        dbf_ref[...] = jnp.zeros_like(dbf_ref)
        through_ref[...] = jnp.zeros_like(through_ref)
        dpre_ref[t:, :] = jnp.zeros((8, BLOCK), f32)
        for c in range(n):
            cf, dtf = cum_ref[chunk(c), :heads], dt_ref[chunk(c), :heads]
            total_f = cf[Q - 1 :, :]
            aux = aux_ref[chunk(c), :]
            scales_ref[c] = split2(
                jnp.concatenate(
                    [
                        jnp.exp(cf) * aux[:, 6:7],
                        dtf * jnp.exp(total_f - cf) * aux[:, 4:5],
                        jnp.broadcast_to(jnp.exp(total_f) * aux[Q - 1 :, 6:7], (16, heads)),
                    ],
                    axis=0,
                )
            )
            ct_ref[c] = jnp.transpose(bc_ref[chunk(c), : 2 * state])[state:, :]

    def through_conv(at):
        sl = pl.ds(at if isinstance(at, int) else pl.multiple_of(at, BLOCK), BLOCK)
        fold = lambda x: jnp.sum(x.reshape(Q // 8, 8, BLOCK), axis=0)
        totals = [jnp.zeros((8, BLOCK), f32) for _ in range(5)]
        for c in range(n):
            conv = conv_ref[chunk(c), :]
            z = dpre_ref[chunk(c), :]
            totals[4] += fold(z)
            totals[0] += fold(z * conv)
            grad = cw_ref[0:1, :] * z
            for k in (1, 2, 3):
                z = dpre_ref[c * Q + k : (c + 1) * Q + k, :] * aux_ref[chunk(c), 7 + k : 8 + k]
                totals[k] += fold(z * conv)
                grad += cw_ref[k : k + 1, :] * z
            dproj_ref[chunk(c), sl] = grad.astype(bf16)
        for k in range(5):
            own_ref[k : k + 1, sl] = jnp.sum(totals[k], axis=0, keepdims=True)

    @pl.when(step < blocks)
    def _():
        adj = jnp.zeros((state, BLOCK), f32)
        for c in reversed(range(n)):
            wide = nn(scales_ref[c], x2_ref[...])
            wide_wf, across = wide[Q : 2 * Q], wide[2 * Q : 2 * Q + 1]
            low_f = low_ref[chunk(c), :].astype(f32)
            adj_low = adj.astype(bf16)
            dvf = wide_wf * nn(bc_ref[chunk(c), :state], adj_low)
            dots_ref[chunk(c), :] += nn((low_f * dvf).astype(bf16), r_ref[...])
            dbf_ref[chunk(c), :] += nt((low_f * wide_wf).astype(bf16), adj_low)
            scal_ref[c : c + 1, :] = jnp.sum(adj * sf_ref[c].astype(f32), axis=0, keepdims=True) * across
            dye = (dy_ref[chunk(c), :].astype(f32) * wide[:Q]).astype(bf16)
            adj = adj * across + nn(ct_ref[c], dye)
            dpre_ref[chunk(c), :] = (dv_ref[chunk(c), :] + dvf) * dsil_ref[chunk(c), :]
        both = nn(split_rows(scal_ref[...]), r_ref[...])
        through_ref[...] += both[:n] + both[n:]
        through_conv(step * BLOCK)
        at = pl.ds(pl.multiple_of(step * BLOCK, BLOCK), BLOCK)
        own_ref[5:6, at] = dog_ref[...]
        skips = nn(split_rows(jnp.broadcast_to(dsk_ref[...], (8, BLOCK))), r_ref[...])
        own_ref[6:7, SKIP_AT : SKIP_AT + Q] += skips[0:1] + skips[8:9]

    @pl.when(step == blocks)
    def _():
        a = jnp.exp(alog_ref[...])
        row, col = iotas((Q, Q))
        before = (col < row).astype(bf16)
        none = jnp.zeros((Q, heads), f32)
        sum_v, sum_a = jnp.zeros((8, 2 * heads), f32), jnp.zeros((8, 2 * heads), f32)
        fold = lambda x: jnp.sum(x.reshape(Q // 8, 8, 2 * heads), axis=0)
        for c in range(n):
            d_bf = jnp.concatenate([dbf_ref[chunk(c), :], jnp.zeros((Q, 3 * state), f32)], axis=1)
            dpre_ref[chunk(c), :] = (dbc_ref[chunk(c), :] + d_bf) * dsil_ref[chunk(c), :]
            dots, dt = dots_ref[chunk(c), :heads], dt_ref[chunk(c), :]
            extra = nn_exact(before, dots) + through_ref[c : c + 1, :heads]
            d_rate = drate_ref[chunk(c), :] + jnp.concatenate([extra, none], axis=1)
            d_dt = dq_ref[chunk(c), :] + jnp.concatenate([dots, none], axis=1)
            d_dt = jnp.where(dt > 0.0, d_dt / jnp.maximum(dt, 1e-37), 0.0)
            d_v = (d_dt - d_rate * a) / (1.0 + jnp.exp(-(dtraw_ref[chunk(c), :] + dtb_ref[...])))
            sum_v += fold(d_v)
            sum_a += fold(d_rate * (-dt * a))
            dproj_ref[chunk(c), channels:] = d_v.astype(bf16)
        own_ref[6:7, BIAS_AT : BIAS_AT + 2 * heads] = jnp.sum(sum_v, axis=0, keepdims=True)
        own_ref[6:7, LOG_AT : LOG_AT + 2 * heads] = jnp.sum(sum_a, axis=0, keepdims=True)
        through_conv(inner)

    @pl.when(step > blocks)
    def _():
        rows = pl.ds(pl.multiple_of((step - blocks - 1) * ROWS, ROWS), ROWS)
        d_normed = nt(dgate_ref[...], side_ref[...]) + nt(dproj_ref[rows, :], w_ref[...])
        x = tok_ref[...].astype(f32)
        inv = lax.rsqrt(jnp.mean(x * x, axis=1, keepdims=True) + eps)
        unit = x * inv
        gains = jnp.sum(d_normed * unit, axis=0, keepdims=True)
        for i in range(d // Q):
            dgain_ref[i : i + 1, :] += gains[:, i * Q : (i + 1) * Q]
        a = d_normed * gain_ref[...]
        dtok_ref[...] = cot_ref[...].astype(f32) + inv * (a - unit * jnp.mean(a * unit, axis=1, keepdims=True))

    if here:
        edges = (0, PIECES[0] * BLOCK, inner, taken)
        for i, acts in enumerate(SUM_BEATS):

            @pl.when(step == i)
            def _():
                for name, which, *index in acts:
                    if name == "make":
                        part = sums[which].part
                        lo = edges[which - 1]
                        for cols in (sums[which].left, sums[which].right):
                            grad = nn(turned_ref[...], dproj_ref[:, lo + cols.start : lo + cols.stop])
                            part[:, :, cols] = grad.reshape(part.shape[:2] + grad.shape[1:]).astype(bf16)
                        sums[which].start()
                    else:
                        getattr(sums[which], name)(*index)


def acts(name, which, *indices):
    return tuple((name, which, i) for i in indices)


SUM_BEATS = (
    acts("pair", 0, 3),
    acts("pair", 0, 2) + acts("far", 0, 3),
    (("make", 1),) + acts("pair", 0, 1) + acts("far", 0, 2) + acts("line", 0, 3),
    acts("pair", 0, 0) + acts("far", 0, 1) + acts("line", 0, 2) + acts("pair", 1, 3, 2, 1, 0),
    acts("far", 0, 0) + acts("line", 0, 1) + acts("far", 1, 3, 2, 1),
    (("make", 2),) + acts("line", 0, 0) + acts("far", 1, 0) + acts("line", 1, 3, 2, 1),
    (("make", 3), ("start", 4), ("finish", 0)) + acts("line", 1, 0) + acts("pair", 2, 3, 2, 1, 0),
    (("finish", 1), ("next", 4, 1)) + acts("pair", 3, 3, 2, 1, 0) + acts("far", 2, 3, 2),
    (("next", 4, 2),) + acts("far", 2, 1, 0) + acts("far", 3, 3, 2) + acts("line", 2, 3, 2),
    (("next", 4, 3),) + acts("far", 3, 1, 0) + acts("line", 2, 1, 0) + acts("line", 3, 3),
    (("start", 5),) + acts("line", 3, 2, 1, 0) + (("finish", 2), ("finish", 4), ("finish", 5), ("finish", 3)),
)


def rear(
    low, dsil, conv, dy, dv, sf, conv_w, x2, r, dog, dsk, dt, cum, dtraw, aux, dbc, drate, dq, dt_bias, a_log,
    turned, w_first, w_side, gain_row, dgate, tokens, cot, given, rows, sizes, here,
):
    inner, channels, heads, state = sizes
    t, d = tokens.shape
    n, blocks = t // Q, inner // BLOCK
    taken = channels + 2 * heads
    steps = blocks + 1 + t // ROWS
    one = pl.Buffered(1)
    wide = lambda limit: pl.BlockSpec((t, BLOCK), lambda i: (0, jnp.minimum(i, limit)))
    short = lambda lead, limit: pl.BlockSpec((lead, BLOCK), lambda i: (0, jnp.minimum(i, limit)))
    whole = lambda a: pl.BlockSpec(a.shape, lambda i: (0, 0), pipeline_mode=one)
    later = lambda width: pl.BlockSpec((ROWS, width), lambda i: (jnp.maximum(i - blocks - 1, 0), 0))
    small = (8, channels)
    scratch = [
        pltpu.VMEM((n, 2 * Q + 16, 2 * heads), bf16),
        pltpu.VMEM((n, state, Q), bf16),
        pltpu.VMEM((t + 8, BLOCK), f32),
        pltpu.VMEM((t, Q), f32),
        pltpu.VMEM((t, state), f32),
        pltpu.VMEM((n, BLOCK), f32),
        pltpu.VMEM((n, Q), f32),
    ]
    if here:
        widths = (PIECES[0] * BLOCK, PIECES[1] * BLOCK, taken - inner)
        out_shape = [small, (8, Q), (rows, 2 * inner)] + [(rows, w) for w in widths]
        own = [pltpu.VMEM((t, taken), bf16), pltpu.VMEM(small, f32), pltpu.VMEM((8, Q), f32)]
        exchange = scatter_scratch(rows, 2 * inner) + [pltpu.SemaphoreType.DMA((16,))]
        for w in widths:
            exchange += [pltpu.VMEM((d // rows, rows, w), bf16)] + scatter_scratch(rows, w)
        exchange += [pltpu.VMEM((9,) + small, f32), pltpu.SemaphoreType.DMA((6,)), pltpu.SemaphoreType.DMA((6,))]
        exchange += [pltpu.VMEM((11, 8, Q), f32), pltpu.SemaphoreType.DMA((10,)), pltpu.SemaphoreType.DMA((10,))]
        scratch = own + scratch + exchange
        outs = [jax.ShapeDtypeStruct(shape, f32) for shape in out_shape]
    else:
        outs = [
            jax.ShapeDtypeStruct(small, f32), jax.ShapeDtypeStruct((8, Q), f32), jax.ShapeDtypeStruct((t, taken), bf16),
        ]
    return pl.pallas_call(
        functools.partial(rear_kernel, sizes, here),
        grid=(steps,),
        in_specs=[
            wide(blocks), wide(blocks), wide(blocks), wide(blocks - 1), wide(blocks - 1),
            pl.BlockSpec((n, state, BLOCK), lambda i: (0, 0, jnp.minimum(i, blocks - 1))),
            short(conv_w.shape[0], blocks), short(2 * heads, blocks - 1),
            pl.BlockSpec((BLOCK, Q), lambda i: (jnp.minimum(i, blocks - 1), 0)),
            short(1, blocks - 1), short(1, blocks - 1),
            pl.BlockSpec((t, BLOCK), lambda i: (0, blocks), pipeline_mode=one),
            whole(dt), whole(cum), whole(dtraw), whole(aux), whole(dbc), whole(drate), whole(dq), whole(dt_bias), whole(a_log),
            whole(turned), whole(w_first), pl.BlockSpec((d, inner), lambda i: (0, 0), pipeline_mode=one), whole(gain_row),
            later(inner), later(d), later(d), pl.BlockSpec(memory_space=pl.ANY),
        ],
        out_specs=[later(d)] + [pl.BlockSpec(o.shape, lambda i: (0, 0)) for o in outs],
        out_shape=[jax.ShapeDtypeStruct((t, d), f32)] + outs,
        scratch_shapes=scratch,
        compiler_params=pltpu.CompilerParams(
            dimension_semantics=("arbitrary",), vmem_limit_bytes=62 * 1024 * 1024, **reaches(here, 1)
        ),
        cost_estimate=pl.CostEstimate(flops=30_000_000_000, bytes_accessed=60_000_000, transcendentals=0),
    )(
        low, dsil, conv, dy, dv, sf, conv_w, x2, r, dog, dsk, low, dt, cum, dtraw, aux, dbc, drate, dq, dt_bias, a_log,
        turned, w_first, w_side, gain_row, dgate, tokens, cot, given,
    )


def unpack(small, taps, inner, heads):
    return (
        small[:taps],
        small[taps],
        small[6, BIAS_AT : BIAS_AT + 2 * heads],
        small[6, LOG_AT : LOG_AT + 2 * heads],
        small[6, SKIP_AT : SKIP_AT + heads],
        small[5, :inner],
    )


def finish_kernel(
    sizes, side_ref, one_ref, two_ref, last_ref, small_ref, gains_ref,
    din_ref, dout_ref, dgain_ref, dcw_ref, dcb_ref, ddtb_ref, dalog_ref, dsk_ref, dog_ref,
):
    inner, channels, heads, rows = sizes
    din_ref[:, :inner] = side_ref[:, :inner]
    at = inner
    for ref in (one_ref, two_ref, last_ref):
        din_ref[:, at : at + ref.shape[1]] = ref[...]
        at += ref.shape[1]
    dout_ref[...] = side_ref[:, inner:]
    taps = dcw_ref.shape[0]
    dcw_ref[...] = small_ref[:taps, :]
    dcb_ref[...] = small_ref[taps, :]
    dog_ref[...] = small_ref[5, :inner]
    ddtb_ref[...] = small_ref[6:7, BIAS_AT : BIAS_AT + 2 * heads]
    dalog_ref[...] = small_ref[6:7, LOG_AT : LOG_AT + 2 * heads]
    dsk_ref[...] = small_ref[6:7, SKIP_AT : SKIP_AT + heads]
    row, col = iotas((Q, Q))
    picked = jnp.zeros((8, Q), f32)
    for i in range(BIAS_AT // Q):
        pick = ((row + i * Q == col + slot(place()) * rows) & (col < rows)).astype(f32).astype(bf16)
        part = jnp.broadcast_to(gains_ref[i : i + 1, :], (8, Q))
        hi = part.astype(bf16)
        mid = (part - hi.astype(f32)).astype(bf16)
        lo = (part - hi.astype(f32) - mid.astype(f32)).astype(bf16)
        picked += nn(hi, pick) + nn(mid, pick) + nn(lo, pick)
    dgain_ref[...] = picked[0:1, :rows]


def finish(sums, small, gains, taps, sizes):
    inner, channels, heads, rows = sizes
    shapes = [
        (rows, inner + channels + 2 * heads), (rows, inner), (1, rows), (taps, channels), (channels,), (1, 2 * heads),
        (1, 2 * heads), (1, heads), (inner,),
    ]
    return pl.pallas_call(
        functools.partial(finish_kernel, sizes),
        out_shape=[jax.ShapeDtypeStruct(shape, f32) for shape in shapes],
    )(*sums, small, gains)


def body(here, tokens, segment_ids, w_in, w_out, norm_gain, conv_w, conv_b, dt_bias, a_log, d_skip, out_gain, cotangent):
    rows = w_in.shape[0]
    d, inner, heads = tokens.shape[1], out_gain.shape[0], d_skip.shape[0]
    parts = d // rows
    channels = conv_w.shape[1]
    state = (channels - inner) // 4
    width = inner // heads
    sizes = (inner, channels, heads, state)
    seg = segment_ids.reshape(-1, Q)
    spread = np.arange(inner)[None, :] // width == np.arange(heads)[:, None]
    x2 = jnp.asarray(np.concatenate([spread, spread], axis=0), bf16)
    r = jnp.asarray(np.pad(spread.T, ((0, 0), (0, Q - heads))), bf16)
    first, own = w_in, w_out.T
    if not here:
        first = lax.all_gather(jnp.concatenate([w_in[:, inner:], norm_gain[:, None]], axis=1), AXES)
    alog_row, dtb_row = a_log[None, :], dt_bias[None, :]
    normed, turned, conv, act, low, dsil, dt, cum, dtraw, aux, sb, w_first, gain_row, w_side = front(
        tokens, seg, conv_w, conv_b, dtb_row, alog_row, x2, first, own, norm_gain.astype(f32)[None, :], sizes, here
    )
    if not here:
        w_side = lax.all_gather(jnp.concatenate([w_in[:, :inner], own], axis=1), AXES)
    w_side = w_side.reshape(d, 2 * inner)
    output, cot_turned, nout, dgate, dy, dv, dbc, drate, dq, sf, d_og, d_sk = middle(
        tokens, act, normed, dt, cum, aux, seg, cotangent, sb, w_side, alog_row, d_skip[None, :], out_gain, x2, r, sizes,
    )
    if here:
        g_side = side(turned, cot_turned, dgate, nout)
    else:
        g_side = jnp.concatenate([nn(turned, dgate), nn(cot_turned, nout)], axis=1)
    g_side = g_side.reshape(parts, rows, 2 * inner)
    d_tokens, small, gains, *sums = rear(
        low, dsil, conv, dy, dv, sf, conv_w, x2, r, d_og, d_sk, dt, cum, dtraw, aux, dbc, drate, dq, dtb_row, alog_row,
        turned, w_first, w_side, gain_row, dgate, tokens, cotangent, g_side, rows, sizes, here,
    )
    if here:
        d_w_in, d_w_out, d_gain, *small = finish(sums, small, gains, conv_w.shape[0], (inner, channels, heads, rows))
        d_gain = d_gain[0]
        small = tuple(a[0] if a.ndim == 2 and a.shape[0] == 1 else a for a in small)
    else:
        dproj = sums[0]
        g_first = nn(turned, dproj).reshape(parts, rows, dproj.shape[1])
        firsts = lax.psum_scatter(g_first, AXES, scatter_dimension=0)
        sides = lax.psum_scatter(g_side, AXES, scatter_dimension=0)
        d_w_in, d_w_out = jnp.concatenate([sides[:, :inner], firsts], axis=1), sides[:, inner:]
        small, gains = lax.psum((small, gains), AXES)
        small, d_gain = unpack(small, conv_w.shape[0], inner, heads), gains.reshape(-1)[:d]
        d_gain = lax.dynamic_slice_in_dim(d_gain, lax.axis_index(AXES) * rows, rows)
    return (output, d_tokens, d_w_in, d_w_out.T, d_gain) + small


def solution(mesh):
    rows, cols, line, none = P(AXES, None), P(None, AXES), P(AXES), P()
    here = dict(mesh.shape) == {"fsdp": 8, "rep": 4}
    return jax.shard_map(
        functools.partial(body, here),
        mesh=mesh,
        in_specs=(rows, line, rows, cols, line, none, none, none, none, none, none, rows),
        out_specs=(rows, rows, rows, cols, line, none, none, none, none, none, none),
        check_vma=False,
    )
```

```python
import functools

import jax
import jax.numpy as jnp
import numpy as np
from jax import lax
from jax.experimental import pallas as pl
from jax.experimental.pallas import tpu as pltpu
from jax.sharding import PartitionSpec as P

eps = 1e-05
Q = 128
SUB = 2
HALO = 16
f32 = jnp.float32
bf16 = jnp.bfloat16
AXES = ("fsdp", "rep")
BIAS_AT, LOG_AT, SKIP_AT = 768, 896, 1024


def nn(a, b):
    return lax.dot_general(a, b, (((1,), (0,)), ((), ())), preferred_element_type=f32)


def nt(a, b):
    return lax.dot_general(a, b, (((1,), (1,)), ((), ())), preferred_element_type=f32)


def tn(a, b):
    return lax.dot_general(a, b, (((0,), (0,)), ((), ())), preferred_element_type=f32)


def split2(x):
    hi = x.astype(bf16)
    lo = (x - hi.astype(f32)).astype(bf16)
    return jnp.concatenate([hi, lo], axis=1)


def split_rows(x):
    hi = x.astype(bf16)
    return jnp.concatenate([hi, (x - hi.astype(f32)).astype(bf16)], axis=0)


def nn_exact(ones_mask, x):
    hi = x.astype(bf16)
    r = x - hi.astype(f32)
    mid = r.astype(bf16)
    lo = (r - mid.astype(f32)).astype(bf16)
    return nn(ones_mask, hi) + (nn(ones_mask, mid) + nn(ones_mask, lo))


def iotas(shape):
    return (
        lax.broadcasted_iota(jnp.int32, shape, 0),
        lax.broadcasted_iota(jnp.int32, shape, 1),
    )


MESH = pl.DeviceIdType.MESH
LINE = 4
STEPS = (0, -1, 1, -2, 2, -3, 3)
LAG = 2


def place():
    f = lax.axis_index("fsdp")
    return f // 4, (f // 2) % 2, f % 2, lax.axis_index("rep")


def flip(at, dy, dx, dc, dz):
    y, x, c, z = at
    return (1 - y if dy else y, 1 - x if dx else x, 1 - c if dc else c, z + dz)


def device(at):
    y, x, c, z = at
    return ((y * 2 + x) * 2 + c, z)


def slot(at):
    y, x, c, z = at
    return ((y * 2 + x) * 2 + c) * LINE + z


def on_line(me, dz):
    z = me[3]
    return z >= -dz if dz < 0 else z < LINE - dz


def when(condition, act):
    if condition is True:
        act()
    else:
        pl.when(condition)(act)


def greet(me):
    barrier = pltpu.get_barrier_semaphore()
    for other in ((0, 0, 1, 0), (0, 1, 0, 0), (1, 0, 0, 0)):
        pl.semaphore_signal(barrier, inc=1, device_id=device(flip(me, *other)), device_id_type=MESH)
    for dz in (-1, 1):

        @pl.when(on_line(me, dz))
        def _():
            pl.semaphore_signal(barrier, inc=1, device_id=device(flip(me, 0, 0, 0, dz)), device_id_type=MESH)

    inside = jnp.where((me[3] > 0) & (me[3] < LINE - 1), 1, 0)
    pl.semaphore_wait(barrier, 4 + inside)


def halves(width):
    cut = (width // 2 + 127) // 128 * 128
    return slice(0, cut), slice(cut, width)


class Gatherer:
    kinds = ("z", "x", "y", "c", "left", "right", "cx", "cy", "cl", "cr")
    count = len(kinds) * len(STEPS)

    def __init__(self, me, own, full, send, recv):
        self.me, self.own, self.full, self.send, self.recv = me, own, full, send, recv
        self.left, self.right = halves(full.shape[2])

    def made(self, kind, dz, block, to, cols=None):
        i = self.kinds.index(kind) * len(STEPS) + STEPS.index(dz)
        at = slot(flip(self.me, *block))
        dst = self.full.at[at] if cols is None else self.full.at[at, :, cols]
        src = dst
        if block == (0, 0, 0, 0):
            src = self.own if cols is None else self.own.at[:, cols]
        return pltpu.make_async_remote_copy(
            src_ref=src, dst_ref=dst, send_sem=self.send.at[i], recv_sem=self.recv.at[i],
            device_id=device(flip(self.me, *to)), device_id_type=MESH,
        )

    def copy(self, kind, dz):
        return {
            "x": lambda: self.made("x", dz, (0, 0, 0, dz), (0, 1, 0, 0)),
            "y": lambda: self.made("y", dz, (0, 0, 0, dz), (1, 0, 0, 0)),
            "c": lambda: self.made("c", dz, (0, 0, 0, dz), (0, 0, 1, 0)),
            "left": lambda: self.made("left", dz, (0, 1, 0, dz), (1, 0, 0, 0), self.left),
            "right": lambda: self.made("right", dz, (1, 0, 0, dz), (0, 1, 0, 0), self.right),
            "cx": lambda: self.made("cx", dz, (0, 1, 0, dz), (0, 0, 1, 0)),
            "cy": lambda: self.made("cy", dz, (1, 0, 0, dz), (0, 0, 1, 0)),
            "cl": lambda: self.made("cl", dz, (1, 1, 0, dz), (0, 0, 1, 0), self.left),
            "cr": lambda: self.made("cr", dz, (1, 1, 0, dz), (0, 0, 1, 0), self.right),
        }[kind]()

    def along(self, dz, way):
        i = self.kinds.index("z") * len(STEPS) + STEPS.index(dz - way)
        at = slot(flip(self.me, 0, 0, 0, dz))
        return pltpu.make_async_remote_copy(
            src_ref=self.full.at[at] if dz else self.own, dst_ref=self.full.at[at],
            send_sem=self.send.at[i], recv_sem=self.recv.at[i],
            device_id=device(flip(self.me, 0, 0, 0, way)), device_id_type=MESH,
        )

    def sent_along(self):
        for dz in STEPS:
            for way in (-1, 1):
                if dz * way <= 0 and abs(dz - way) < LINE:
                    yield dz, way, on_line(self.me, way) & (True if dz == 0 else on_line(self.me, dz))

    def each(self, act):
        for dz in STEPS:
            when(True if dz == 0 else on_line(self.me, dz), functools.partial(act, dz))

    def start(self):
        for dz, way, ok in self.sent_along():
            if dz == 0:
                when(ok, lambda dz=dz, way=way: self.along(dz, way).start())
        self.spread(0)

    def spread(self, dz):
        for kind in ("x", "y", "c"):
            self.copy(kind, dz).start()

    def column(self, dz):
        if dz == 0:
            return
        way = -1 if dz > 0 else 1
        self.along_arrived(dz)
        if abs(dz) < LINE - 1:
            when(on_line(self.me, way), lambda: self.along(dz, way).start())
        self.spread(dz)

    def along_arrived(self, dz):
        i = self.kinds.index("z") * len(STEPS) + STEPS.index(dz)
        ref = self.full.at[slot(flip(self.me, 0, 0, 0, dz))]
        pltpu.make_async_remote_copy(
            src_ref=ref, dst_ref=ref, send_sem=self.send.at[i], recv_sem=self.recv.at[i],
            device_id=device(flip(self.me, 0, 0, 0, 1 if dz > 0 else -1)), device_id_type=MESH,
        ).wait_recv()

    def corner(self, dz):
        self.copy("x", dz).wait_recv()
        self.copy("left", dz).start()
        self.copy("cx", dz).start()
        self.copy("y", dz).wait_recv()
        self.copy("right", dz).start()
        self.copy("cy", dz).start()

    def last(self, dz):
        self.copy("left", dz).wait_recv()
        self.copy("cl", dz).start()
        self.copy("right", dz).wait_recv()
        self.copy("cr", dz).start()

    def beat(self, t):
        for lag, act in ((0, self.column), (LAG, self.corner), (2 * LAG, self.last)):
            if 0 <= t - lag < len(STEPS):
                dz = STEPS[t - lag]
                when(True if dz == 0 else on_line(self.me, dz), functools.partial(act, dz))

    beats = len(STEPS) + 2 * LAG

    def finish(self):
        def act(dz):
            for kind in ("c", "cx", "cy", "cl", "cr"):
                self.copy(kind, dz).wait_recv()
            for kind in self.kinds[1:]:
                self.copy(kind, dz).wait_send()

        self.each(act)
        for dz, way, ok in self.sent_along():
            when(ok, lambda dz=dz, way=way: self.along(dz, way).wait_send())


def partner(at, dy, dx, dc, k):
    return flip(at, dy, dx, dc, 0)[:3] + ({0: at[3], 1: at[3] + 1 - 2 * (at[3] % 2), 2: (at[3] + 2) % 4, 3: 3 - at[3]}[k],)


CUBE = [(0, 0, 1, 0), (0, 1, 0, 0), (1, 0, 0, 0), (0, 1, 1, 0), (1, 0, 1, 0), (1, 1, 0, 0), (1, 1, 1, 0)]


def greet_all(me):
    barrier = pltpu.get_barrier_semaphore()
    others = CUBE + [(0, 0, 0, 1), (0, 0, 0, 2), (0, 0, 0, 3)]
    for other in others:
        pl.semaphore_signal(barrier, inc=1, device_id=device(partner(me, *other)), device_id_type=MESH)
    pl.semaphore_wait(barrier, len(others))


BLOCKS = ((1, 1), (0, 1), (1, 0), (0, 0))


ORDER = (3, 2, 1, 0)


class Scatterer:
    count = 59

    def __init__(self, me, part, out, mine, from_core, from_pair, from_far, from_line, send, recv, here=None):
        self.me, self.part, self.out = me, part, out
        self.mine, self.from_core, self.from_pair, self.from_far, self.from_line = (
            mine, from_core, from_pair, from_far, from_line,
        )
        self.send, self.recv, self.here = send, recv, here
        self.left, self.right = halves(part.shape[2])

    def copy(self, name, index):
        if name == "core":
            b, k, half = index // 8, index // 2 % 4, index % 2
            cols = self.right if half else self.left
            src = self.part.at[slot(partner(self.me, *BLOCKS[b], 1, k)), :, cols]
            dst, to, i = self.from_core.at[b, k, :, cols], (0, 0, 1, 0), index
        elif name == "x":
            b, k = index // 4, index % 4
            src, dst = self.mine.at[b, k, :, self.left], self.from_pair.at[b, k, :, self.left]
            to, i = (0, 1, 0, 0), 32 + index
        elif name == "y":
            b, k = index // 4, index % 4
            src, dst = self.mine.at[2 * b, k, :, self.right], self.from_pair.at[b, k, :, self.right]
            to, i = (1, 0, 0, 0), 40 + index
        elif name == "fy":
            src, dst = self.mine.at[2, index, :, self.left], self.from_far.at[index, :, self.left]
            to, i = (1, 0, 0, 0), 48 + index
        elif name == "fx":
            src, dst = self.mine.at[1, index, :, self.right], self.from_far.at[index, :, self.right]
            to, i = (0, 1, 0, 0), 52 + index
        else:
            src, dst, to, i = self.mine.at[3, index], self.from_line.at[index - 1], (0, 0, 0, index), 55 + index
        return pltpu.make_async_remote_copy(
            src_ref=src, dst_ref=dst, send_sem=self.send.at[i], recv_sem=self.recv.at[i],
            device_id=device(partner(self.me, *to)), device_id_type=MESH,
        )

    def local(self, b, k):
        own = slot(partner(self.me, *BLOCKS[b], 0, k))
        return pltpu.make_async_copy(self.part.at[own], self.mine.at[b, k], self.here.at[b * 4 + k])

    def start(self, *cuts):
        for k in ORDER:
            for b in range(4):
                for half in cuts or (0, 1):
                    self.copy("core", b * 8 + k * 2 + half).start()
                if self.here is not None:
                    self.local(b, k).start()

    def add(self, b, k, cols, others):
        total = self.mine[b, k, :, cols].astype(f32)
        for ref in others:
            total += ref.astype(f32)
        return total

    def pair(self, k):
        for b in range(4):
            for half in (0, 1):
                self.copy("core", b * 8 + k * 2 + half).wait_recv()
            if self.here is not None:
                self.local(b, k).wait()
                own = self.mine[b, k]
            else:
                own = self.part[slot(partner(self.me, *BLOCKS[b], 0, k))]
            self.mine[b, k] = own + self.from_core[b, k]
            if b < 2:
                self.copy("x", b * 4 + k).start()
            if b % 2 == 0:
                self.copy("y", b * 2 + k).start()

    def far(self, k):
        self.copy("x", k).wait_recv()
        self.mine[2, k, :, self.left] = self.mine[2, k, :, self.left] + self.from_pair[0, k, :, self.left]
        self.copy("fy", k).start()
        self.copy("y", k).wait_recv()
        self.mine[1, k, :, self.right] = self.mine[1, k, :, self.right] + self.from_pair[0, k, :, self.right]
        self.copy("fx", k).start()

    def line(self, k):
        for made in (self.copy("x", 4 + k), self.copy("y", 4 + k), self.copy("fy", k), self.copy("fx", k)):
            made.wait_recv()
        if k:
            self.mine[3, k] = self.add(3, k, slice(None), [self.from_pair[1, k], self.from_far[k]]).astype(bf16)
            self.copy("z", k).start()

    def finish(self):
        for k in (1, 2, 3):
            self.copy("z", k).wait_recv()
        self.out[...] = self.add(
            3, 0, slice(None),
            [self.from_pair[1, 0], self.from_far[0], self.from_line[0], self.from_line[1], self.from_line[2]],
        )
        for name, indices in (
            ("core", range(32)), ("x", range(8)), ("y", range(8)), ("fy", range(4)), ("fx", range(4)), ("z", (1, 2, 3)),
        ):
            for i in indices:
                self.copy(name, i).wait_send()


def scatter_scratch(rows, width):
    vmem = lambda *lead: pltpu.VMEM(lead + (rows, width), bf16)
    return [
        vmem(4, 4), vmem(4, 4), vmem(2, 4), vmem(4), vmem(3),
        pltpu.SemaphoreType.DMA((Scatterer.count,)), pltpu.SemaphoreType.DMA((Scatterer.count,)),
    ]


class Summer:
    def __init__(self, me, own, out, held, send, recv):
        self.me, self.own, self.out, self.held, self.send, self.recv = me, own, out, held, send, recv

    def copy(self, i):
        src = self.own if i == 0 else self.held.at[5 + min(i, 3)]
        to = ((0, 0, 1, 0), (0, 1, 0, 0), (1, 0, 0, 0), (0, 0, 0, 1), (0, 0, 0, 2), (0, 0, 0, 3))[i]
        return pltpu.make_async_remote_copy(
            src_ref=src, dst_ref=self.held.at[i], send_sem=self.send.at[i], recv_sem=self.recv.at[i],
            device_id=device(partner(self.me, *to)), device_id_type=MESH,
        )

    def start(self):
        self.copy(0).start()

    def next(self, i):
        self.copy(i - 1).wait_recv()
        before = self.own[...] if i == 1 else self.held[4 + i]
        self.held[5 + i] = before + self.held[i - 1]
        for j in (i,) if i < 3 else (3, 4, 5):
            self.copy(j).start()

    def finish(self):
        for j in (3, 4, 5):
            self.copy(j).wait_recv()
        self.out[...] = (self.held[8] + self.held[3]) + (self.held[4] + self.held[5])
        for j in range(6):
            self.copy(j).wait_send()


class Quick:
    def __init__(self, me, own, out, held, send, recv):
        self.me, self.own, self.out, self.held, self.send, self.recv = me, own, out, held, send, recv

    def copy(self, i):
        near = i < len(CUBE)
        to = CUBE[i] if near else (0, 0, 0, i - len(CUBE) + 1)
        return pltpu.make_async_remote_copy(
            src_ref=self.own if near else self.held.at[10], dst_ref=self.held.at[i],
            send_sem=self.send.at[i], recv_sem=self.recv.at[i],
            device_id=device(partner(self.me, *to)), device_id_type=MESH,
        )

    def start(self):
        for i in range(7):
            self.copy(i).start()

    def finish(self):
        for i in range(7):
            self.copy(i).wait_recv()
        self.held[10] = self.own[...] + functools.reduce(jnp.add, [self.held[i] for i in range(7)])
        for i in (7, 8, 9):
            self.copy(i).start()
        for i in (7, 8, 9):
            self.copy(i).wait_recv()
        self.out[...] = (self.held[10] + self.held[7]) + (self.held[8] + self.held[9])
        for i in range(10):
            self.copy(i).wait_send()


AUX = 16


def features(seg_ref, at):
    last = seg_ref.shape[0] - 1
    line = lambda i: jnp.broadcast_to(seg_ref[pl.ds(i, 1), :].astype(f32), (8, Q))
    seg = line(at)
    before = jnp.where(at > 0, line(jnp.maximum(at - 1, 0)), -1.0)
    after = jnp.where(at < last, line(jnp.minimum(at + 1, last)), -1.0)
    lane = lax.broadcasted_iota(jnp.int32, (8, Q), 1)
    earlier = [jnp.where(lane < k, pltpu.roll(before, k, 1), pltpu.roll(seg, k, 1)) == seg for k in (1, 2, 3)]
    later = [
        jnp.where(lane < Q - k, pltpu.roll(seg, Q - k, 1), pltpu.roll(after, Q - k, 1)) == seg for k in (1, 2, 3)
    ]
    edges = [seg == x for x in (seg[:, Q - 1 :], seg[:, :1], before[:, Q - 1 :], after[:, :1])]
    one = lambda mask: jnp.where(mask, 1.0, 0.0)
    lines = [one(m) for m in earlier] + [seg] + [one(m) for m in edges + later]
    row = lax.broadcasted_iota(jnp.int32, (8, Q), 0)
    blocks = []
    for i in range(0, AUX, 8):
        block = jnp.zeros((8, Q), f32)
        for j, x in enumerate(lines[i : i + 8]):
            block = jnp.where(row == j, x, block)
        blocks.append(block)
    return jnp.transpose(jnp.concatenate(blocks + [jnp.zeros((Q - AUX, Q), f32)], axis=0))


def reaches(here, number):
    return dict(collective_id=number, has_side_effects=True) if here else {}


OTHERS_AT = 3
OTHERS_LAG = 4
BEATS = (5, 6, 7, 8, 9, 10, 11, 11, 11)


def front_kernel(
    sizes, here,
    tok_ref, halo_ref, seg_ref, cw_ref, cb_ref, dtb_ref, alog_ref, x2_ref, first_ref, own_ref, gain_in_ref,
    normed_ref, turned_ref, conv_ref, act_ref, low_ref, dsil_ref, dt_ref, cum_ref, dtraw_ref, aux_ref, sb_ref, w_ref, gain_ref,
    full_ref,
    ext_ref, column_ref, state_ref, land_ref, near_ref, side_ref, send_ref, recv_ref, copy_ref,
):
    inner, channels, heads, state = sizes
    step = pl.program_id(0)
    taken = channels + 2 * heads
    if here:
        me = place()
        urgent = Gatherer(me, near_ref, land_ref, send_ref.at[0], recv_ref.at[0])
        others = Gatherer(me, side_ref, full_ref, send_ref.at[1], recv_ref.at[1])
        mine = [
            pltpu.make_async_copy(near_ref, land_ref.at[slot(me)], copy_ref.at[0]),
            pltpu.make_async_copy(side_ref, full_ref.at[slot(me)], copy_ref.at[1]),
        ]

    @pl.when(step == 0)
    def _():
        state_ref[...] = jnp.zeros_like(state_ref)
        if here:
            near_ref[:, :taken] = first_ref[:, inner:]
            gain_in = gain_in_ref[...]
            gain_in = jnp.concatenate([gain_in, jnp.zeros((1, Q - gain_in.shape[1]), f32)], axis=1)
            gain_in = jnp.transpose(jnp.broadcast_to(gain_in, (Q, Q)))
            near_ref[:, taken:] = gain_in[: near_ref.shape[0], 0:1].astype(bf16)
            side_ref[:, :inner] = first_ref[:, :inner]
            side_ref[:, inner:] = own_ref[...]
            greet(me)
            urgent.start()
            mine[0].start()
            for t in range(Gatherer.beats):
                if t == OTHERS_AT:
                    others.start()
                    mine[1].start()
                urgent.beat(t)
                if 0 <= t - OTHERS_LAG < BEATS[0]:
                    others.beat(t - OTHERS_LAG)
            mine[0].wait()
            urgent.finish()
            source = land_ref
        else:
            source = first_ref
        rows = source.shape[1]
        group = 1 if rows % 16 == 0 else 48 // rows
        for j in range(0, source.shape[0], group):
            block = jnp.concatenate([source[j + i].astype(f32) for i in range(group)], axis=0)
            at = slice(j * rows, (j + group) * rows)
            w_ref[at, :] = block[:, :taken].astype(bf16)
            column_ref[at, :] = jnp.broadcast_to(block[:, taken:], (block.shape[0], Q))
        for at in range(0, gain_ref.shape[1], Q):
            gain_ref[:, at : at + Q] = jnp.transpose(column_ref[at : at + Q, :])[0:1, :]

    gain = gain_ref[...]

    def norm(x):
        x = x.astype(f32)
        inv = lax.rsqrt(jnp.mean(x * x, axis=1, keepdims=True) + eps)
        return (x * inv * gain).astype(bf16)

    normed = norm(tok_ref[...])
    normed_ref[...] = normed
    turned_ref[...] = jnp.transpose(normed)
    both = jnp.concatenate([norm(halo_ref[...]), normed], axis=0)
    dt_raw = nn(normed, w_ref[:, channels : channels + 2 * heads])
    dtraw_ref[...] = dt_raw
    aux = features(seg_ref, pl.num_programs(0) - 1 - step)
    aux_ref[...] = aux[:, : aux_ref.shape[1]]
    m1, m2, m3 = aux[:, 0:1], aux[:, 1:2], aux[:, 2:3]
    block = 256
    for at in range(0, channels, block):
        sl = slice(at, at + block)
        ext_ref[:, sl] = nn(both, w_ref[:, at : at + block])
        x0 = ext_ref[HALO : HALO + Q, sl]
        conv_ref[:, sl] = x0
        pre = cb_ref[sl][None, :] + cw_ref[0:1, sl] * x0
        pre += cw_ref[1:2, sl] * (ext_ref[HALO - 1 : HALO - 1 + Q, sl] * m1)
        pre += cw_ref[2:3, sl] * (ext_ref[HALO - 2 : HALO - 2 + Q, sl] * m2)
        pre += cw_ref[3:4, sl] * (ext_ref[HALO - 3 : HALO - 3 + Q, sl] * m3)
        sig = 1.0 / (1.0 + jnp.exp(-pre))
        act = pre * sig
        act_ref[:, sl] = act
        low_ref[:, sl] = act.astype(bf16)
        dsil_ref[:, sl] = sig * (1.0 + pre * (1.0 - sig))
    v = dt_raw + dtb_ref[...]
    dt = jnp.maximum(v, 0.0) + jnp.log1p(jnp.exp(-jnp.abs(v)))
    dt_ref[...] = dt
    rate = -dt * jnp.exp(alog_ref[...])
    row, col = iotas((Q, Q))
    cum = nn_exact((col <= row).astype(bf16), rate)
    cum_ref[...] = cum
    sb_ref[0] = state_ref[...].astype(bf16)
    weight = dt[:, heads:] * jnp.exp(cum[:, heads:] - rate[:, heads:]) * aux[:, 5:6]
    whole = jnp.exp(cum[Q - 1 :, heads:]) * aux[0:1, 7:8]
    scales = split2(jnp.concatenate([weight, jnp.broadcast_to(whole, (8, heads))], axis=0))
    b_bwd = jnp.transpose(act_ref[:, inner + 2 * state :])[:state].astype(bf16)
    for at in range(0, inner, block):
        sl = slice(at, at + block)
        wide = nn(scales, x2_ref[:, sl])
        vs = (low_ref[:, sl].astype(f32) * wide[:Q]).astype(bf16)
        state_ref[:, sl] = state_ref[:, sl] * wide[Q : Q + 1] + nn(b_bwd, vs)
    if here:
        steps = len(BEATS) - 1
        for i in range(steps):

            @pl.when(step == i)
            def _():
                for t in range(BEATS[i], BEATS[i + 1]):
                    others.beat(t)
                if i == steps - 1:
                    mine[1].wait()
                    others.finish()


def front(tokens, seg, conv_w, conv_b, dt_bias, a_log, x2, first, own, gain, sizes, here):
    inner, channels, heads, state = sizes
    t, d = tokens.shape
    n = t // Q
    rev = lambda i: (n - 1 - i, 0)
    fixed = lambda i: (0, 0)
    blk = lambda width: pl.BlockSpec((Q, width), rev)
    whole = lambda a: pl.BlockSpec(a.shape, lambda i: (0,) * a.ndim)
    anywhere = pl.BlockSpec(memory_space=pl.ANY)
    per = Q // HALO
    out = lambda width, dtype: jax.ShapeDtypeStruct((t, width), dtype)
    taken = channels + 2 * heads
    rows = own.shape[0]
    return pl.pallas_call(
        functools.partial(front_kernel, sizes, here),
        grid=(n,),
        in_specs=[
            blk(d),
            pl.BlockSpec((HALO, d), lambda i: (jnp.maximum((n - 1 - i) * per - 1, 0), 0)),
            whole(seg), whole(conv_w), whole(conv_b), whole(dt_bias), whole(a_log), whole(x2), whole(first), whole(own),
            whole(gain),
        ],
        out_specs=[
            blk(d), pl.BlockSpec((d, Q), lambda i: (0, n - 1 - i)), blk(channels), blk(channels), blk(channels), blk(channels),
            blk(2 * heads), blk(2 * heads), blk(2 * heads), blk(AUX),
            pl.BlockSpec((1, state, inner), lambda i: (n - 1 - i, 0, 0)),
            pl.BlockSpec((d, taken), fixed), pl.BlockSpec((1, d), fixed),
            anywhere,
        ],
        out_shape=[
            out(d, bf16), jax.ShapeDtypeStruct((d, t), bf16),
            out(channels, f32), out(channels, f32), out(channels, bf16), out(channels, f32),
            out(2 * heads, f32), out(2 * heads, f32), out(2 * heads, f32), out(AUX, f32),
            jax.ShapeDtypeStruct((n, state, inner), bf16),
            jax.ShapeDtypeStruct((d, taken), bf16), jax.ShapeDtypeStruct((1, d), f32),
            jax.ShapeDtypeStruct((32, rows, 2 * inner) if here else (1, 8, Q), bf16),
        ],
        scratch_shapes=[
            pltpu.VMEM((HALO + Q, channels), f32),
            pltpu.VMEM((d, Q), f32),
            pltpu.VMEM((state, inner), f32),
            pltpu.VMEM((32, rows, taken + 1) if here else (1, 8, Q), bf16),
            pltpu.VMEM((rows, taken + 1), bf16),
            pltpu.VMEM((rows, 2 * inner), bf16),
            pltpu.SemaphoreType.DMA((2, Gatherer.count)),
            pltpu.SemaphoreType.DMA((2, Gatherer.count)),
            pltpu.SemaphoreType.DMA((2,)),
        ],
        compiler_params=pltpu.CompilerParams(
            dimension_semantics=("arbitrary",), vmem_limit_bytes=60 * 1024 * 1024, **reaches(here, 0)
        ),
        cost_estimate=pl.CostEstimate(flops=5_000_000_000, bytes_accessed=50_000_000, transcendentals=0),
    )(tokens, tokens, seg, conv_w, conv_b, dt_bias, a_log, x2, first, own, gain)


def middle_chunk(
    sizes, step,
    act_ref, dt_ref, cum_ref, aux_ref, seg_ref, cot_ref, sb_ref,
    alog_ref, og_ref, x2_ref, r_ref,
    turned_ref, nout_ref, dgate_ref, dy_ref, dv_ref, dbc_ref, drate_ref, dq_ref, sf_ref, dog_ref, dsk_ref,
    decay_ref, mix_ref, state_ref, adj_ref, ssm_ref, gated_ref, dno_ref, yf_ref, yb_ref, wide_ref,
    p_ref, q_ref, scal_ref, gate_ref, skip_ref,
):
    inner, channels, heads, state = sizes
    quad = 256

    sf_ref[0] = state_ref[...].astype(bf16)
    aux = aux_ref[...]
    row, col = iotas((Q, Q))
    lower = col < row
    same = aux[:, 3:4] == seg_ref[pl.ds(step, 1), :].astype(f32)
    b_f = act_ref[:, inner : inner + state].astype(bf16)
    b_f_turned = jnp.transpose(act_ref[:, inner : inner + 2 * state])[:state].astype(bf16)
    c_f = act_ref[:, inner + state : inner + 2 * state].astype(bf16)
    b_b = act_ref[:, inner + 2 * state : inner + 3 * state].astype(bf16)
    c_b = act_ref[:, inner + 3 * state :].astype(bf16)
    c_b_turned = jnp.transpose(act_ref[:, inner + 2 * state :])[state:].astype(bf16)
    g = jnp.where(same & (col != row), jnp.where(lower, nt(c_f, b_f), nt(c_b, b_b)), 0.0)
    dt = dt_ref[...]
    cum = cum_ref[...]
    rate = -dt * jnp.exp(alog_ref[...])
    cf, cb = cum[:, :heads], cum[:, heads:] - rate[:, heads:]
    dtf, dtb = dt[:, :heads], dt[:, heads:]
    total_f, total_b = cum[Q - 1 :, :heads], cum[Q - 1 :, heads:]
    ldt = jnp.log(jnp.maximum(dt, 1e-37))
    rows = jnp.transpose(
        jnp.concatenate(
            [cf - ldt[:, :heads], cb + ldt[:, heads:], jnp.zeros((Q, Q - 2 * heads), f32)], axis=1
        )
    )
    scales = split2(
        jnp.concatenate(
            [
                jnp.exp(cf) * aux[:, 6:7],
                jnp.exp(total_b - cb) * aux[:, 7:8],
                dtf * jnp.exp(total_f - cf) * aux[:, 4:5],
                dtb * jnp.exp(cb) * aux[:, 5:6],
                jnp.broadcast_to(jnp.exp(total_f) * aux[Q - 1 :, 6:7], (8, heads)),
                jnp.broadcast_to(jnp.exp(total_b) * aux[0:1, 7:8], (8, heads)),
            ],
            axis=0,
        )
    )
    lane = lax.broadcasted_iota(jnp.int32, (1, Q), 1)
    first = (lane < Q // 2).astype(bf16)
    second = (lane >= Q // 2).astype(bf16)

    def apart(x):
        return jnp.concatenate([x * first, x * second], axis=0)

    squares = jnp.zeros((Q, quad), f32)
    dots = jnp.zeros((Q, quad), f32)
    turned_ref[...] = jnp.transpose(cot_ref[...])
    for at in range(0, inner, quad):
        sl = slice(at, at + quad)
        wide_ref[:, sl] = nn(scales, x2_ref[:, sl])
        v = act_ref[:, sl]
        low = v.astype(bf16)
        yf = nn(c_f, state_ref[:, sl].astype(bf16)) * wide_ref[:Q, sl]
        yb = nn(c_b, sb_ref[0, :, sl]) * wide_ref[Q : 2 * Q, sl]
        yf_ref[:, sl] = yf
        yb_ref[:, sl] = yb
        parts = []
        for half in range(2):
            mixes = []
            for h in (at // 64 + 2 * half, at // 64 + 2 * half + 1):
                gap = jnp.where(
                    lower,
                    cf[:, h : h + 1] - rows[h : h + 1, :],
                    rows[heads + h : heads + h + 1, :] - cb[:, h : h + 1],
                )
                decay = jnp.exp(gap)
                decay_ref[h] = decay
                mix = (g * decay).astype(bf16)
                mix_ref[h * Q : (h + 1) * Q, :] = mix
                mixes.append(mix)
            parts.append(
                nn(jnp.concatenate(mixes, axis=1), apart(low[:, half * Q : (half + 1) * Q]))
            )
        ssm = jnp.concatenate(parts, axis=1) + yf + yb + skip_ref[:, sl] * v
        ssm_ref[:, sl] = ssm
        gate = gate_ref[:, sl]
        gated = ssm * (gate / (1.0 + jnp.exp(-gate)))
        gated_ref[:, sl] = gated
        dno = dno_ref[:, sl]
        squares += gated * gated
        dots += dno * og_ref[sl][None, :] * gated

    inv = lax.rsqrt(jnp.sum(squares, axis=1, keepdims=True) / inner + eps)
    drag = inv * (inv * jnp.sum(dots, axis=1, keepdims=True) / inner)
    dg = jnp.zeros((Q, Q), f32)
    d_cf = jnp.zeros((Q, state), f32)
    d_cb = jnp.zeros((Q, state), f32)
    d_bb = jnp.zeros((Q, state), f32)
    heads_of = jnp.zeros((3 * Q, Q), f32)
    for at in range(0, inner, quad):
        sl = slice(at, at + quad)
        v = act_ref[:, sl]
        low = v.astype(bf16)
        low_f = low.astype(f32)
        ssm, gate, gated, dno = ssm_ref[:, sl], gate_ref[:, sl], gated_ref[:, sl], dno_ref[:, sl]
        og = og_ref[sl][None, :]
        unit = gated * inv
        nout_ref[:, sl] = (unit * og).astype(bf16)
        dog_ref[:, sl] += jnp.sum(dno * unit, axis=0, keepdims=True)
        d_gated = inv * (dno * og) - gated * (inv * drag)
        sig = 1.0 / (1.0 + jnp.exp(-gate))
        d_ssm = d_gated * (gate * sig)
        dgate_ref[:, sl] = (d_gated * ssm * (sig * (1.0 + gate * (1.0 - sig)))).astype(bf16)
        dsk_ref[:, sl] += jnp.sum(d_ssm * v, axis=0, keepdims=True)
        dy = d_ssm.astype(bf16)
        dy_ref[:, sl] = dy
        dy_f = dy.astype(f32)
        parts = []
        for half in range(2):
            h0 = at // 64 + 2 * half
            cut = slice(half * Q, (half + 1) * Q)
            d_mix = nt(dy[:, cut], apart(low[:, cut]))
            for i in range(2):
                h = h0 + i
                x = d_mix[:, i * Q : (i + 1) * Q] * decay_ref[h]
                dg += x
                full = x * g
                under = jnp.where(lower, full, 0.0)
                over = full - under
                q_ref[h : h + 1, :] = jnp.sum(under, axis=0, keepdims=True)
                q_ref[heads + h : heads + h + 1, :] = jnp.sum(over, axis=0, keepdims=True)
                p_ref[:, h : h + 1] = jnp.sum(under, axis=1, keepdims=True)
                p_ref[:, heads + h : heads + h + 1] = jnp.sum(over, axis=1, keepdims=True)
            parts.append(tn(mix_ref[h0 * Q : (h0 + 2) * Q, :], apart(dy[:, cut])))
        adj = adj_ref[:, sl]
        adj_low = adj.astype(bf16)
        sf_low = state_ref[:, sl].astype(bf16)
        sb_low = sb_ref[0, :, sl]
        wide_wb = wide_ref[3 * Q : 4 * Q, sl]
        dvb = wide_wb * nn(b_b, adj_low)
        dv_ref[:, sl] = d_ssm * skip_ref[:, sl] + jnp.concatenate(parts, axis=1) + dvb
        prods = jnp.concatenate(
            [
                (dy_f * yf_ref[:, sl]).astype(bf16),
                (dy_f * yb_ref[:, sl]).astype(bf16),
                (low_f * dvb).astype(bf16),
            ],
            axis=0,
        )
        heads_of += nn(prods, r_ref[sl, :])
        dye_f = (dy_f * wide_ref[:Q, sl]).astype(bf16)
        dye_b = (dy_f * wide_ref[Q : 2 * Q, sl]).astype(bf16)
        vs_f = (low_f * wide_ref[2 * Q : 3 * Q, sl]).astype(bf16)
        vs_b = (low_f * wide_wb).astype(bf16)
        d_cf += nt(dye_f, sf_low)
        d_cb += nt(dye_b, sb_low)
        d_bb += nt(vs_b, adj_low)
        across_b = wide_ref[4 * Q + 8 : 4 * Q + 9, sl]
        scal_ref[:, sl] = jnp.sum(adj * sb_low.astype(f32), axis=0, keepdims=True) * across_b
        adj_ref[:, sl] = adj * across_b + nn(c_b_turned, dye_b)
        state_ref[:, sl] = state_ref[:, sl] * wide_ref[4 * Q : 4 * Q + 1, sl] + nn(b_f_turned, vs_f)

    dg = jnp.where(same & (col != row), dg, 0.0)
    dg_f = jnp.where(lower, dg, 0.0)
    dg_b = (dg - dg_f).astype(bf16)
    dg_f = dg_f.astype(bf16)
    dbc_ref[...] = jnp.concatenate(
        [tn(dg_f, c_f), d_cf + nn(dg_f, b_f), d_bb + tn(dg_b, c_b), d_cb + nn(dg_b, b_b)], axis=1
    )
    q_cols = jnp.transpose(q_ref[...])[:, : 2 * heads]
    dots_f, dots_b, dots_v = heads_of[:Q, :heads], heads_of[Q : 2 * Q, :heads], heads_of[2 * Q :, :heads]
    through = nn(split_rows(jnp.broadcast_to(scal_ref[...], (8, inner))), r_ref[...])
    through = (through[0:1] + through[8:9])[:, :heads]
    diff = p_ref[:, : 2 * heads] - q_cols
    d_rate_f = nn_exact((col >= row).astype(bf16), diff[:, :heads] + dots_f)
    d_rate_b = (
        nn_exact((col <= row).astype(bf16), diff[:, heads:] + dots_b)
        + nn_exact((col > row).astype(bf16), dots_v)
        + through
    )
    drate_ref[...] = jnp.concatenate([d_rate_f, d_rate_b], axis=1)
    dq_ref[...] = jnp.concatenate([q_cols[:, :heads], q_cols[:, heads:] + dots_v], axis=1)


def middle_kernel(
    sizes,
    tok_ref, act_ref, normed_ref, dt_ref, cum_ref, aux_ref, seg_ref, cot_ref, sb_ref, w_ref,
    alog_ref, skip_in_ref, og_ref, x2_ref, r_ref,
    out_ref, turned_ref, nout_ref, dgate_ref, dy_ref, dv_ref, dbc_ref, drate_ref, dq_ref, sf_ref, dog_ref, dsk_ref,
    *scratch,
):
    inner, _, heads, _ = sizes
    state_ref, adj_ref, dno_ref, q_ref, gate_ref, skip_ref = (scratch[i] for i in (2, 3, 6, 11, 13, 14))
    step = pl.program_id(0)

    @pl.when(step == 0)
    def _():
        state_ref[...] = jnp.zeros_like(state_ref)
        adj_ref[...] = jnp.zeros_like(adj_ref)
        dog_ref[...] = jnp.zeros_like(dog_ref)
        dsk_ref[...] = jnp.zeros_like(dsk_ref)
        q_ref[...] = jnp.zeros_like(q_ref)
        skip_ref[...] = nn(split2(jnp.broadcast_to(skip_in_ref[...], (8, heads))), x2_ref[...])[0:1]

    for at in range(0, inner, 256):
        sl = slice(at, at + 256)
        gate_ref[:, sl] = nn(normed_ref[...], w_ref[:, sl])
        dno_ref[:, sl] = nn(cot_ref[...], w_ref[:, inner + at : inner + at + 256])
    for sub in range(SUB):
        rows = slice(sub * Q, (sub + 1) * Q)
        cut = lambda *refs: [r.at[rows] for r in refs]
        held = [r.at[rows] if i in (6, 13) else r for i, r in enumerate(scratch)]
        middle_chunk(
            sizes, step * SUB + sub,
            *cut(act_ref, dt_ref, cum_ref, aux_ref), seg_ref, cot_ref.at[rows], sb_ref.at[sub : sub + 1],
            alog_ref, og_ref, x2_ref, r_ref,
            turned_ref.at[:, rows],
            *cut(nout_ref, dgate_ref, dy_ref, dv_ref, dbc_ref, drate_ref, dq_ref), sf_ref.at[sub : sub + 1], dog_ref, dsk_ref,
            *held,
        )
    out_ref[...] = (tok_ref[...].astype(f32) + nt(nout_ref[...], w_ref[:, inner:])).astype(bf16)


def middle(tokens, act, normed, dt, cum, aux, seg, cot, sb, w_side, a_log, skip, og, x2, r, sizes):
    inner, channels, heads, state = sizes
    t, d = tokens.shape
    n = t // Q // SUB
    fwd = lambda i: (i, 0)
    fixed = lambda i: (0, 0)
    cube = lambda i: (i, 0, 0)
    blk = lambda width: pl.BlockSpec((SUB * Q, width), fwd)
    whole = lambda a: pl.BlockSpec(a.shape, fixed)
    out = lambda width, dtype: jax.ShapeDtypeStruct((t, width), dtype)
    line = jax.ShapeDtypeStruct((1, inner), f32)
    return pl.pallas_call(
        functools.partial(middle_kernel, sizes),
        grid=(n,),
        in_specs=[
            blk(d), blk(channels), blk(d), blk(2 * heads), blk(2 * heads), blk(aux.shape[1]),
            whole(seg), blk(d), pl.BlockSpec((SUB, state, inner), cube),
            whole(w_side), whole(a_log), whole(skip), pl.BlockSpec(og.shape, lambda i: (0,)), whole(x2), whole(r),
        ],
        out_specs=[
            blk(d), pl.BlockSpec((d, SUB * Q), lambda i: (0, i)), blk(inner), blk(inner), blk(inner), blk(inner), blk(4 * state),
            blk(2 * heads), blk(2 * heads), pl.BlockSpec((SUB, state, inner), cube),
            pl.BlockSpec((1, inner), fixed), pl.BlockSpec((1, inner), fixed),
        ],
        out_shape=[
            out(d, bf16), jax.ShapeDtypeStruct((d, t), bf16),
            out(inner, bf16), out(inner, bf16), out(inner, bf16), out(inner, f32),
            out(4 * state, f32), out(2 * heads, f32), out(2 * heads, f32),
            jax.ShapeDtypeStruct((n * SUB, state, inner), bf16), line, line,
        ],
        scratch_shapes=[
            pltpu.VMEM((heads, Q, Q), f32),
            pltpu.VMEM((heads * Q, Q), bf16),
            pltpu.VMEM((state, inner), f32),
            pltpu.VMEM((state, inner), f32),
            pltpu.VMEM((Q, inner), f32),
            pltpu.VMEM((Q, inner), f32),
            pltpu.VMEM((SUB * Q, inner), f32),
            pltpu.VMEM((Q, inner), f32),
            pltpu.VMEM((Q, inner), f32),
            pltpu.VMEM((4 * Q + 16, inner), f32),
            pltpu.VMEM((Q, Q), f32),
            pltpu.VMEM((Q, Q), f32),
            pltpu.VMEM((1, inner), f32),
            pltpu.VMEM((SUB * Q, inner), f32),
            pltpu.VMEM((1, inner), f32),
        ],
        compiler_params=pltpu.CompilerParams(
            dimension_semantics=("arbitrary",), vmem_limit_bytes=60 * 1024 * 1024
        ),
        cost_estimate=pl.CostEstimate(flops=30_000_000_000, bytes_accessed=60_000_000, transcendentals=0),
    )(tokens, act, normed, dt, cum, aux, seg, cot, sb, w_side, a_log, skip, og, x2, r)


def side_kernel(half, a_ref, b_ref, u_ref, v_ref, out_ref):
    step = pl.program_id(0)

    @pl.when(step < half)
    def _():
        out_ref[...] = nn(a_ref[...], u_ref[...]).astype(bf16)

    @pl.when(step >= half)
    def _():
        out_ref[...] = nn(b_ref[...], v_ref[...]).astype(bf16)


def side(a, b, u, v):
    d, t = a.shape
    block = 768
    half = u.shape[1] // block
    fixed = lambda i: (0, 0)
    return pl.pallas_call(
        functools.partial(side_kernel, half),
        grid=(2 * half,),
        in_specs=[
            pl.BlockSpec((d, t), fixed), pl.BlockSpec((d, t), fixed),
            pl.BlockSpec((t, block), lambda i: (0, jnp.minimum(i, half - 1))),
            pl.BlockSpec((t, block), lambda i: (0, jnp.maximum(i - half, 0))),
        ],
        out_specs=pl.BlockSpec((d, block), lambda i: (0, i)),
        out_shape=jax.ShapeDtypeStruct((d, 2 * u.shape[1]), bf16),
        compiler_params=pltpu.CompilerParams(
            dimension_semantics=("arbitrary",), vmem_limit_bytes=60 * 1024 * 1024
        ),
        cost_estimate=pl.CostEstimate(flops=4 * d * t * u.shape[1], bytes_accessed=14_000_000, transcendentals=0),
    )(a, b, u, v)


BLOCK = 256
ROWS = 256
PIECES = (3, 3)


def rear_kernel(
    sizes, here,
    low_ref, dsil_ref, conv_ref, dy_ref, dv_ref, sf_ref, cw_ref, x2_ref, r_ref, dog_ref, dsk_ref,
    bc_ref, dt_ref, cum_ref, dtraw_ref, aux_ref, dbc_ref, drate_ref, dq_ref, dtb_ref, alog_ref,
    turned_ref, w_ref, side_ref, gain_ref,
    dgate_ref, tok_ref, cot_ref, given_ref,
    *rest,
):
    inner, channels, heads, state = sizes
    blocks = inner // BLOCK
    step = pl.program_id(0)
    t, d = low_ref.shape[0], turned_ref.shape[0]
    n = t // Q
    taken = channels + 2 * heads
    if here:
        dtok_ref, total_ref, gains_ref, *sum_refs = rest[:7]
        (
            dproj_ref, own_ref, dgain_ref, scales_ref, ct_ref, dpre_ref, dots_ref, dbf_ref, scal_ref, through_ref, *exchange,
        ) = rest[7:]
        me = place()
        sums = [Scatterer(me, given_ref, sum_refs[0], *exchange[:8])]
        for i in range(3):
            part_ref, *held = exchange[8 + 8 * i : 16 + 8 * i]
            sums.append(Scatterer(me, part_ref, sum_refs[1 + i], *held))
        sums.append(Summer(me, own_ref, total_ref, *exchange[32:35]))
        sums.append(Quick(me, dgain_ref, gains_ref, *exchange[35:]))
    else:
        dtok_ref, own_ref, dgain_ref, dproj_ref = rest[:4]
        scales_ref, ct_ref, dpre_ref, dots_ref, dbf_ref, scal_ref, through_ref = rest[4:]

    chunk = lambda c: slice(c * Q, (c + 1) * Q)

    @pl.when(step == 0)
    def _():
        if here:
            greet_all(me)
            sums[0].start()
        own_ref[...] = jnp.zeros_like(own_ref)
        dgain_ref[...] = jnp.zeros_like(dgain_ref)
        dots_ref[...] = jnp.zeros_like(dots_ref)
        dbf_ref[...] = jnp.zeros_like(dbf_ref)
        through_ref[...] = jnp.zeros_like(through_ref)
        dpre_ref[t:, :] = jnp.zeros((8, BLOCK), f32)
        for c in range(n):
            cf, dtf = cum_ref[chunk(c), :heads], dt_ref[chunk(c), :heads]
            total_f = cf[Q - 1 :, :]
            aux = aux_ref[chunk(c), :]
            scales_ref[c] = split2(
                jnp.concatenate(
                    [
                        jnp.exp(cf) * aux[:, 6:7],
                        dtf * jnp.exp(total_f - cf) * aux[:, 4:5],
                        jnp.broadcast_to(jnp.exp(total_f) * aux[Q - 1 :, 6:7], (16, heads)),
                    ],
                    axis=0,
                )
            )
            ct_ref[c] = jnp.transpose(bc_ref[chunk(c), : 2 * state])[state:, :]

    def through_conv(at):
        sl = pl.ds(at if isinstance(at, int) else pl.multiple_of(at, BLOCK), BLOCK)
        fold = lambda x: jnp.sum(x.reshape(Q // 8, 8, BLOCK), axis=0)
        totals = [jnp.zeros((8, BLOCK), f32) for _ in range(5)]
        for c in range(n):
            conv = conv_ref[chunk(c), :]
            z = dpre_ref[chunk(c), :]
            totals[4] += fold(z)
            totals[0] += fold(z * conv)
            grad = cw_ref[0:1, :] * z
            for k in (1, 2, 3):
                z = dpre_ref[c * Q + k : (c + 1) * Q + k, :] * aux_ref[chunk(c), 7 + k : 8 + k]
                totals[k] += fold(z * conv)
                grad += cw_ref[k : k + 1, :] * z
            dproj_ref[chunk(c), sl] = grad.astype(bf16)
        for k in range(5):
            own_ref[k : k + 1, sl] = jnp.sum(totals[k], axis=0, keepdims=True)

    @pl.when(step < blocks)
    def _():
        adj = jnp.zeros((state, BLOCK), f32)
        for c in reversed(range(n)):
            wide = nn(scales_ref[c], x2_ref[...])
            wide_wf, across = wide[Q : 2 * Q], wide[2 * Q : 2 * Q + 1]
            low_f = low_ref[chunk(c), :].astype(f32)
            adj_low = adj.astype(bf16)
            dvf = wide_wf * nn(bc_ref[chunk(c), :state], adj_low)
            dots_ref[chunk(c), :] += nn((low_f * dvf).astype(bf16), r_ref[...])
            dbf_ref[chunk(c), :] += nt((low_f * wide_wf).astype(bf16), adj_low)
            scal_ref[c : c + 1, :] = jnp.sum(adj * sf_ref[c].astype(f32), axis=0, keepdims=True) * across
            dye = (dy_ref[chunk(c), :].astype(f32) * wide[:Q]).astype(bf16)
            adj = adj * across + nn(ct_ref[c], dye)
            dpre_ref[chunk(c), :] = (dv_ref[chunk(c), :] + dvf) * dsil_ref[chunk(c), :]
        both = nn(split_rows(scal_ref[...]), r_ref[...])
        through_ref[...] += both[:n] + both[n:]
        through_conv(step * BLOCK)
        at = pl.ds(pl.multiple_of(step * BLOCK, BLOCK), BLOCK)
        own_ref[5:6, at] = dog_ref[...]
        skips = nn(split_rows(jnp.broadcast_to(dsk_ref[...], (8, BLOCK))), r_ref[...])
        own_ref[6:7, SKIP_AT : SKIP_AT + Q] += skips[0:1] + skips[8:9]

    @pl.when(step == blocks)
    def _():
        a = jnp.exp(alog_ref[...])
        row, col = iotas((Q, Q))
        before = (col < row).astype(bf16)
        none = jnp.zeros((Q, heads), f32)
        sum_v, sum_a = jnp.zeros((8, 2 * heads), f32), jnp.zeros((8, 2 * heads), f32)
        fold = lambda x: jnp.sum(x.reshape(Q // 8, 8, 2 * heads), axis=0)
        for c in range(n):
            d_bf = jnp.concatenate([dbf_ref[chunk(c), :], jnp.zeros((Q, 3 * state), f32)], axis=1)
            dpre_ref[chunk(c), :] = (dbc_ref[chunk(c), :] + d_bf) * dsil_ref[chunk(c), :]
            dots, dt = dots_ref[chunk(c), :heads], dt_ref[chunk(c), :]
            extra = nn_exact(before, dots) + through_ref[c : c + 1, :heads]
            d_rate = drate_ref[chunk(c), :] + jnp.concatenate([extra, none], axis=1)
            d_dt = dq_ref[chunk(c), :] + jnp.concatenate([dots, none], axis=1)
            d_dt = jnp.where(dt > 0.0, d_dt / jnp.maximum(dt, 1e-37), 0.0)
            d_v = (d_dt - d_rate * a) / (1.0 + jnp.exp(-(dtraw_ref[chunk(c), :] + dtb_ref[...])))
            sum_v += fold(d_v)
            sum_a += fold(d_rate * (-dt * a))
            dproj_ref[chunk(c), channels:] = d_v.astype(bf16)
        own_ref[6:7, BIAS_AT : BIAS_AT + 2 * heads] = jnp.sum(sum_v, axis=0, keepdims=True)
        own_ref[6:7, LOG_AT : LOG_AT + 2 * heads] = jnp.sum(sum_a, axis=0, keepdims=True)
        through_conv(inner)

    @pl.when(step > blocks)
    def _():
        rows = pl.ds(pl.multiple_of((step - blocks - 1) * ROWS, ROWS), ROWS)
        d_normed = nt(dgate_ref[...], side_ref[...]) + nt(dproj_ref[rows, :], w_ref[...])
        x = tok_ref[...].astype(f32)
        inv = lax.rsqrt(jnp.mean(x * x, axis=1, keepdims=True) + eps)
        unit = x * inv
        gains = jnp.sum(d_normed * unit, axis=0, keepdims=True)
        for i in range(d // Q):
            dgain_ref[i : i + 1, :] += gains[:, i * Q : (i + 1) * Q]
        a = d_normed * gain_ref[...]
        dtok_ref[...] = cot_ref[...].astype(f32) + inv * (a - unit * jnp.mean(a * unit, axis=1, keepdims=True))

    if here:
        edges = (0, PIECES[0] * BLOCK, inner, taken)
        for i, acts in enumerate(SUM_BEATS):

            @pl.when(step == i)
            def _():
                for name, which, *index in acts:
                    if name == "make":
                        part = sums[which].part
                        lo = edges[which - 1]
                        for cols in (sums[which].left, sums[which].right):
                            grad = nn(turned_ref[...], dproj_ref[:, lo + cols.start : lo + cols.stop])
                            part[:, :, cols] = grad.reshape(part.shape[:2] + grad.shape[1:]).astype(bf16)
                        sums[which].start()
                    else:
                        getattr(sums[which], name)(*index)


def acts(name, which, *indices):
    return tuple((name, which, i) for i in indices)


SUM_BEATS = (
    acts("pair", 0, 3),
    acts("pair", 0, 2) + acts("far", 0, 3),
    (("make", 1),) + acts("pair", 0, 1) + acts("far", 0, 2) + acts("line", 0, 3),
    acts("pair", 0, 0) + acts("far", 0, 1) + acts("line", 0, 2) + acts("pair", 1, 3, 2, 1, 0),
    acts("far", 0, 0) + acts("line", 0, 1) + acts("far", 1, 3, 2, 1),
    (("make", 2),) + acts("line", 0, 0) + acts("far", 1, 0) + acts("line", 1, 3, 2, 1),
    (("make", 3), ("start", 4), ("finish", 0)) + acts("line", 1, 0) + acts("pair", 2, 3, 2, 1, 0),
    (("finish", 1), ("next", 4, 1)) + acts("pair", 3, 3, 2, 1, 0) + acts("far", 2, 3, 2),
    (("next", 4, 2),) + acts("far", 2, 1, 0) + acts("far", 3, 3, 2) + acts("line", 2, 3, 2),
    (("next", 4, 3),) + acts("far", 3, 1, 0) + acts("line", 2, 1, 0) + acts("line", 3, 3),
    (("start", 5),) + acts("line", 3, 2, 1, 0) + (("finish", 2), ("finish", 4), ("finish", 5), ("finish", 3)),
)


def rear(
    low, dsil, conv, dy, dv, sf, conv_w, x2, r, dog, dsk, dt, cum, dtraw, aux, dbc, drate, dq, dt_bias, a_log,
    turned, w_first, w_side, gain_row, dgate, tokens, cot, given, rows, sizes, here,
):
    inner, channels, heads, state = sizes
    t, d = tokens.shape
    n, blocks = t // Q, inner // BLOCK
    taken = channels + 2 * heads
    steps = blocks + 1 + t // ROWS
    one = pl.Buffered(1)
    wide = lambda limit: pl.BlockSpec((t, BLOCK), lambda i: (0, jnp.minimum(i, limit)))
    short = lambda lead, limit: pl.BlockSpec((lead, BLOCK), lambda i: (0, jnp.minimum(i, limit)))
    whole = lambda a: pl.BlockSpec(a.shape, lambda i: (0, 0), pipeline_mode=one)
    later = lambda width: pl.BlockSpec((ROWS, width), lambda i: (jnp.maximum(i - blocks - 1, 0), 0))
    small = (8, channels)
    scratch = [
        pltpu.VMEM((n, 2 * Q + 16, 2 * heads), bf16),
        pltpu.VMEM((n, state, Q), bf16),
        pltpu.VMEM((t + 8, BLOCK), f32),
        pltpu.VMEM((t, Q), f32),
        pltpu.VMEM((t, state), f32),
        pltpu.VMEM((n, BLOCK), f32),
        pltpu.VMEM((n, Q), f32),
    ]
    if here:
        widths = (PIECES[0] * BLOCK, PIECES[1] * BLOCK, taken - inner)
        out_shape = [small, (8, Q), (rows, 2 * inner)] + [(rows, w) for w in widths]
        own = [pltpu.VMEM((t, taken), bf16), pltpu.VMEM(small, f32), pltpu.VMEM((8, Q), f32)]
        exchange = scatter_scratch(rows, 2 * inner) + [pltpu.SemaphoreType.DMA((16,))]
        for w in widths:
            exchange += [pltpu.VMEM((d // rows, rows, w), bf16)] + scatter_scratch(rows, w)
        exchange += [pltpu.VMEM((9,) + small, f32), pltpu.SemaphoreType.DMA((6,)), pltpu.SemaphoreType.DMA((6,))]
        exchange += [pltpu.VMEM((11, 8, Q), f32), pltpu.SemaphoreType.DMA((10,)), pltpu.SemaphoreType.DMA((10,))]
        scratch = own + scratch + exchange
        outs = [jax.ShapeDtypeStruct(shape, f32) for shape in out_shape]
    else:
        outs = [
            jax.ShapeDtypeStruct(small, f32), jax.ShapeDtypeStruct((8, Q), f32), jax.ShapeDtypeStruct((t, taken), bf16),
        ]
    return pl.pallas_call(
        functools.partial(rear_kernel, sizes, here),
        grid=(steps,),
        in_specs=[
            wide(blocks), wide(blocks), wide(blocks), wide(blocks - 1), wide(blocks - 1),
            pl.BlockSpec((n, state, BLOCK), lambda i: (0, 0, jnp.minimum(i, blocks - 1))),
            short(conv_w.shape[0], blocks), short(2 * heads, blocks - 1),
            pl.BlockSpec((BLOCK, Q), lambda i: (jnp.minimum(i, blocks - 1), 0)),
            short(1, blocks - 1), short(1, blocks - 1),
            pl.BlockSpec((t, BLOCK), lambda i: (0, blocks), pipeline_mode=one),
            whole(dt), whole(cum), whole(dtraw), whole(aux), whole(dbc), whole(drate), whole(dq), whole(dt_bias), whole(a_log),
            whole(turned), whole(w_first), pl.BlockSpec((d, inner), lambda i: (0, 0), pipeline_mode=one), whole(gain_row),
            later(inner), later(d), later(d), pl.BlockSpec(memory_space=pl.ANY),
        ],
        out_specs=[later(d)] + [pl.BlockSpec(o.shape, lambda i: (0, 0)) for o in outs],
        out_shape=[jax.ShapeDtypeStruct((t, d), f32)] + outs,
        scratch_shapes=scratch,
        compiler_params=pltpu.CompilerParams(
            dimension_semantics=("arbitrary",), vmem_limit_bytes=62 * 1024 * 1024, **reaches(here, 1)
        ),
        cost_estimate=pl.CostEstimate(flops=30_000_000_000, bytes_accessed=60_000_000, transcendentals=0),
    )(
        low, dsil, conv, dy, dv, sf, conv_w, x2, r, dog, dsk, low, dt, cum, dtraw, aux, dbc, drate, dq, dt_bias, a_log,
        turned, w_first, w_side, gain_row, dgate, tokens, cot, given,
    )


def unpack(small, taps, inner, heads):
    return (
        small[:taps],
        small[taps],
        small[6, BIAS_AT : BIAS_AT + 2 * heads],
        small[6, LOG_AT : LOG_AT + 2 * heads],
        small[6, SKIP_AT : SKIP_AT + heads],
        small[5, :inner],
    )


def finish_kernel(
    sizes, side_ref, one_ref, two_ref, last_ref, small_ref, gains_ref,
    din_ref, dout_ref, dgain_ref, dcw_ref, dcb_ref, ddtb_ref, dalog_ref, dsk_ref, dog_ref,
):
    inner, channels, heads, rows = sizes
    din_ref[:, :inner] = side_ref[:, :inner]
    at = inner
    for ref in (one_ref, two_ref, last_ref):
        din_ref[:, at : at + ref.shape[1]] = ref[...]
        at += ref.shape[1]
    dout_ref[...] = side_ref[:, inner:]
    taps = dcw_ref.shape[0]
    dcw_ref[...] = small_ref[:taps, :]
    dcb_ref[...] = small_ref[taps, :]
    dog_ref[...] = small_ref[5, :inner]
    ddtb_ref[...] = small_ref[6:7, BIAS_AT : BIAS_AT + 2 * heads]
    dalog_ref[...] = small_ref[6:7, LOG_AT : LOG_AT + 2 * heads]
    dsk_ref[...] = small_ref[6:7, SKIP_AT : SKIP_AT + heads]
    row, col = iotas((Q, Q))
    picked = jnp.zeros((8, Q), f32)
    for i in range(BIAS_AT // Q):
        pick = ((row + i * Q == col + slot(place()) * rows) & (col < rows)).astype(f32).astype(bf16)
        part = jnp.broadcast_to(gains_ref[i : i + 1, :], (8, Q))
        hi = part.astype(bf16)
        mid = (part - hi.astype(f32)).astype(bf16)
        lo = (part - hi.astype(f32) - mid.astype(f32)).astype(bf16)
        picked += nn(hi, pick) + nn(mid, pick) + nn(lo, pick)
    dgain_ref[...] = picked[0:1, :rows]


def finish(sums, small, gains, taps, sizes):
    inner, channels, heads, rows = sizes
    shapes = [
        (rows, inner + channels + 2 * heads), (rows, inner), (1, rows), (taps, channels), (channels,), (1, 2 * heads),
        (1, 2 * heads), (1, heads), (inner,),
    ]
    return pl.pallas_call(
        functools.partial(finish_kernel, sizes),
        out_shape=[jax.ShapeDtypeStruct(shape, f32) for shape in shapes],
    )(*sums, small, gains)


def body(here, tokens, segment_ids, w_in, w_out, norm_gain, conv_w, conv_b, dt_bias, a_log, d_skip, out_gain, cotangent):
    rows = w_in.shape[0]
    d, inner, heads = tokens.shape[1], out_gain.shape[0], d_skip.shape[0]
    parts = d // rows
    channels = conv_w.shape[1]
    state = (channels - inner) // 4
    width = inner // heads
    sizes = (inner, channels, heads, state)
    seg = segment_ids.reshape(-1, Q)
    spread = np.arange(inner)[None, :] // width == np.arange(heads)[:, None]
    x2 = jnp.asarray(np.concatenate([spread, spread], axis=0), bf16)
    r = jnp.asarray(np.pad(spread.T, ((0, 0), (0, Q - heads))), bf16)
    first, own = w_in, w_out.T
    if not here:
        first = lax.all_gather(jnp.concatenate([w_in[:, inner:], norm_gain[:, None]], axis=1), AXES)
    alog_row, dtb_row = a_log[None, :], dt_bias[None, :]
    normed, turned, conv, act, low, dsil, dt, cum, dtraw, aux, sb, w_first, gain_row, w_side = front(
        tokens, seg, conv_w, conv_b, dtb_row, alog_row, x2, first, own, norm_gain.astype(f32)[None, :], sizes, here
    )
    if not here:
        w_side = lax.all_gather(jnp.concatenate([w_in[:, :inner], own], axis=1), AXES)
    w_side = w_side.reshape(d, 2 * inner)
    output, cot_turned, nout, dgate, dy, dv, dbc, drate, dq, sf, d_og, d_sk = middle(
        tokens, act, normed, dt, cum, aux, seg, cotangent, sb, w_side, alog_row, d_skip[None, :], out_gain, x2, r, sizes,
    )
    if here:
        g_side = side(turned, cot_turned, dgate, nout)
    else:
        g_side = jnp.concatenate([nn(turned, dgate), nn(cot_turned, nout)], axis=1)
    g_side = g_side.reshape(parts, rows, 2 * inner)
    d_tokens, small, gains, *sums = rear(
        low, dsil, conv, dy, dv, sf, conv_w, x2, r, d_og, d_sk, dt, cum, dtraw, aux, dbc, drate, dq, dtb_row, alog_row,
        turned, w_first, w_side, gain_row, dgate, tokens, cotangent, g_side, rows, sizes, here,
    )
    if here:
        d_w_in, d_w_out, d_gain, *small = finish(sums, small, gains, conv_w.shape[0], (inner, channels, heads, rows))
        d_gain = d_gain[0]
        small = tuple(a[0] if a.ndim == 2 and a.shape[0] == 1 else a for a in small)
    else:
        dproj = sums[0]
        g_first = nn(turned, dproj).reshape(parts, rows, dproj.shape[1])
        firsts = lax.psum_scatter(g_first, AXES, scatter_dimension=0)
        sides = lax.psum_scatter(g_side, AXES, scatter_dimension=0)
        d_w_in, d_w_out = jnp.concatenate([sides[:, :inner], firsts], axis=1), sides[:, inner:]
        small, gains = lax.psum((small, gains), AXES)
        small, d_gain = unpack(small, conv_w.shape[0], inner, heads), gains.reshape(-1)[:d]
        d_gain = lax.dynamic_slice_in_dim(d_gain, lax.axis_index(AXES) * rows, rows)
    return (output, d_tokens, d_w_in, d_w_out.T, d_gain) + small


def solution(mesh):
    rows, cols, line, none = P(AXES, None), P(None, AXES), P(AXES), P()
    here = dict(mesh.shape) == {"fsdp": 8, "rep": 4}
    return jax.shard_map(
        functools.partial(body, here),
        mesh=mesh,
        in_specs=(rows, line, rows, cols, line, none, none, none, none, none, none, rows),
        out_specs=(rows, rows, rows, cols, line, none, none, none, none, none, none),
        check_vma=False,
    )
```
